32 devices in a mesh: expert: 8 (over z, x), tensor: 4 (over y, core).
Axes of the slice: x: 2, y: 2, z: 4, core: 2. Of those that a mesh axis runs over, the one named last changes fastest.
Arguments:
- layer_input: bfloat16 [2, 1024, 2048], P(None, 'expert'), may hold values from -6 to 6
- positions: int32 [2, 1024], P(None, 'expert'), may hold values from 0 to 127, as said below
- parents: int32 [2, 8, 4], P(None, 'expert'), may hold values from 0 to 2, as said below
- routes: int32 [2, 1024, 4], P(None, 'expert'), may hold values from 0 to 7, as said below
- route_slots: int32 [2, 1024, 4], P(None, 'expert'), may hold values from 0 to 127, as said below
- norm1_gain: bfloat16 [2048], P('expert'), may hold values from 0.5 to 1.5
- project_weight: bfloat16 [2048, 3, 2048], P('expert', None, 'tensor'), may hold values from -0.125 to 0.125
- project_bias: bfloat16 [3, 2048], P(None, ('tensor', 'expert')), may hold values from -0.59765625 to 0.59765625
- output_weight: bfloat16 [2048, 2048], P('tensor', 'expert'), may hold values from -0.75 to 0.75
- norm2_gain: bfloat16 [2048], P('expert'), may hold values from 0.5 to 1.5
- router_weight: bfloat16 [2048, 8], P('expert'), may hold values from -0.0625 to 0.0625
- shared_vector: bfloat16 [2048], P('expert'), may hold values from -0.125 to 0.125
- shared_gate: bfloat16 [2048, 5632], P('expert', 'tensor'), may hold values from -0.125 to 0.125
- shared_up: bfloat16 [2048, 5632], P('expert', 'tensor'), may hold values from -0.125 to 0.125
- shared_down: bfloat16 [5632, 2048], P('tensor', 'expert'), may hold values from -0.078125 to 0.078125
- expert_gate: bfloat16 [8, 2048, 1408], P('expert', None, 'tensor'), may hold values from -0.125 to 0.125
- expert_up: bfloat16 [8, 2048, 1408], P('expert', None, 'tensor'), may hold values from -0.125 to 0.125
- expert_down: bfloat16 [8, 1408, 2048], P('expert', 'tensor'), may hold values from -0.15625 to 0.15625
- cotangent: bfloat16 [2, 1024, 2048], P(None, 'expert'), may hold values from -6 to 6
Outputs:
- layer_output: bfloat16 [2, 1024, 2048], P(None, 'expert')
- input_grad: float32 [2, 1024, 2048], P(None, 'expert')
- norm1_gain_grad: float32 [2048], P('expert')
- project_weight_grad: float32 [2048, 3, 2048], P('expert', None, 'tensor')
- project_bias_grad: float32 [3, 2048], P(None, ('tensor', 'expert'))
- output_weight_grad: float32 [2048, 2048], P('tensor', 'expert')
- norm2_gain_grad: float32 [2048], P('expert')
- router_weight_grad: float32 [2048, 8], P('expert')
- shared_vector_grad: float32 [2048], P('expert')
- shared_gate_grad: float32 [2048, 5632], P('expert', 'tensor')
- shared_up_grad: float32 [2048, 5632], P('expert', 'tensor')
- shared_down_grad: float32 [5632, 2048], P('tensor', 'expert')
- expert_gate_grad: float32 [8, 2048, 1408], P('expert', None, 'tensor')
- expert_up_grad: float32 [8, 2048, 1408], P('expert', None, 'tensor')
- expert_down_grad: float32 [8, 1408, 2048], P('expert', 'tensor')
The draws below stay inside these ranges and needn't reach their ends.
Inputs may be any that keep to these rules, and one draw needn't show every extreme that they name: positions[m, t] is 32 times the number of strict ancestors of the segment of t in its tree, plus the index of t within its segment. parents[m, j, 0] = 0 for the root segment; for s > 0, parents[m, j, s] < s is the parent of segment s. `routes`: each token names 4 different experts. route_slots[m, t, k] counts the pairs (t', k') before (t, k), in the order of token then route, among the 128 tokens of the same tree, whose route names the same expert.
All inputs are finite; a program needn't handle non-finite values.
Results may differ from the reference program's by a relative error of at most 0.02.
Values may be sent and summed in bfloat16 or wider, within the bound.
A program may use at most 192 MiB of HBM per device.

```python
import jax
import jax.numpy as jnp
from jax import lax

D = 2048
HEADS = 16
HD = 128
FE = 1408
FS = 5632
TOP = 4
MB = 2
SEQ = 128
SEG = 32
NSEG = 4
TOK = 1024
EXPERTS = 8
CAP = 80
N_EXPERT = 8


def tree_parents(key):
    tree_key = jax.random.fold_in(key, 11)
    segment_ids = jnp.arange(NSEG, dtype=jnp.int32)
    raw_draw = jax.random.randint(tree_key, (MB, N_EXPERT, NSEG), 0, 1 << 20, dtype=jnp.int32)
    random_parent = raw_draw % jnp.maximum(segment_ids, 1)
    chain_parent = jnp.maximum(segment_ids - 1, 0)
    tree_ids = jnp.arange(N_EXPERT, dtype=jnp.int32)[None, :, None]
    return jnp.where(tree_ids == 0, chain_parent, random_parent).astype(jnp.int32)


def draw_parents(key, part):
    return tree_parents(key)


def draw_positions(key, part):
    parent_ids = tree_parents(key)
    segment_ids = jnp.arange(NSEG, dtype=jnp.int32)

    def deepen(loop_index, depths):
        parent_depth = jnp.take_along_axis(depths, parent_ids, axis=2)
        return jnp.where(segment_ids == loop_index, parent_depth + 1, depths)
    depths = lax.fori_loop(1, NSEG, deepen, jnp.zeros((MB, N_EXPERT, NSEG), jnp.int32))
    within = jnp.arange(SEG, dtype=jnp.int32)
    offsets = depths[..., None] * SEG + within
    return offsets.reshape(MB, N_EXPERT * SEQ).astype(jnp.int32)


def route_pairs(key):
    route_key = jax.random.fold_in(key, 23)
    hot_key, score_key, force_key = jax.random.split(route_key, 3)
    blocks = MB * N_EXPERT
    expert_ids = jnp.arange(EXPERTS, dtype=jnp.int32)
    block_ids = jnp.arange(blocks, dtype=jnp.int32)[:, None, None]
    hot_expert = jax.random.randint(hot_key, (blocks, 1, 1), 0, EXPERTS, dtype=jnp.int32)
    noise_draw = jax.random.randint(score_key, (blocks, SEQ, EXPERTS), 0, 1 << 16, dtype=jnp.int32)
    forced_draw = jax.random.randint(force_key, (blocks, SEQ, 1), 0, 2, dtype=jnp.int32)
    forced = jnp.where(block_ids % N_EXPERT == 0, 1, forced_draw)
    scores = noise_draw * EXPERTS + expert_ids + forced * (expert_ids == hot_expert).astype(jnp.int32) * (1 << 24)
    chosen = lax.top_k(scores, TOP)[1].astype(jnp.int32)
    onehot = (chosen[..., None] == expert_ids).astype(jnp.int32).reshape(blocks, SEQ * TOP, EXPERTS)
    earlier = jnp.cumsum(onehot, axis=1) - onehot
    slot_ids = jnp.sum(earlier * onehot, axis=2).reshape(MB, N_EXPERT * SEQ, TOP)
    return (chosen.reshape(MB, N_EXPERT * SEQ, TOP), slot_ids.astype(jnp.int32))


def draw_routes(key, part):
    return route_pairs(key)[0]


def draw_route_slots(key, part):
    return route_pairs(key)[1]


def with_spikes(array, stream_key, source, target, shards_of, factor):
    def block_of(axis_at):
        return (jnp.arange(array.shape[axis_at]) // (array.shape[axis_at] // shards_of)).reshape((-1,) + (1,) * (array.ndim - 1 - axis_at))

    one_side = jax.random.permutation(stream_key, shards_of)[block_of(target)]
    other_side = (block_of(target) + shards_of // 2) % shards_of
    return jnp.where((block_of(source) == one_side) | (block_of(source) == other_side), factor * array, array)


def block_scale(key, shape, cuts, smallest, largest):
    level = 1.0
    for position, shards_of in cuts:
        heights = jax.random.uniform(jax.random.fold_in(jax.random.fold_in(key, 6), position), (shards_of,), jnp.float32, smallest / len(cuts), largest / len(cuts))
        level = level * jnp.repeat(jnp.exp(heights), shape[position] // shards_of).reshape((-1,) + (1,) * (len(shape) - 1 - position))
    return level


def centred(own_key, dims, spread, bound, cuts=(), kind=jnp.bfloat16):
    gain = block_scale(own_key, dims, cuts, -0.22, 0.18) if cuts else 1.0
    values = jax.random.normal(own_key, dims, jnp.float32) * spread * gain
    return jnp.minimum(jnp.maximum(values, -bound), bound).astype(kind)


def gaussian_with(stream_key, extent, deviation, limit, shards, heavy, held_as=jnp.bfloat16):
    entries = deviation * jax.random.normal(stream_key, extent, jnp.float32)
    if shards:
        entries = entries * block_scale(stream_key, extent, shards, -0.22, 0.18)
    return jnp.clip(with_spikes(entries, jax.random.fold_in(stream_key, 3), *heavy), -limit, limit).astype(held_as)


def setup_inputs(seed: int = 0) -> dict:
    key_list = jax.random.split(jax.random.key(seed), 20)
    layer_input = centred(key_list[0], (MB, TOK, D), 1.0, 6.0, ((1, 8),))
    positions = draw_positions(jax.random.fold_in(key_list[19], 71), 0)
    parents = draw_parents(jax.random.fold_in(key_list[19], 71), 0)
    routes = draw_routes(jax.random.fold_in(key_list[19], 71), 0)
    route_slots = draw_route_slots(jax.random.fold_in(key_list[19], 71), 0)
    norm1_gain = jnp.clip(1.0 + 0.1 * jax.random.normal(key_list[5], (D,), jnp.float32), 0.5, 1.5).astype(jnp.bfloat16)
    project_weight = centred(key_list[6], (D, 3, HEADS * HD), D ** -0.5, 0.125, ((0, 8), (2, 4)))
    project_bias = centred(key_list[7], (3, HEADS * HD), 0.1, 0.59765625, ((1, 32),))
    output_weight = centred(key_list[8], (HEADS * HD, D), (HEADS * HD // 32) ** -0.5, 0.75, ((0, 4), (1, 8)))
    norm2_gain = jnp.clip(1.0 + 0.1 * jax.random.normal(key_list[9], (D,), jnp.float32), 0.5, 1.5).astype(jnp.bfloat16)
    router_weight = centred(key_list[10], (D, EXPERTS), (4 * D) ** -0.5, 0.0625, ((0, 8),))
    shared_vector = centred(key_list[11], (D,), D ** -0.5, 0.125, ((0, 8),))
    shared_gate = centred(key_list[12], (D, FS), D ** -0.5, 0.125, ((0, 8), (1, 4)))
    shared_up = centred(key_list[13], (D, FS), D ** -0.5, 0.125, ((0, 8), (1, 4)))
    shared_down = centred(key_list[14], (FS, D), FS ** -0.5, 0.078125, ((0, 4), (1, 8)))
    expert_gate = centred(key_list[15], (EXPERTS, D, FE), D ** -0.5, 0.125, ((0, 8), (2, 4)))
    expert_up = centred(key_list[16], (EXPERTS, D, FE), D ** -0.5, 0.125, ((0, 8), (2, 4)))
    expert_down = centred(key_list[17], (EXPERTS, FE, D), FE ** -0.5, 0.15625, ((0, 8), (1, 4)))
    cotangent = gaussian_with(key_list[18], (MB, TOK, D), 1.0, 6.0, ((1, 8),), (1, 2, 8, 2.0))
    return {"layer_input": layer_input, "positions": positions, "parents": parents, "routes": routes, "route_slots": route_slots, "norm1_gain": norm1_gain, "project_weight": project_weight, "project_bias": project_bias, "output_weight": output_weight, "norm2_gain": norm2_gain, "router_weight": router_weight, "shared_vector": shared_vector, "shared_gate": shared_gate, "shared_up": shared_up, "shared_down": shared_down, "expert_gate": expert_gate, "expert_up": expert_up, "expert_down": expert_down, "cotangent": cotangent}


@jax.custom_vjp
def low(v):
    return lax.optimization_barrier(v.astype(jnp.bfloat16)).astype(jnp.float32)

@jax.custom_vjp
def low_back(v):
    return v

def low_keep(v):
    return (low(v), None)

def low_pass(kept, grad):
    return (grad,)

def back_keep(v):
    return (v, None)

def back_low(kept, grad):
    return (low(grad),)
low.defvjp(low_keep, low_pass)
low_back.defvjp(back_keep, back_low)
EPSILON = 1e-06
ROPE_BASE = 1000000.0
HIGHEST = lax.Precision.HIGHEST

def highest_dot(left_side, right_side):
    return jnp.dot(left_side, right_side, precision=HIGHEST, preferred_element_type=jnp.float32)

def rope_tables(position_row, head_size):
    half_size = head_size // 2
    inverse = ROPE_BASE ** (-(jnp.arange(half_size, dtype=jnp.float32) * 2.0 / head_size))
    angles = position_row.astype(jnp.float32)[:, None] * inverse[None, :]
    cosine = jnp.cos(angles)
    sine_table = jnp.sin(angles)
    return (jnp.concatenate([cosine, cosine], 1), jnp.concatenate([sine_table, sine_table], 1))

def rotate(vectors, cosine, sine_table):
    half_size = vectors.shape[-1] // 2
    turned = jnp.concatenate([-vectors[..., half_size:], vectors[..., :half_size]], -1)
    return vectors * cosine[:, None, :] + turned * sine_table[:, None, :]

def tree_mask(parent_row, seg_len):
    segment_count = parent_row.shape[0]
    segment_ids = jnp.arange(segment_count, dtype=jnp.int32)
    step_matrix = ((parent_row[:, None] == segment_ids[None, :]) & (segment_ids[:, None] > 0)).astype(jnp.float32)
    identity = jnp.eye(segment_count, dtype=jnp.float32)

    def extend(loop_index, reached):
        return jnp.minimum(identity + jnp.dot(step_matrix, reached, precision=HIGHEST), 1.0)
    reached = lax.fori_loop(0, segment_count, extend, identity)
    expanded = jnp.repeat(jnp.repeat(reached, seg_len, 0), seg_len, 1) > 0.5
    token_ids = jnp.arange(segment_count * seg_len, dtype=jnp.int32)
    return expanded & (token_ids[None, :] <= token_ids[:, None])

def forward(layer_in, gain_first, project_weight, project_bias, output_weight, gain_second, router_weight, shared_vector, shared_gate, shared_up, shared_down, expert_gate, expert_up, expert_down, position_rows, parent_rows, route_rows, slot_rows):
    score_scale = HD ** (-0.5)
    norm_one = lax.rsqrt(lax.optimization_barrier(jnp.mean(layer_in * layer_in, -1, keepdims=True)) + EPSILON)
    normed_one = low(layer_in * norm_one * gain_first)
    projected = low_back(highest_dot(normed_one, project_weight.reshape(D, 3 * HEADS * HD)) + project_bias.reshape(-1))
    projected = projected.reshape(TOK, 3, HEADS, HD)
    cosine, sine_table = rope_tables(position_rows, HD)
    queries = low(rotate(projected[:, 0], cosine, sine_table))
    key_rows = low(rotate(projected[:, 1], cosine, sine_table))
    values = low(projected[:, 2])

    def tree_attention(pieces):
        query_tree, key_tree, value_tree, parent_row = pieces
        allowed = tree_mask(parent_row, SEG)
        scores = low_back(jnp.einsum('qhd,khd->hqk', query_tree, key_tree, precision=HIGHEST) * score_scale)
        scores = jnp.where(allowed[None], scores, -1e+30)
        attention_probs = low(jax.nn.softmax(scores, axis=-1))
        return jnp.einsum('hqk,khd->qhd', attention_probs, value_tree, precision=HIGHEST)
    heads_out = lax.map(jax.checkpoint(tree_attention), (queries.reshape(N_EXPERT, SEQ, HEADS, HD), key_rows.reshape(N_EXPERT, SEQ, HEADS, HD), values.reshape(N_EXPERT, SEQ, HEADS, HD), parent_rows))
    heads_out = low_back(low(heads_out.reshape(TOK, HEADS * HD)))
    attention = low_back(highest_dot(heads_out, output_weight))
    hidden_state = layer_in + attention
    norm_two = lax.rsqrt(lax.optimization_barrier(jnp.mean(hidden_state * hidden_state, -1, keepdims=True)) + EPSILON)
    normed_two = low(hidden_state * norm_two * gain_second)
    logits = low_back(highest_dot(normed_two, router_weight))
    router_prob = jax.nn.softmax(logits, axis=-1)
    picked = jnp.take_along_axis(router_prob, route_rows, axis=1)
    route_gates = picked / lax.optimization_barrier(jnp.sum(picked, -1, keepdims=True))
    shared_scale = jax.nn.sigmoid(low_back(highest_dot(normed_two, shared_vector[:, None]))[:, 0])
    gate_shared = low_back(highest_dot(normed_two, shared_gate))
    up_shared = low_back(highest_dot(normed_two, shared_up))
    hidden_shared = low(jax.nn.silu(gate_shared) * up_shared)
    shared_out = low_back(highest_dot(hidden_shared, shared_down))
    source_ids = jnp.arange(TOK, dtype=jnp.int32) // SEQ
    valid = slot_rows < CAP
    slot_index = route_rows * (N_EXPERT * CAP) + source_ids[:, None] * CAP + jnp.minimum(slot_rows, CAP - 1)
    slot_total = EXPERTS * N_EXPERT * CAP
    token_ids = jnp.broadcast_to(jnp.arange(TOK, dtype=jnp.int32)[:, None], (TOK, TOP))
    target = jnp.where(valid, slot_index, slot_total).astype(jnp.int32).reshape(-1)
    slot_table = jnp.full((slot_total,), TOK, jnp.int32).at[target].set(token_ids.reshape(-1), mode='drop')
    padded = jnp.concatenate([normed_two, jnp.zeros((1, D), normed_two.dtype)], 0)
    owner_rows = padded[slot_table].reshape(EXPERTS, N_EXPERT * CAP, D)

    def run_expert(pieces):
        row_block, gate_matrix, up_matrix, down_matrix = pieces
        gate_expert = low_back(highest_dot(row_block, gate_matrix))
        up_expert = low_back(highest_dot(row_block, up_matrix))
        hidden_expert = low(jax.nn.silu(gate_expert) * up_expert)
        return highest_dot(hidden_expert, down_matrix)
    expert_out = lax.map(jax.checkpoint(run_expert), (owner_rows, expert_gate, expert_up, expert_down)).reshape(slot_total, D)
    keep_mask = valid.astype(normed_two.dtype)
    safe_index = jnp.where(valid, slot_index, 0).astype(jnp.int32)
    pair_out = low_back(expert_out[safe_index]) * keep_mask[..., None]
    routed = lax.optimization_barrier(jnp.sum(route_gates[..., None] * pair_out, 1))
    return hidden_state + shared_scale[:, None] * shared_out + routed

def reference(layer_input, positions, parents, routes, route_slots, norm1_gain, project_weight, project_bias, output_weight, norm2_gain, router_weight, shared_vector, shared_gate, shared_up, shared_down, expert_gate, expert_up, expert_down, cotangent):
    weights = [weight_array.astype(jnp.float32) for weight_array in (norm1_gain, project_weight, project_bias, output_weight, norm2_gain, router_weight, shared_vector, shared_gate, shared_up, shared_down, expert_gate, expert_up, expert_down)]
    running = [jnp.zeros(weight_array.shape, jnp.float32) for weight_array in weights]
    outputs = []
    input_grads = []
    for batch_index in range(MB):

        def layer_call(layer_in, *parameters):
            return forward(layer_in, *parameters, positions[batch_index], parents[batch_index], routes[batch_index], route_slots[batch_index])
        result, pullback = jax.vjp(layer_call, layer_input[batch_index].astype(jnp.float32), *weights)
        gradient = pullback(cotangent[batch_index].astype(jnp.float32))
        outputs.append(result.astype(jnp.bfloat16))
        input_grads.append(gradient[0])
        running = [total_sum + grad_part for total_sum, grad_part in zip(running, gradient[1:])]
    return (jnp.stack(outputs), jnp.stack(input_grads), running[0], running[1], running[2], running[3], running[4], running[5], running[6], running[7], running[8], running[9], running[10], running[11], running[12])
```

```python
import jax
import jax.numpy as jnp
from jax import lax
from jax.sharding import Mesh, PartitionSpec as P

HD = 128
SEG = 32


EPSILON = 1e-06
ROPE_BASE = 1000000.0


def product(left_side, right_side):
    return jnp.dot(left_side, right_side, preferred_element_type=jnp.float32)


def product_left(left_side, right_side):
    return lax.dot_general(
        left_side, right_side, (((0,), (0,)), ((), ())), preferred_element_type=jnp.float32
    )


def product_right(left_side, right_side):
    return lax.dot_general(
        left_side, right_side, (((1,), (1,)), ((), ())), preferred_element_type=jnp.float32
    )


def silu_slope(inputs):
    sigmoid_value = jax.nn.sigmoid(inputs)
    return sigmoid_value * (1.0 + inputs * (1.0 - sigmoid_value))


def rope_tables(position_row, head_size):
    half_size = head_size // 2
    inverse = ROPE_BASE ** (-(jnp.arange(half_size, dtype=jnp.float32) * 2.0 / head_size))
    angles = position_row.astype(jnp.float32)[:, None] * inverse[None, :]
    cosine = jnp.cos(angles)
    sine_table = jnp.sin(angles)
    return (jnp.concatenate([cosine, cosine], 1), jnp.concatenate([sine_table, sine_table], 1))


def rotate(vectors, cosine, sine_table):
    half_size = vectors.shape[-1] // 2
    turned = jnp.concatenate([-vectors[..., half_size:], vectors[..., :half_size]], -1)
    return vectors * cosine[:, None, :] + turned * sine_table[:, None, :]


def unrotate(gradient, cosine, sine_table):
    half_size = gradient.shape[-1] // 2
    scaled = gradient * sine_table[:, None, :]
    turned = jnp.concatenate([scaled[..., half_size:], -scaled[..., :half_size]], -1)
    return gradient * cosine[:, None, :] + turned


def tree_mask(parent_row, seg_len):
    segment_count = parent_row.shape[0]
    segment_ids = jnp.arange(segment_count, dtype=jnp.int32)
    step_matrix = (
        (parent_row[:, None] == segment_ids[None, :]) & (segment_ids[:, None] > 0)
    ).astype(jnp.float32)
    identity = jnp.eye(segment_count, dtype=jnp.float32)

    def extend(loop_index, reached):
        return jnp.minimum(
            identity + jnp.dot(step_matrix, reached, precision=lax.Precision.HIGHEST), 1.0
        )

    reached = lax.fori_loop(0, segment_count, extend, identity)
    expanded = jnp.repeat(jnp.repeat(reached, seg_len, 0), seg_len, 1) > 0.5
    token_ids = jnp.arange(segment_count * seg_len, dtype=jnp.int32)
    return expanded & (token_ids[None, :] <= token_ids[:, None])


def gathered_shards(
    layer_input,
    positions,
    parents,
    routes,
    route_slots,
    norm1_gain,
    project_weight,
    project_bias,
    output_weight,
    norm2_gain,
    router_weight,
    shared_vector,
    shared_gate,
    shared_up,
    shared_down,
    expert_gate,
    expert_up,
    expert_down,
    cotangent,
):
    micro_count, seq_rows, model_width = layer_input.shape
    top_count = routes.shape[2]
    expert_count = router_weight.shape[1]
    capacity = seq_rows * top_count * 5 // (4 * expert_count)
    slot_total = expert_count * capacity
    gathered = (
        lax.all_gather(norm1_gain, "expert", axis=0, tiled=True),
        lax.all_gather(project_weight, "expert", axis=0, tiled=True),
        lax.all_gather(project_bias, "expert", axis=1, tiled=True),
        lax.all_gather(output_weight, "expert", axis=1, tiled=True),
        lax.all_gather(norm2_gain, "expert", axis=0, tiled=True),
        lax.all_gather(router_weight, "expert", axis=0, tiled=True),
        lax.all_gather(shared_vector, "expert", axis=0, tiled=True),
        lax.all_gather(shared_gate, "expert", axis=0, tiled=True),
        lax.all_gather(shared_up, "expert", axis=0, tiled=True),
        lax.all_gather(shared_down, "expert", axis=1, tiled=True),
    )
    (
        gain_first,
        project_in,
        bias_in,
        project_out,
        gain_second,
        router_full,
        vector_full,
        shared_gates,
        shared_ups,
        shared_downs,
    ) = gathered
    local_width = project_in.shape[2]
    head_count = local_width // HD
    shared_local = shared_gates.shape[1]
    project_flat = project_in.reshape(model_width, 3 * local_width)
    bias_flat = bias_in.astype(jnp.float32).reshape(3 * local_width)
    gain_one = gain_first.astype(jnp.float32)
    gain_two = gain_second.astype(jnp.float32)
    small_weights = jnp.concatenate([router_full, vector_full[:, None]], 1)
    expert_gates = expert_gate[0]
    expert_ups = expert_up[0]
    expert_downs = expert_down[0]
    score_scale = HD ** (-0.5)
    expert_ids = jnp.arange(expert_count, dtype=jnp.int32)
    pair_ids = jnp.arange(seq_rows * top_count, dtype=jnp.int32).reshape(seq_rows, top_count)
    zero_row = jnp.zeros((1, model_width), jnp.bfloat16)
    stored = []
    layer_outputs = []
    for batch_index in range(micro_count):
        input_rows = layer_input[batch_index].astype(jnp.float32)
        norm_one = lax.rsqrt(jnp.mean(input_rows * input_rows, -1, keepdims=True) + EPSILON)
        normed_one = (input_rows * norm_one * gain_one).astype(jnp.bfloat16)
        projected = (product(normed_one, project_flat) + bias_flat).reshape(
            seq_rows, 3, head_count, HD
        )
        cosine, sine_table = rope_tables(positions[batch_index], HD)
        queries = rotate(projected[:, 0], cosine, sine_table).astype(jnp.bfloat16)
        key_rows = rotate(projected[:, 1], cosine, sine_table).astype(jnp.bfloat16)
        values = projected[:, 2].astype(jnp.bfloat16)
        allowed = tree_mask(parents[batch_index, 0], SEG)
        scores = (
            jnp.einsum("qhd,khd->hqk", queries, key_rows, preferred_element_type=jnp.float32)
            * score_scale
        )
        masked = jnp.where(allowed[None], scores, -1e30)
        highest = jnp.max(masked, -1, keepdims=True)
        exponent = jnp.exp(masked - highest)
        row_total = jnp.sum(exponent, -1, keepdims=True)
        attention_probs = exponent / row_total
        log_total = highest + jnp.log(row_total)
        heads_out = (
            jnp.einsum(
                "hqk,khd->qhd",
                attention_probs.astype(jnp.bfloat16),
                values,
                preferred_element_type=jnp.float32,
            )
            .astype(jnp.bfloat16)
            .reshape(seq_rows, local_width)
        )
        attention = lax.psum(product(heads_out, project_out), "tensor")
        hidden_state = input_rows + attention
        norm_two = lax.rsqrt(jnp.mean(hidden_state * hidden_state, -1, keepdims=True) + EPSILON)
        normed_two = (hidden_state * norm_two * gain_two).astype(jnp.bfloat16)
        small_logits = product(normed_two, small_weights)
        router_prob = jax.nn.softmax(small_logits[:, :expert_count], axis=-1)
        onehot = (routes[batch_index][..., None] == expert_ids).astype(jnp.float32)
        picked = jnp.sum(onehot * router_prob[:, None, :], -1)
        picked_sum = jnp.sum(picked, -1, keepdims=True)
        route_gates = picked / picked_sum
        shared_scale = jax.nn.sigmoid(small_logits[:, expert_count])
        gate_shared = product(normed_two, shared_gates)
        up_shared = product(normed_two, shared_ups)
        hidden_shared = (jax.nn.silu(gate_shared) * up_shared).astype(jnp.bfloat16)
        shared_part = product(hidden_shared, shared_downs)
        slot_rows = route_slots[batch_index]
        valid = slot_rows < capacity
        keep_mask = valid.astype(jnp.float32)
        slot_index = routes[batch_index] * capacity + jnp.minimum(slot_rows, capacity - 1)
        safe_index = jnp.where(valid, slot_index, 0)
        target = jnp.where(valid, slot_index, slot_total).reshape(-1)
        slot_table = (
            jnp.full((slot_total,), seq_rows * top_count, jnp.int32)
            .at[target]
            .set(pair_ids.reshape(-1), mode="drop")
        )
        padded = jnp.concatenate([normed_two, zero_row], 0)
        outgoing = padded[slot_table // top_count].reshape(expert_count, capacity, model_width)
        received = lax.all_to_all(outgoing, "expert", split_axis=0, concat_axis=0, tiled=True)
        run_owner_rows = received.reshape(-1, model_width)
        run_gate_expert = product(run_owner_rows, expert_gates)
        run_up_expert = product(run_owner_rows, expert_ups)
        run_hidden_expert = (jax.nn.silu(run_gate_expert) * run_up_expert).astype(jnp.bfloat16)
        expert_rows = product(run_hidden_expert, expert_downs).reshape(
            received.shape[0], received.shape[1], model_width
        )
        returned = lax.all_to_all(expert_rows, "expert", split_axis=0, concat_axis=0, tiled=True)
        returned, received = (returned, received)
        pair_out = returned.reshape(slot_total, -1)[safe_index] * keep_mask[..., None]
        routed = jnp.sum(route_gates[..., None] * pair_out, 1)
        shared_out, routed_full = lax.psum((shared_part, routed), "tensor")
        layer_outputs.append(
            (hidden_state + shared_scale[:, None] * shared_out + routed_full).astype(jnp.bfloat16)
        )
        stored.append(
            (
                input_rows,
                norm_one,
                normed_one,
                cosine,
                sine_table,
                queries,
                key_rows,
                values,
                allowed,
                log_total,
                heads_out,
                hidden_state,
                norm_two,
                normed_two,
                router_prob,
                onehot,
                picked_sum,
                route_gates,
                shared_scale,
                gate_shared,
                up_shared,
                hidden_shared,
                shared_out,
                pair_out,
                safe_index,
                keep_mask,
                slot_table,
                received,
            )
        )
    grad_gain_one = jnp.zeros((model_width,), jnp.float32)
    grad_gain_two = jnp.zeros((model_width,), jnp.float32)
    grad_project = jnp.zeros((model_width, 3 * local_width), jnp.float32)
    grad_bias = jnp.zeros((3 * local_width,), jnp.float32)
    grad_output = jnp.zeros((local_width, model_width), jnp.float32)
    grad_small = jnp.zeros((model_width, expert_count + 1), jnp.float32)
    grad_shared_gate = jnp.zeros((model_width, shared_local), jnp.float32)
    grad_shared_up = jnp.zeros((model_width, shared_local), jnp.float32)
    grad_shared_down = jnp.zeros((shared_local, model_width), jnp.float32)
    grad_expert_gate = jnp.zeros(expert_gates.shape, jnp.float32)
    grad_expert_up = jnp.zeros(expert_ups.shape, jnp.float32)
    grad_expert_down = jnp.zeros(expert_downs.shape, jnp.float32)
    input_grads = [None] * micro_count
    for batch_index in reversed(range(micro_count)):
        (
            input_rows,
            norm_one,
            normed_one,
            cosine,
            sine_table,
            queries,
            key_rows,
            values,
            allowed,
            log_total,
            heads_out,
            hidden_state,
            norm_two,
            normed_two,
            router_prob,
            onehot,
            picked_sum,
            route_gates,
            shared_scale,
            gate_shared,
            up_shared,
            hidden_shared,
            shared_out,
            pair_out,
            safe_index,
            keep_mask,
            slot_table,
            received,
        ) = stored[batch_index]
        upstream = cotangent[batch_index].astype(jnp.float32)
        shared_grad = (shared_scale[:, None] * upstream).astype(jnp.bfloat16)
        scale_grad = jnp.sum(upstream * shared_out, -1) * shared_scale * (1.0 - shared_scale)
        gate_part = jnp.sum(upstream[:, None, :] * pair_out, -1)
        pair_grad = (
            (route_gates[..., None] * upstream[:, None, :])
            .astype(jnp.bfloat16)
            .reshape(seq_rows * top_count, model_width)
        )
        outgoing_grad = jnp.concatenate([pair_grad, zero_row], 0)[slot_table].reshape(
            expert_count, capacity, model_width
        )
        arrived = lax.all_to_all(outgoing_grad, "expert", split_axis=0, concat_axis=0, tiled=True)
        owner_rows = received.reshape(-1, model_width)
        owner_grads = arrived.reshape(-1, model_width)
        gate_expert = product(owner_rows, expert_gates)
        up_expert = product(owner_rows, expert_ups)
        active_expert = jax.nn.silu(gate_expert)
        hidden_expert = (active_expert * up_expert).astype(jnp.bfloat16)
        hidden_expert_grad = product_right(owner_grads, expert_downs)
        grad_expert_down = grad_expert_down + product_left(hidden_expert, owner_grads)
        gate_expert_grad = (hidden_expert_grad * up_expert * silu_slope(gate_expert)).astype(
            jnp.bfloat16
        )
        up_expert_grad = (hidden_expert_grad * active_expert).astype(jnp.bfloat16)
        grad_expert_gate = grad_expert_gate + product_left(owner_rows, gate_expert_grad)
        grad_expert_up = grad_expert_up + product_left(owner_rows, up_expert_grad)
        row_grad = product_right(gate_expert_grad, expert_gates) + product_right(
            up_expert_grad, expert_ups
        )
        row_back = lax.all_to_all(
            row_grad.reshape(expert_count, capacity, model_width),
            "expert",
            split_axis=0,
            concat_axis=0,
            tiled=True,
        )
        routed_back = jnp.sum(
            row_back.reshape(slot_total, model_width)[safe_index] * keep_mask[..., None], 1
        )
        hidden_shared_grad = product_right(shared_grad, shared_downs)
        grad_shared_down = grad_shared_down + product_left(hidden_shared, shared_grad)
        gate_shared_grad = (hidden_shared_grad * up_shared * silu_slope(gate_shared)).astype(
            jnp.bfloat16
        )
        up_shared_grad = (hidden_shared_grad * jax.nn.silu(gate_shared)).astype(jnp.bfloat16)
        grad_shared_gate = grad_shared_gate + product_left(normed_two, gate_shared_grad)
        grad_shared_up = grad_shared_up + product_left(normed_two, up_shared_grad)
        normed_part = (
            product_right(gate_shared_grad, shared_gates)
            + product_right(up_shared_grad, shared_ups)
            + routed_back
        )
        normed_sum, gate_grad = lax.psum((normed_part, gate_part), "tensor")
        picked_grad = (gate_grad - jnp.sum(gate_grad * route_gates, -1, keepdims=True)) / picked_sum
        prob_grad = jnp.sum(picked_grad[..., None] * onehot, 1)
        logit_grad = router_prob * (prob_grad - jnp.sum(router_prob * prob_grad, -1, keepdims=True))
        small_grad = jnp.concatenate([logit_grad, scale_grad[:, None]], 1).astype(jnp.bfloat16)
        grad_small = grad_small + product_left(normed_two, small_grad)
        normed_two_grad = normed_sum + product_right(small_grad, small_weights)
        grad_gain_two = grad_gain_two + jnp.sum(normed_two_grad * hidden_state * norm_two, 0)
        scaled_two = normed_two_grad * gain_two
        hidden_grad = (
            upstream
            + norm_two * scaled_two
            - hidden_state * norm_two**3 * jnp.mean(scaled_two * hidden_state, -1, keepdims=True)
        )
        attention_grad = hidden_grad.astype(jnp.bfloat16)
        grad_output = grad_output + product_left(heads_out, attention_grad)
        heads_grad = (
            product_right(attention_grad, project_out)
            .astype(jnp.bfloat16)
            .reshape(seq_rows, head_count, HD)
        )
        scores = (
            jnp.einsum("qhd,khd->hqk", queries, key_rows, preferred_element_type=jnp.float32)
            * score_scale
        )
        masked = jnp.where(allowed[None], scores, -1e30)
        attention_probs = jnp.exp(masked - log_total)
        value_grad = jnp.einsum(
            "hqk,qhd->khd",
            attention_probs.astype(jnp.bfloat16),
            heads_grad,
            preferred_element_type=jnp.float32,
        )
        prob_grads = jnp.einsum(
            "qhd,khd->hqk", heads_grad, values, preferred_element_type=jnp.float32
        )
        score_grad = (
            attention_probs
            * (prob_grads - jnp.sum(attention_probs * prob_grads, -1, keepdims=True))
        ).astype(jnp.bfloat16)
        query_grad = (
            jnp.einsum("hqk,khd->qhd", score_grad, key_rows, preferred_element_type=jnp.float32)
            * score_scale
        )
        key_grad = (
            jnp.einsum("hqk,qhd->khd", score_grad, queries, preferred_element_type=jnp.float32)
            * score_scale
        )
        projected_grad = (
            jnp.stack(
                [
                    unrotate(query_grad, cosine, sine_table),
                    unrotate(key_grad, cosine, sine_table),
                    value_grad,
                ],
                1,
            )
            .astype(jnp.bfloat16)
            .reshape(seq_rows, 3 * local_width)
        )
        grad_bias = grad_bias + jnp.sum(projected_grad.astype(jnp.float32), 0)
        grad_project = grad_project + product_left(normed_one, projected_grad)
        normed_one_grad = lax.psum(
            product_right(projected_grad, project_flat).astype(jnp.bfloat16), "tensor"
        ).astype(jnp.float32)
        grad_gain_one = grad_gain_one + jnp.sum(normed_one_grad * input_rows * norm_one, 0)
        scaled_one = normed_one_grad * gain_one
        input_grads[batch_index] = (
            hidden_grad
            + norm_one * scaled_one
            - input_rows * norm_one**3 * jnp.mean(scaled_one * input_rows, -1, keepdims=True)
        )
    reduced = (
        lax.psum_scatter(
            grad_gain_one.astype(jnp.bfloat16), "expert", scatter_dimension=0, tiled=True
        ).astype(jnp.float32),
        lax.psum_scatter(
            grad_project.reshape(model_width, 3, local_width).astype(jnp.bfloat16),
            "expert",
            scatter_dimension=0,
            tiled=True,
        ).astype(jnp.float32),
        lax.psum_scatter(
            grad_bias.reshape(3, local_width).astype(jnp.bfloat16),
            "expert",
            scatter_dimension=1,
            tiled=True,
        ).astype(jnp.float32),
        lax.psum_scatter(
            grad_output.astype(jnp.bfloat16), "expert", scatter_dimension=1, tiled=True
        ).astype(jnp.float32),
        lax.psum_scatter(
            grad_gain_two.astype(jnp.bfloat16), "expert", scatter_dimension=0, tiled=True
        ).astype(jnp.float32),
        lax.psum_scatter(
            grad_small[:, :expert_count].astype(jnp.bfloat16),
            "expert",
            scatter_dimension=0,
            tiled=True,
        ).astype(jnp.float32),
        lax.psum_scatter(
            grad_small[:, expert_count].astype(jnp.bfloat16),
            "expert",
            scatter_dimension=0,
            tiled=True,
        ).astype(jnp.float32),
        lax.psum_scatter(
            grad_shared_gate.astype(jnp.bfloat16), "expert", scatter_dimension=0, tiled=True
        ).astype(jnp.float32),
        lax.psum_scatter(
            grad_shared_up.astype(jnp.bfloat16), "expert", scatter_dimension=0, tiled=True
        ).astype(jnp.float32),
        lax.psum_scatter(
            grad_shared_down.astype(jnp.bfloat16), "expert", scatter_dimension=1, tiled=True
        ).astype(jnp.float32),
    )
    return (
        jnp.stack(layer_outputs),
        jnp.stack(input_grads),
        reduced[0],
        reduced[1],
        reduced[2],
        reduced[3],
        reduced[4],
        reduced[5],
        reduced[6],
        reduced[7],
        reduced[8],
        reduced[9],
        grad_expert_gate[None],
        grad_expert_up[None],
        grad_expert_down[None],
    )


AXES = ("z", "x", "y", "c")
CHIPS = ("z", "x", "y")


def gather_chips(rows):
    return lax.all_gather(rows, CHIPS, axis=0, tiled=True)


def scatter_chips(rows):
    return lax.psum_scatter(rows, CHIPS, scatter_dimension=0, tiled=True)


def tree_masks(parent_rows, seg_len):
    tree_count, segment_count = parent_rows.shape
    segment_ids = jnp.arange(segment_count, dtype=jnp.int32)
    step_matrix = (
        (parent_rows[:, :, None] == segment_ids) & (segment_ids[:, None] > 0)
    )
    reached = jnp.broadcast_to(jnp.eye(segment_count, dtype=bool), step_matrix.shape)
    for _ in range(segment_count):
        reached = jnp.eye(segment_count, dtype=bool) | jnp.any(
            step_matrix[:, :, :, None] & reached[:, None, :, :], 2
        )
    expanded = jnp.repeat(jnp.repeat(reached, seg_len, 1), seg_len, 2)
    token_ids = jnp.arange(segment_count * seg_len, dtype=jnp.int32)
    return expanded & (token_ids[None, :] <= token_ids[:, None])


def turn(rows):
    half = rows.shape[-1] // 2
    return jnp.concatenate([-rows[..., half:], rows[..., :half]], -1)


def turn_back(rows):
    half = rows.shape[-1] // 2
    return jnp.concatenate([rows[..., half:], -rows[..., :half]], -1)


def chip_shards(
    layer_input,
    positions,
    parents,
    routes,
    route_slots,
    norm1_gain,
    project_weight,
    project_bias,
    output_weight,
    norm2_gain,
    router_weight,
    shared_vector,
    shared_gate,
    shared_up,
    shared_down,
    expert_gate,
    expert_up,
    expert_down,
    cotangent,
):
    f32, bf16 = jnp.float32, jnp.bfloat16
    micro_count, seq_rows, model_width = layer_input.shape
    top_count = routes.shape[2]
    expert_count = router_weight.shape[1]
    capacity = seq_rows * top_count * 5 // (4 * expert_count)
    z, x, y, c = [lax.axis_index(a) for a in AXES]
    here = z * 2 + x
    trees = expert_count
    tokens = trees * seq_rows
    own_rows = seq_rows // 2
    slice_rows = norm1_gain.shape[0]
    score_scale = HD ** (-0.5)

    def own(array):
        return lax.dynamic_slice(
            array, (c, y * own_rows, 0), (1, own_rows, model_width)
        )[0]

    own_input = own(layer_input)
    own_cotangent = own(cotangent)

    def mine(array):
        return lax.dynamic_index_in_dim(array, c, 0, keepdims=False).astype(bf16).reshape(-1)

    pieces = [
        norm1_gain,
        norm2_gain,
        shared_vector,
        router_weight.T.reshape(-1),
        project_bias.reshape(-1),
        mine(positions),
        mine(parents),
        mine(routes),
        mine(route_slots),
    ]
    sizes = [p.shape[0] for p in pieces]
    small = lax.all_gather(jnp.concatenate(pieces), AXES, axis=0, tiled=False)
    small = small.reshape(trees, 2, 2, -1)
    starts = [sum(sizes[:i]) for i in range(len(sizes))]

    def part(i):
        return small[..., starts[i] : starts[i] + sizes[i]]

    gain_one = part(0)[:, 0, 0].reshape(-1).astype(f32)
    gain_two = part(1)[:, 0, 0].reshape(-1).astype(f32)
    vector_full = part(2)[:, 0, 0].reshape(-1)
    router_full = (
        part(3)[:, 0, 0]
        .reshape(trees, expert_count, slice_rows)
        .transpose(1, 0, 2)
        .reshape(expert_count, model_width)
    )
    small_weights = jnp.concatenate([router_full, vector_full[None]], 0)
    bias_full = part(4).reshape(trees, 4, 3, -1).transpose(2, 1, 0, 3).reshape(3, -1)
    head = y * trees + here
    bias_head = lax.dynamic_slice(bias_full, (0, head * HD), (3, HD)).astype(f32)

    def by_tree(i):
        return lax.dynamic_index_in_dim(part(i)[:, 0], c, 1, keepdims=False)

    all_positions = by_tree(5).reshape(-1).astype(f32)
    all_parents = by_tree(6).astype(jnp.int32)
    all_routes = by_tree(7).reshape(tokens, top_count).astype(jnp.int32)
    all_slots = by_tree(8).reshape(tokens, top_count).astype(jnp.int32)

    local_heads = project_weight.shape[2] // HD
    half_rows = slice_rows // 2

    def swap_cores(array):
        return lax.all_to_all(array, "c", split_axis=0, concat_axis=0, tiled=True)

    def swap_chips(array):
        return lax.all_to_all(array, ("z", "x"), split_axis=0, concat_axis=0, tiled=True)

    def join_cores(array, axis):
        return lax.all_gather(array, "c", axis=axis, tiled=True)

    send = project_weight.transpose(1, 0, 2).reshape(3, 2, half_rows, local_heads, HD)
    send = send.transpose(1, 3, 0, 2, 4)
    send = swap_cores(send).reshape(2 * local_heads, 3, half_rows, HD)
    got = swap_chips(send)
    got = join_cores(got.transpose(1, 0, 2, 3)[:, :, None], 2)
    project_head = got.reshape(3, model_width, HD)
    send = output_weight.reshape(local_heads, HD, 2, half_rows).transpose(2, 0, 1, 3)
    send = swap_cores(send).reshape(2 * local_heads, HD, half_rows)
    got = swap_chips(send)
    got = join_cores(got.transpose(1, 0, 2)[:, :, None], 2)
    output_head = got.reshape(HD, model_width)

    sub = shared_down.shape[0] // trees
    send = jnp.stack(
        [shared_gate.T.reshape(trees, sub, -1), shared_up.T.reshape(trees, sub, -1), shared_down.reshape(trees, sub, -1)],
        1,
    )
    got = swap_chips(send).transpose(1, 2, 0, 3).reshape(3, sub, model_width)
    shared_three = join_cores(got, 1)
    expert_three = join_cores(jnp.stack([expert_gate[0].T, expert_up[0].T, expert_down[0]]), 1)
    routed_units = expert_three.shape[1]
    shared_units = shared_three.shape[1]
    three = jnp.concatenate([expert_three, shared_three], 1)
    gate_rows, up_rows, down_rows = three[0], three[1], three[2]

    all_input = gather_chips(own_input).astype(f32)
    all_cotangent = gather_chips(own_cotangent)
    norm_one = lax.rsqrt(jnp.mean(all_input * all_input, -1, keepdims=True) + EPSILON)
    normed_one = (all_input * norm_one * gain_one).astype(bf16)
    half_size = HD // 2
    inverse = ROPE_BASE ** (-(jnp.arange(half_size, dtype=f32) * 2.0 / HD))
    angles = all_positions[:, None] * inverse[None, :]
    cosine = jnp.cos(angles)
    sine = jnp.sin(angles)
    cosine = jnp.concatenate([cosine, cosine], 1)
    sine = jnp.concatenate([sine, sine], 1)
    raw = [product(normed_one, project_head[i]) + bias_head[i] for i in range(3)]
    tree_shape = (trees, seq_rows, HD)
    queries = (raw[0] * cosine + turn(raw[0]) * sine).astype(bf16).reshape(tree_shape)
    key_rows = (raw[1] * cosine + turn(raw[1]) * sine).astype(bf16).reshape(tree_shape)
    values = raw[2].astype(bf16).reshape(tree_shape)
    allowed = tree_masks(all_parents, SEG)
    scores = (
        jnp.einsum("tqd,tkd->tqk", queries, key_rows, preferred_element_type=f32)
        * score_scale
    )
    masked = jnp.where(allowed, scores, -1e30)
    highest = jnp.max(masked, -1, keepdims=True)
    exponent = jnp.exp(masked - highest)
    attention_probs = exponent / jnp.sum(exponent, -1, keepdims=True)
    probs_low = attention_probs.astype(bf16)
    heads_out = (
        jnp.einsum("tqk,tkd->tqd", probs_low, values, preferred_element_type=f32)
        .astype(bf16)
        .reshape(tokens, HD)
    )
    attention = scatter_chips(product(heads_out, output_head).astype(bf16)).astype(f32)
    own_rows_in = own_input.astype(f32)
    own_norm_one = lax.rsqrt(jnp.mean(own_rows_in * own_rows_in, -1, keepdims=True) + EPSILON)
    hidden_state = own_rows_in + attention
    norm_two = lax.rsqrt(jnp.mean(hidden_state * hidden_state, -1, keepdims=True) + EPSILON)
    own_normed_two = (hidden_state * norm_two * gain_two).astype(bf16)

    def route(rows, route_rows):
        logits = product_right(small_weights, rows)
        prob = jax.nn.softmax(logits[:expert_count], axis=0)
        expert_ids = jnp.arange(expert_count, dtype=jnp.int32)
        onehot = (route_rows.T[:, None, :] == expert_ids[None, :, None]).astype(f32)
        picked_sum = jnp.sum(jnp.sum(onehot, 0) * prob, 0, keepdims=True)
        scale = jax.nn.sigmoid(logits[expert_count])
        return prob, onehot, picked_sum, scale

    normed_two = gather_chips(own_normed_two)
    prob, onehot, picked_sum, shared_scale = route(normed_two, all_routes)
    kept = (all_slots.T < capacity).astype(f32)
    gates = jnp.sum(onehot * kept[:, None, :], 0) * prob / picked_sum
    gate_here = lax.dynamic_index_in_dim(gates, here, 0, keepdims=False)

    scales = jnp.concatenate(
        [
            jnp.broadcast_to(gate_here, (routed_units, tokens)),
            jnp.broadcast_to(shared_scale, (shared_units, tokens)),
        ],
        0,
    )
    gate_units = product_right(gate_rows, normed_two)
    up_units = product_right(up_rows, normed_two)
    grad_units = product_right(down_rows, all_cotangent)
    sigmoid = jax.nn.sigmoid(gate_units)
    active = gate_units * sigmoid
    hidden = active * up_units
    both = hidden * grad_units
    expert_dot = jnp.sum(both[:routed_units], 0)
    shared_dot = jnp.sum(both[routed_units:], 0)
    scaled_hidden = (hidden * scales).astype(bf16)
    hidden_grad = grad_units * scales
    gate_grad = (
        hidden_grad * up_units * (sigmoid * (1.0 + gate_units * (1.0 - sigmoid)))
    ).astype(bf16)
    up_grad = (hidden_grad * active).astype(bf16)
    ffn_part = product_left(scaled_hidden, down_rows).astype(bf16)
    normed_part = (product_left(gate_grad, gate_rows) + product_left(up_grad, up_rows)).astype(bf16)
    dots = jnp.where(jnp.arange(expert_count)[:, None] == here, expert_dot, 0.0)
    dots = jnp.concatenate([dots, shared_dot[None]], 0)
    ffn_out = scatter_chips(ffn_part).astype(f32)
    own_output = (hidden_state + ffn_out).astype(bf16)
    normed_sum = scatter_chips(normed_part).astype(f32)
    all_dots = lax.psum(dots, CHIPS)
    three_grad = jnp.stack(
        [product(gate_grad, normed_two), product(up_grad, normed_two), product(scaled_hidden, all_cotangent)]
    ).astype(bf16)

    valid_gate = jnp.sum(onehot * kept[:, None, :], 0)
    every_gate = jnp.sum(onehot, 0) * prob / picked_sum
    kept_dots = all_dots[:expert_count] * valid_gate
    picked_grad = (kept_dots - jnp.sum(kept_dots * every_gate, 0, keepdims=True)) / picked_sum
    prob_grad = picked_grad * jnp.sum(onehot, 0)
    logit_grad = prob * (prob_grad - jnp.sum(prob * prob_grad, 0, keepdims=True))
    scale_grad = all_dots[expert_count] * shared_scale * (1.0 - shared_scale)
    small_grad = jnp.concatenate([logit_grad, scale_grad[None]], 0).astype(bf16)
    first = here * seq_rows + y * own_rows
    own_small = lax.dynamic_slice(small_grad, (0, first), (expert_count + 1, own_rows))
    grad_small = product(own_small, own_normed_two)
    normed_two_grad = normed_sum + product_left(own_small, small_weights)
    upstream = own_cotangent.astype(f32)
    grad_gain_two = jnp.sum(normed_two_grad * hidden_state * norm_two, 0)
    scaled_two = normed_two_grad * gain_two
    hidden_grad_rows = (
        upstream
        + norm_two * scaled_two
        - hidden_state * norm_two**3 * jnp.mean(scaled_two * hidden_state, -1, keepdims=True)
    )
    attention_grad = gather_chips(hidden_grad_rows.astype(bf16))

    output_grad = product_left(heads_out, attention_grad).astype(bf16)
    heads_grad = product_right(attention_grad, output_head).astype(bf16).reshape(tree_shape)
    value_grad = jnp.einsum("tqk,tqd->tkd", probs_low, heads_grad, preferred_element_type=f32)
    prob_grads = jnp.einsum("tqd,tkd->tqk", heads_grad, values, preferred_element_type=f32)
    score_grad = (
        attention_probs
        * (prob_grads - jnp.sum(attention_probs * prob_grads, -1, keepdims=True))
    ).astype(bf16)
    query_grad = jnp.einsum("tqk,tkd->tqd", score_grad, key_rows, preferred_element_type=f32)
    key_grad = jnp.einsum("tqk,tqd->tkd", score_grad, queries, preferred_element_type=f32)
    query_grad = (query_grad * score_scale).reshape(tokens, HD)
    key_grad = (key_grad * score_scale).reshape(tokens, HD)
    query_grad = query_grad * cosine + turn_back(query_grad * sine)
    key_grad = key_grad * cosine + turn_back(key_grad * sine)
    raw_grads = [g.astype(bf16) for g in (query_grad, key_grad, value_grad.reshape(tokens, HD))]
    bias_grad = jnp.stack([jnp.sum(g.astype(f32), 0) for g in raw_grads])
    project_grad = jnp.stack([product_left(normed_one, g) for g in raw_grads]).astype(bf16)
    normed_part = sum(product_right(g, project_head[i]) for i, g in enumerate(raw_grads))
    normed_one_grad = scatter_chips(normed_part.astype(bf16)).astype(f32)
    grad_gain_one = jnp.sum(normed_one_grad * own_rows_in * own_norm_one, 0)
    scaled_one = normed_one_grad * gain_one
    own_grad = (
        hidden_grad_rows
        + own_norm_one * scaled_one
        - own_rows_in * own_norm_one**3 * jnp.mean(scaled_one * own_rows_in, -1, keepdims=True)
    )
    layer_output = lax.all_gather(own_output, ("c", "y"), axis=0, tiled=True).reshape(micro_count, seq_rows, model_width)
    input_grad = lax.all_gather(own_grad, ("c", "y"), axis=0, tiled=True).reshape(micro_count, seq_rows, model_width)

    bias_place = lax.dynamic_update_slice(jnp.zeros((3, bias_full.shape[1]), f32), bias_grad, (0, head * HD))
    vectors = jnp.concatenate([grad_small, grad_gain_one[None], grad_gain_two[None]], 0)
    vectors = lax.psum(jnp.concatenate([vectors.reshape(-1), bias_place.reshape(-1)]), AXES)
    split = (expert_count + 3) * model_width
    bias_sum = vectors[split:].reshape(3, -1)
    vectors = lax.dynamic_slice(vectors[:split].reshape(-1, model_width), (0, here * slice_rows), (expert_count + 3, slice_rows))
    bias_width = project_bias.shape[1]
    bias_out = lax.dynamic_slice(bias_sum, (0, ((y * 2 + c) * trees + here) * bias_width), (3, bias_width))

    def sum_cores(array, axis):
        return lax.psum_scatter(array, "c", scatter_dimension=axis, tiled=True)

    send = project_grad.reshape(3, trees, 2, half_rows, HD)
    send = sum_cores(send, 2).reshape(3, trees, half_rows, HD).transpose(1, 0, 2, 3)
    got = swap_chips(send).reshape(2, local_heads, 3, half_rows, HD)
    got = swap_cores(got).reshape(2, local_heads, 3, half_rows, HD)
    project_out = got.transpose(0, 3, 2, 1, 4).reshape(slice_rows, 3, local_heads * HD).astype(f32)
    send = output_grad.reshape(HD, trees, 2, half_rows)
    send = sum_cores(send, 2).reshape(HD, trees, half_rows).transpose(1, 0, 2)
    got = swap_chips(send).reshape(2, local_heads, HD, half_rows)
    got = swap_cores(got).reshape(2, local_heads, HD, half_rows)
    output_out = got.transpose(1, 2, 0, 3).reshape(local_heads * HD, slice_rows).astype(f32)
    expert_sum = sum_cores(three_grad[:, :routed_units], 1).astype(f32)
    shared_sum = sum_cores(three_grad[:, routed_units:], 1)
    send = shared_sum.reshape(3, sub, trees, slice_rows).transpose(2, 0, 1, 3)
    got = swap_chips(send).transpose(1, 0, 2, 3).reshape(3, trees * sub, slice_rows).astype(f32)
    return (
        layer_output,
        input_grad,
        vectors[expert_count + 1],
        project_out,
        bias_out,
        output_out,
        vectors[expert_count + 2],
        vectors[:expert_count].T,
        vectors[expert_count],
        got[0].T,
        got[1].T,
        got[2],
        expert_sum[0].T[None],
        expert_sum[1].T[None],
        expert_sum[2][None],
    )


def spread(body, mesh, rows, columns):
    def named(*dims):
        names = {"expert": rows, "tensor": columns, "both": (*columns, *rows), None: None}
        return P(*(names[d] for d in dims))

    return jax.shard_map(
        body,
        mesh=mesh,
        in_specs=(
            named(None, "expert", None),
            named(None, "expert"),
            named(None, "expert", None),
            named(None, "expert", None),
            named(None, "expert", None),
            named("expert"),
            named("expert", None, "tensor"),
            named(None, "both"),
            named("tensor", "expert"),
            named("expert"),
            named("expert", None),
            named("expert"),
            named("expert", "tensor"),
            named("expert", "tensor"),
            named("tensor", "expert"),
            named("expert", None, "tensor"),
            named("expert", None, "tensor"),
            named("expert", "tensor", None),
            named(None, "expert", None),
        ),
        out_specs=(
            named(None, "expert", None),
            named(None, "expert", None),
            named("expert"),
            named("expert", None, "tensor"),
            named(None, "both"),
            named("tensor", "expert"),
            named("expert"),
            named("expert", None),
            named("expert"),
            named("expert", "tensor"),
            named("expert", "tensor"),
            named("tensor", "expert"),
            named("expert", None, "tensor"),
            named("expert", None, "tensor"),
            named("expert", "tensor", None),
        ),
        check_vma=False,
    )


def solution(mesh):
    expert_devices, tensor_devices = mesh.shape["expert"], mesh.shape["tensor"]

    def layer(*arrays):
        heads = arrays[6].shape[2] // HD
        trees = arrays[0].shape[1] // (SEG * arrays[2].shape[2])
        if (
            tensor_devices == 4
            and expert_devices % 2 == 0
            and heads == 2 * expert_devices
            and arrays[10].shape[1] == expert_devices
            and trees == expert_devices
            and arrays[0].shape[0] == 2
        ):
            grid = Mesh(mesh.devices.reshape(expert_devices // 2, 2, 2, 2), AXES)
            body = spread(chip_shards, grid, ("z", "x"), ("y", "c"))
        else:
            body = spread(gathered_shards, mesh, ("expert",), ("tensor",))
        return body(*arrays)

    return layer
```

```python
import jax
import jax.numpy as jnp
from jax import lax
from jax.experimental import pallas as pl
from jax.experimental.pallas import tpu as pltpu
from jax.sharding import Mesh, PartitionSpec as P

HD = 128
SEG = 32


EPSILON = 1e-06
ROPE_BASE = 1000000.0


def product(left_side, right_side):
    return jnp.dot(left_side, right_side, preferred_element_type=jnp.float32)


def product_left(left_side, right_side):
    return lax.dot_general(
        left_side, right_side, (((0,), (0,)), ((), ())), preferred_element_type=jnp.float32
    )


def product_right(left_side, right_side):
    return lax.dot_general(
        left_side, right_side, (((1,), (1,)), ((), ())), preferred_element_type=jnp.float32
    )


def silu_slope(inputs):
    sigmoid_value = jax.nn.sigmoid(inputs)
    return sigmoid_value * (1.0 + inputs * (1.0 - sigmoid_value))


def rope_tables(position_row, head_size):
    half_size = head_size // 2
    inverse = ROPE_BASE ** (-(jnp.arange(half_size, dtype=jnp.float32) * 2.0 / head_size))
    angles = position_row.astype(jnp.float32)[:, None] * inverse[None, :]
    cosine = jnp.cos(angles)
    sine_table = jnp.sin(angles)
    return (jnp.concatenate([cosine, cosine], 1), jnp.concatenate([sine_table, sine_table], 1))


def rotate(vectors, cosine, sine_table):
    half_size = vectors.shape[-1] // 2
    turned = jnp.concatenate([-vectors[..., half_size:], vectors[..., :half_size]], -1)
    return vectors * cosine[:, None, :] + turned * sine_table[:, None, :]


def unrotate(gradient, cosine, sine_table):
    half_size = gradient.shape[-1] // 2
    scaled = gradient * sine_table[:, None, :]
    turned = jnp.concatenate([scaled[..., half_size:], -scaled[..., :half_size]], -1)
    return gradient * cosine[:, None, :] + turned


def tree_mask(parent_row, seg_len):
    segment_count = parent_row.shape[0]
    segment_ids = jnp.arange(segment_count, dtype=jnp.int32)
    step_matrix = (
        (parent_row[:, None] == segment_ids[None, :]) & (segment_ids[:, None] > 0)
    ).astype(jnp.float32)
    identity = jnp.eye(segment_count, dtype=jnp.float32)

    def extend(loop_index, reached):
        return jnp.minimum(
            identity + jnp.dot(step_matrix, reached, precision=lax.Precision.HIGHEST), 1.0
        )

    reached = lax.fori_loop(0, segment_count, extend, identity)
    expanded = jnp.repeat(jnp.repeat(reached, seg_len, 0), seg_len, 1) > 0.5
    token_ids = jnp.arange(segment_count * seg_len, dtype=jnp.int32)
    return expanded & (token_ids[None, :] <= token_ids[:, None])


def gathered_shards(
    layer_input,
    positions,
    parents,
    routes,
    route_slots,
    norm1_gain,
    project_weight,
    project_bias,
    output_weight,
    norm2_gain,
    router_weight,
    shared_vector,
    shared_gate,
    shared_up,
    shared_down,
    expert_gate,
    expert_up,
    expert_down,
    cotangent,
):
    micro_count, seq_rows, model_width = layer_input.shape
    top_count = routes.shape[2]
    expert_count = router_weight.shape[1]
    capacity = seq_rows * top_count * 5 // (4 * expert_count)
    slot_total = expert_count * capacity
    gathered = (
        lax.all_gather(norm1_gain, "expert", axis=0, tiled=True),
        lax.all_gather(project_weight, "expert", axis=0, tiled=True),
        lax.all_gather(project_bias, "expert", axis=1, tiled=True),
        lax.all_gather(output_weight, "expert", axis=1, tiled=True),
        lax.all_gather(norm2_gain, "expert", axis=0, tiled=True),
        lax.all_gather(router_weight, "expert", axis=0, tiled=True),
        lax.all_gather(shared_vector, "expert", axis=0, tiled=True),
        lax.all_gather(shared_gate, "expert", axis=0, tiled=True),
        lax.all_gather(shared_up, "expert", axis=0, tiled=True),
        lax.all_gather(shared_down, "expert", axis=1, tiled=True),
    )
    (
        gain_first,
        project_in,
        bias_in,
        project_out,
        gain_second,
        router_full,
        vector_full,
        shared_gates,
        shared_ups,
        shared_downs,
    ) = gathered
    local_width = project_in.shape[2]
    head_count = local_width // HD
    shared_local = shared_gates.shape[1]
    project_flat = project_in.reshape(model_width, 3 * local_width)
    bias_flat = bias_in.astype(jnp.float32).reshape(3 * local_width)
    gain_one = gain_first.astype(jnp.float32)
    gain_two = gain_second.astype(jnp.float32)
    small_weights = jnp.concatenate([router_full, vector_full[:, None]], 1)
    expert_gates = expert_gate[0]
    expert_ups = expert_up[0]
    expert_downs = expert_down[0]
    score_scale = HD ** (-0.5)
    expert_ids = jnp.arange(expert_count, dtype=jnp.int32)
    pair_ids = jnp.arange(seq_rows * top_count, dtype=jnp.int32).reshape(seq_rows, top_count)
    zero_row = jnp.zeros((1, model_width), jnp.bfloat16)
    stored = []
    layer_outputs = []
    for batch_index in range(micro_count):
        input_rows = layer_input[batch_index].astype(jnp.float32)
        norm_one = lax.rsqrt(jnp.mean(input_rows * input_rows, -1, keepdims=True) + EPSILON)
        normed_one = (input_rows * norm_one * gain_one).astype(jnp.bfloat16)
        projected = (product(normed_one, project_flat) + bias_flat).reshape(
            seq_rows, 3, head_count, HD
        )
        cosine, sine_table = rope_tables(positions[batch_index], HD)
        queries = rotate(projected[:, 0], cosine, sine_table).astype(jnp.bfloat16)
        key_rows = rotate(projected[:, 1], cosine, sine_table).astype(jnp.bfloat16)
        values = projected[:, 2].astype(jnp.bfloat16)
        allowed = tree_mask(parents[batch_index, 0], SEG)
        scores = (
            jnp.einsum("qhd,khd->hqk", queries, key_rows, preferred_element_type=jnp.float32)
            * score_scale
        )
        masked = jnp.where(allowed[None], scores, -1e30)
        highest = jnp.max(masked, -1, keepdims=True)
        exponent = jnp.exp(masked - highest)
        row_total = jnp.sum(exponent, -1, keepdims=True)
        attention_probs = exponent / row_total
        log_total = highest + jnp.log(row_total)
        heads_out = (
            jnp.einsum(
                "hqk,khd->qhd",
                attention_probs.astype(jnp.bfloat16),
                values,
                preferred_element_type=jnp.float32,
            )
            .astype(jnp.bfloat16)
            .reshape(seq_rows, local_width)
        )
        attention = lax.psum(product(heads_out, project_out), "tensor")
        hidden_state = input_rows + attention
        norm_two = lax.rsqrt(jnp.mean(hidden_state * hidden_state, -1, keepdims=True) + EPSILON)
        normed_two = (hidden_state * norm_two * gain_two).astype(jnp.bfloat16)
        small_logits = product(normed_two, small_weights)
        router_prob = jax.nn.softmax(small_logits[:, :expert_count], axis=-1)
        onehot = (routes[batch_index][..., None] == expert_ids).astype(jnp.float32)
        picked = jnp.sum(onehot * router_prob[:, None, :], -1)
        picked_sum = jnp.sum(picked, -1, keepdims=True)
        route_gates = picked / picked_sum
        shared_scale = jax.nn.sigmoid(small_logits[:, expert_count])
        gate_shared = product(normed_two, shared_gates)
        up_shared = product(normed_two, shared_ups)
        hidden_shared = (jax.nn.silu(gate_shared) * up_shared).astype(jnp.bfloat16)
        shared_part = product(hidden_shared, shared_downs)
        slot_rows = route_slots[batch_index]
        valid = slot_rows < capacity
        keep_mask = valid.astype(jnp.float32)
        slot_index = routes[batch_index] * capacity + jnp.minimum(slot_rows, capacity - 1)
        safe_index = jnp.where(valid, slot_index, 0)
        target = jnp.where(valid, slot_index, slot_total).reshape(-1)
        slot_table = (
            jnp.full((slot_total,), seq_rows * top_count, jnp.int32)
            .at[target]
            .set(pair_ids.reshape(-1), mode="drop")
        )
        padded = jnp.concatenate([normed_two, zero_row], 0)
        outgoing = padded[slot_table // top_count].reshape(expert_count, capacity, model_width)
        received = lax.all_to_all(outgoing, "expert", split_axis=0, concat_axis=0, tiled=True)
        run_owner_rows = received.reshape(-1, model_width)
        run_gate_expert = product(run_owner_rows, expert_gates)
        run_up_expert = product(run_owner_rows, expert_ups)
        run_hidden_expert = (jax.nn.silu(run_gate_expert) * run_up_expert).astype(jnp.bfloat16)
        expert_rows = product(run_hidden_expert, expert_downs).reshape(
            received.shape[0], received.shape[1], model_width
        )
        returned = lax.all_to_all(expert_rows, "expert", split_axis=0, concat_axis=0, tiled=True)
        returned, received = (returned, received)
        pair_out = returned.reshape(slot_total, -1)[safe_index] * keep_mask[..., None]
        routed = jnp.sum(route_gates[..., None] * pair_out, 1)
        shared_out, routed_full = lax.psum((shared_part, routed), "tensor")
        layer_outputs.append(
            (hidden_state + shared_scale[:, None] * shared_out + routed_full).astype(jnp.bfloat16)
        )
        stored.append(
            (
                input_rows,
                norm_one,
                normed_one,
                cosine,
                sine_table,
                queries,
                key_rows,
                values,
                allowed,
                log_total,
                heads_out,
                hidden_state,
                norm_two,
                normed_two,
                router_prob,
                onehot,
                picked_sum,
                route_gates,
                shared_scale,
                gate_shared,
                up_shared,
                hidden_shared,
                shared_out,
                pair_out,
                safe_index,
                keep_mask,
                slot_table,
                received,
            )
        )
    grad_gain_one = jnp.zeros((model_width,), jnp.float32)
    grad_gain_two = jnp.zeros((model_width,), jnp.float32)
    grad_project = jnp.zeros((model_width, 3 * local_width), jnp.float32)
    grad_bias = jnp.zeros((3 * local_width,), jnp.float32)
    grad_output = jnp.zeros((local_width, model_width), jnp.float32)
    grad_small = jnp.zeros((model_width, expert_count + 1), jnp.float32)
    grad_shared_gate = jnp.zeros((model_width, shared_local), jnp.float32)
    grad_shared_up = jnp.zeros((model_width, shared_local), jnp.float32)
    grad_shared_down = jnp.zeros((shared_local, model_width), jnp.float32)
    grad_expert_gate = jnp.zeros(expert_gates.shape, jnp.float32)
    grad_expert_up = jnp.zeros(expert_ups.shape, jnp.float32)
    grad_expert_down = jnp.zeros(expert_downs.shape, jnp.float32)
    input_grads = [None] * micro_count
    for batch_index in reversed(range(micro_count)):
        (
            input_rows,
            norm_one,
            normed_one,
            cosine,
            sine_table,
            queries,
            key_rows,
            values,
            allowed,
            log_total,
            heads_out,
            hidden_state,
            norm_two,
            normed_two,
            router_prob,
            onehot,
            picked_sum,
            route_gates,
            shared_scale,
            gate_shared,
            up_shared,
            hidden_shared,
            shared_out,
            pair_out,
            safe_index,
            keep_mask,
            slot_table,
            received,
        ) = stored[batch_index]
        upstream = cotangent[batch_index].astype(jnp.float32)
        shared_grad = (shared_scale[:, None] * upstream).astype(jnp.bfloat16)
        scale_grad = jnp.sum(upstream * shared_out, -1) * shared_scale * (1.0 - shared_scale)
        gate_part = jnp.sum(upstream[:, None, :] * pair_out, -1)
        pair_grad = (
            (route_gates[..., None] * upstream[:, None, :])
            .astype(jnp.bfloat16)
            .reshape(seq_rows * top_count, model_width)
        )
        outgoing_grad = jnp.concatenate([pair_grad, zero_row], 0)[slot_table].reshape(
            expert_count, capacity, model_width
        )
        arrived = lax.all_to_all(outgoing_grad, "expert", split_axis=0, concat_axis=0, tiled=True)
        owner_rows = received.reshape(-1, model_width)
        owner_grads = arrived.reshape(-1, model_width)
        gate_expert = product(owner_rows, expert_gates)
        up_expert = product(owner_rows, expert_ups)
        active_expert = jax.nn.silu(gate_expert)
        hidden_expert = (active_expert * up_expert).astype(jnp.bfloat16)
        hidden_expert_grad = product_right(owner_grads, expert_downs)
        grad_expert_down = grad_expert_down + product_left(hidden_expert, owner_grads)
        gate_expert_grad = (hidden_expert_grad * up_expert * silu_slope(gate_expert)).astype(
            jnp.bfloat16
        )
        up_expert_grad = (hidden_expert_grad * active_expert).astype(jnp.bfloat16)
        grad_expert_gate = grad_expert_gate + product_left(owner_rows, gate_expert_grad)
        grad_expert_up = grad_expert_up + product_left(owner_rows, up_expert_grad)
        row_grad = product_right(gate_expert_grad, expert_gates) + product_right(
            up_expert_grad, expert_ups
        )
        row_back = lax.all_to_all(
            row_grad.reshape(expert_count, capacity, model_width),
            "expert",
            split_axis=0,
            concat_axis=0,
            tiled=True,
        )
        routed_back = jnp.sum(
            row_back.reshape(slot_total, model_width)[safe_index] * keep_mask[..., None], 1
        )
        hidden_shared_grad = product_right(shared_grad, shared_downs)
        grad_shared_down = grad_shared_down + product_left(hidden_shared, shared_grad)
        gate_shared_grad = (hidden_shared_grad * up_shared * silu_slope(gate_shared)).astype(
            jnp.bfloat16
        )
        up_shared_grad = (hidden_shared_grad * jax.nn.silu(gate_shared)).astype(jnp.bfloat16)
        grad_shared_gate = grad_shared_gate + product_left(normed_two, gate_shared_grad)
        grad_shared_up = grad_shared_up + product_left(normed_two, up_shared_grad)
        normed_part = (
            product_right(gate_shared_grad, shared_gates)
            + product_right(up_shared_grad, shared_ups)
            + routed_back
        )
        normed_sum, gate_grad = lax.psum((normed_part, gate_part), "tensor")
        picked_grad = (gate_grad - jnp.sum(gate_grad * route_gates, -1, keepdims=True)) / picked_sum
        prob_grad = jnp.sum(picked_grad[..., None] * onehot, 1)
        logit_grad = router_prob * (prob_grad - jnp.sum(router_prob * prob_grad, -1, keepdims=True))
        small_grad = jnp.concatenate([logit_grad, scale_grad[:, None]], 1).astype(jnp.bfloat16)
        grad_small = grad_small + product_left(normed_two, small_grad)
        normed_two_grad = normed_sum + product_right(small_grad, small_weights)
        grad_gain_two = grad_gain_two + jnp.sum(normed_two_grad * hidden_state * norm_two, 0)
        scaled_two = normed_two_grad * gain_two
        hidden_grad = (
            upstream
            + norm_two * scaled_two
            - hidden_state * norm_two**3 * jnp.mean(scaled_two * hidden_state, -1, keepdims=True)
        )
        attention_grad = hidden_grad.astype(jnp.bfloat16)
        grad_output = grad_output + product_left(heads_out, attention_grad)
        heads_grad = (
            product_right(attention_grad, project_out)
            .astype(jnp.bfloat16)
            .reshape(seq_rows, head_count, HD)
        )
        scores = (
            jnp.einsum("qhd,khd->hqk", queries, key_rows, preferred_element_type=jnp.float32)
            * score_scale
        )
        masked = jnp.where(allowed[None], scores, -1e30)
        attention_probs = jnp.exp(masked - log_total)
        value_grad = jnp.einsum(
            "hqk,qhd->khd",
            attention_probs.astype(jnp.bfloat16),
            heads_grad,
            preferred_element_type=jnp.float32,
        )
        prob_grads = jnp.einsum(
            "qhd,khd->hqk", heads_grad, values, preferred_element_type=jnp.float32
        )
        score_grad = (
            attention_probs
            * (prob_grads - jnp.sum(attention_probs * prob_grads, -1, keepdims=True))
        ).astype(jnp.bfloat16)
        query_grad = (
            jnp.einsum("hqk,khd->qhd", score_grad, key_rows, preferred_element_type=jnp.float32)
            * score_scale
        )
        key_grad = (
            jnp.einsum("hqk,qhd->khd", score_grad, queries, preferred_element_type=jnp.float32)
            * score_scale
        )
        projected_grad = (
            jnp.stack(
                [
                    unrotate(query_grad, cosine, sine_table),
                    unrotate(key_grad, cosine, sine_table),
                    value_grad,
                ],
                1,
            )
            .astype(jnp.bfloat16)
            .reshape(seq_rows, 3 * local_width)
        )
        grad_bias = grad_bias + jnp.sum(projected_grad.astype(jnp.float32), 0)
        grad_project = grad_project + product_left(normed_one, projected_grad)
        normed_one_grad = lax.psum(
            product_right(projected_grad, project_flat).astype(jnp.bfloat16), "tensor"
        ).astype(jnp.float32)
        grad_gain_one = grad_gain_one + jnp.sum(normed_one_grad * input_rows * norm_one, 0)
        scaled_one = normed_one_grad * gain_one
        input_grads[batch_index] = (
            hidden_grad
            + norm_one * scaled_one
            - input_rows * norm_one**3 * jnp.mean(scaled_one * input_rows, -1, keepdims=True)
        )
    reduced = (
        lax.psum_scatter(
            grad_gain_one.astype(jnp.bfloat16), "expert", scatter_dimension=0, tiled=True
        ).astype(jnp.float32),
        lax.psum_scatter(
            grad_project.reshape(model_width, 3, local_width).astype(jnp.bfloat16),
            "expert",
            scatter_dimension=0,
            tiled=True,
        ).astype(jnp.float32),
        lax.psum_scatter(
            grad_bias.reshape(3, local_width).astype(jnp.bfloat16),
            "expert",
            scatter_dimension=1,
            tiled=True,
        ).astype(jnp.float32),
        lax.psum_scatter(
            grad_output.astype(jnp.bfloat16), "expert", scatter_dimension=1, tiled=True
        ).astype(jnp.float32),
        lax.psum_scatter(
            grad_gain_two.astype(jnp.bfloat16), "expert", scatter_dimension=0, tiled=True
        ).astype(jnp.float32),
        lax.psum_scatter(
            grad_small[:, :expert_count].astype(jnp.bfloat16),
            "expert",
            scatter_dimension=0,
            tiled=True,
        ).astype(jnp.float32),
        lax.psum_scatter(
            grad_small[:, expert_count].astype(jnp.bfloat16),
            "expert",
            scatter_dimension=0,
            tiled=True,
        ).astype(jnp.float32),
        lax.psum_scatter(
            grad_shared_gate.astype(jnp.bfloat16), "expert", scatter_dimension=0, tiled=True
        ).astype(jnp.float32),
        lax.psum_scatter(
            grad_shared_up.astype(jnp.bfloat16), "expert", scatter_dimension=0, tiled=True
        ).astype(jnp.float32),
        lax.psum_scatter(
            grad_shared_down.astype(jnp.bfloat16), "expert", scatter_dimension=1, tiled=True
        ).astype(jnp.float32),
    )
    return (
        jnp.stack(layer_outputs),
        jnp.stack(input_grads),
        reduced[0],
        reduced[1],
        reduced[2],
        reduced[3],
        reduced[4],
        reduced[5],
        reduced[6],
        reduced[7],
        reduced[8],
        reduced[9],
        grad_expert_gate[None],
        grad_expert_up[None],
        grad_expert_down[None],
    )


AXES = ("z", "x", "y", "c")


MESH_ID = pl.DeviceIdType.MESH
VMEM_LIMIT = 60 * 1024 * 1024


def positions_here():
    return tuple(lax.axis_index(a) for a in AXES)


def planes_from(z):
    return (z, z + 1 - 2 * (z % 2), 2 - z // 2, 3 * (1 - z // 2))


def greet(barrier, partners):
    for partner in partners:
        pl.semaphore_signal(barrier, inc=1, device_id=partner, device_id_type=MESH_ID)
    pl.semaphore_wait(barrier, len(partners))


def near_partners(z, x, y):
    planes = planes_from(z)
    return [{"x": 1 - x}, {"y": 1 - y}] + [{"z": p} for p in planes[1:]]


class Sends:
    def __init__(self):
        self.open = []

    def start(self, source, target, send, receive, where):
        copy = pltpu.make_async_remote_copy(
            src_ref=source, dst_ref=target, send_sem=send, recv_sem=receive, device_id=where, device_id_type=MESH_ID
        )
        copy.start()
        self.open.append(copy)

    def finish(self):
        for copy in self.open:
            copy.wait_send()
        self.open = []


def arrive(buffer, receive):
    pltpu.make_async_copy(buffer, buffer, receive).wait()


class Gather:
    def __init__(self, held, send, receive, cut, sends):
        self.held, self.send, self.receive, self.sends = held, send, receive, sends
        width = held.shape[-1]
        self.left, self.right = pl.ds(0, cut), pl.ds(cut, width - cut)
        self.z, self.x, self.y, _ = positions_here()
        self.planes = planes_from(self.z)

    def block(self, plane, x, y, columns=None):
        if columns is None:
            return self.held.at[plane, x, y]
        return self.held.at[plane, x, y, :, columns]

    def pass_on(self, plane, x, y, columns, slot, axis):
        here = self.x if axis == "x" else self.y
        ref = self.block(plane, x, y, columns)
        self.sends.start(ref, ref, self.send.at[slot, plane], self.receive.at[slot, plane], {axis: 1 - here})

    def begin(self):
        own = self.block(self.z, self.x, self.y)
        for step, plane in enumerate(self.planes[1:]):
            self.sends.start(own, own, self.send.at[6, step], self.receive.at[6, self.z], {"z": plane})

    def first(self, step):
        plane, x, y = self.planes[step], self.x, self.y
        if step:
            arrive(self.block(plane, x, y), self.receive.at[6, plane])
        self.pass_on(plane, x, y, self.left, 0, "x")
        self.pass_on(plane, x, y, self.right, 1, "y")
        self.pass_on(plane, x, y, self.left, 2, "y")
        self.pass_on(plane, x, y, self.right, 3, "x")

    def second(self, step):
        plane, x, y = self.planes[step], self.x, self.y
        arrive(self.block(plane, 1 - x, y, self.left), self.receive.at[0, plane])
        self.pass_on(plane, 1 - x, y, self.left, 4, "y")
        arrive(self.block(plane, x, 1 - y, self.right), self.receive.at[1, plane])
        self.pass_on(plane, x, 1 - y, self.right, 5, "x")

    def whole(self, step):
        plane, x, y = self.planes[step], self.x, self.y
        arrive(self.block(plane, x, 1 - y, self.left), self.receive.at[2, plane])
        arrive(self.block(plane, 1 - x, y, self.right), self.receive.at[3, plane])
        arrive(self.block(plane, 1 - x, 1 - y, self.left), self.receive.at[4, plane])
        arrive(self.block(plane, 1 - x, 1 - y, self.right), self.receive.at[5, plane])

    @staticmethod
    def semaphores():
        return [pltpu.SemaphoreType.DMA((7, 4)), pltpu.SemaphoreType.DMA((7, 4))]


class Reduce:
    def __init__(self, parts, buffers, cut, sends):
        self.parts, self.sends = parts, sends
        self.one_left, self.one_right, self.two_left, self.two_right, self.last, self.send, self.receive = buffers
        width = parts.shape[-1]
        self.left, self.right = pl.ds(0, cut), pl.ds(cut, width - cut)
        self.z, self.x, self.y, _ = positions_here()
        self.planes = planes_from(self.z)

    @staticmethod
    def buffers(rows, width, cut):
        bf16 = jnp.bfloat16
        return [
            pltpu.VMEM((4, 2, rows, cut), bf16),
            pltpu.VMEM((4, 2, rows, width - cut), bf16),
            pltpu.VMEM((4, rows, cut), bf16),
            pltpu.VMEM((4, rows, width - cut), bf16),
            pltpu.VMEM((4, rows, width), bf16),
            pltpu.SemaphoreType.DMA((5, 4)),
            pltpu.SemaphoreType.DMA((5, 4)),
        ]

    def first(self, step):
        plane = self.planes[step]
        self.sends.start(
            self.parts.at[plane, :, 1 - self.y, :, self.left], self.one_left.at[plane],
            self.send.at[0, plane], self.receive.at[0, plane], {"y": 1 - self.y},
        )
        self.sends.start(
            self.parts.at[plane, 1 - self.x, :, :, self.right], self.one_right.at[plane],
            self.send.at[1, plane], self.receive.at[1, plane], {"x": 1 - self.x},
        )

    def add(self, ref, other):
        ref[...] = (ref[...].astype(jnp.float32) + other[...].astype(jnp.float32)).astype(ref.dtype)

    def second(self, step):
        plane, x, y = self.planes[step], self.x, self.y
        arrive(self.one_left.at[plane], self.receive.at[0, plane])
        away = self.parts.at[plane, 1 - x, y, :, self.left]
        self.add(away, self.one_left.at[plane, 1 - x])
        self.sends.start(away, self.two_left.at[plane], self.send.at[2, plane], self.receive.at[2, plane], {"x": 1 - x})
        arrive(self.one_right.at[plane], self.receive.at[1, plane])
        away = self.parts.at[plane, x, 1 - y, :, self.right]
        self.add(away, self.one_right.at[plane, 1 - y])
        self.sends.start(away, self.two_right.at[plane], self.send.at[3, plane], self.receive.at[3, plane], {"y": 1 - y})
        self.add(self.parts.at[plane, x, y, :, self.left], self.one_left.at[plane, x])
        self.add(self.parts.at[plane, x, y, :, self.right], self.one_right.at[plane, y])

    def third(self, step):
        plane, x, y = self.planes[step], self.x, self.y
        here = self.parts.at[plane, x, y]
        arrive(self.two_left.at[plane], self.receive.at[2, plane])
        arrive(self.two_right.at[plane], self.receive.at[3, plane])
        self.add(here.at[:, self.left], self.two_left.at[plane])
        self.add(here.at[:, self.right], self.two_right.at[plane])
        if step:
            self.sends.start(here, self.last.at[self.z], self.send.at[4, plane], self.receive.at[4, self.z], {"z": plane})

    def total(self):
        here = self.parts[self.z, self.x, self.y].astype(jnp.float32)
        for plane in self.planes[1:]:
            arrive(self.last.at[plane], self.receive.at[4, plane])
            here = here + self.last[plane].astype(jnp.float32)
        return here


def gather_call(own, collective):
    rows, width = own.shape

    def kernel(own_ref, out_ref, send, receive):
        z, x, y, _ = positions_here()
        greet(pltpu.get_barrier_semaphore(), near_partners(z, x, y))
        out_ref[z, x, y] = own_ref[...]
        sends = Sends()
        gather = Gather(out_ref, send, receive, width // 2, sends)
        gather.first(0)
        gather.begin()
        gather.second(0)
        for step in range(1, 4):
            gather.first(step)
            gather.second(step)
        for step in range(4):
            gather.whole(step)
        sends.finish()

    vmem = pl.BlockSpec(memory_space=pltpu.VMEM)
    return pl.pallas_call(
        kernel,
        name=f"gather_{collective}",
        out_shape=jax.ShapeDtypeStruct((4, 2, 2, rows, width), own.dtype),
        in_specs=[vmem],
        out_specs=vmem,
        scratch_shapes=Gather.semaphores(),
        compiler_params=pltpu.CompilerParams(
            collective_id=collective, has_side_effects=True, vmem_limit_bytes=VMEM_LIMIT
        ),
    )(own)


def reduce_call(parts, collective):
    rows, width = parts.shape[-2:]

    def kernel(parts_ref, out_ref, held, *buffers):
        z, x, y, _ = positions_here()
        held[...] = parts_ref[...]
        greet(pltpu.get_barrier_semaphore(), near_partners(z, x, y))
        sends = Sends()
        add = Reduce(held, buffers, width // 2, sends)
        for step in (3, 2, 1, 0):
            add.first(step)
        add.second(3)
        add.second(2)
        add.third(3)
        add.second(1)
        add.third(2)
        add.second(0)
        add.third(1)
        add.third(0)
        out_ref[...] = add.total()
        sends.finish()

    vmem = pl.BlockSpec(memory_space=pltpu.VMEM)
    return pl.pallas_call(
        kernel,
        name=f"reduce_{collective}",
        out_shape=jax.ShapeDtypeStruct((rows, width), jnp.float32),
        in_specs=[vmem],
        out_specs=vmem,
        scratch_shapes=[pltpu.VMEM(parts.shape, parts.dtype), *Reduce.buffers(rows, width, width // 2)],
        compiler_params=pltpu.CompilerParams(
            collective_id=collective, has_side_effects=True, vmem_limit_bytes=VMEM_LIMIT
        ),
    )(parts)


EXTRA = 128


def dot_nn(a, b):
    return lax.dot_general(a, b, (((1,), (0,)), ((), ())), preferred_element_type=jnp.float32)


def dot_nt(a, b):
    return lax.dot_general(a, b, (((1,), (1,)), ((), ())), preferred_element_type=jnp.float32)


def dot_tn(a, b):
    return lax.dot_general(a, b, (((0,), (0,)), ((), ())), preferred_element_type=jnp.float32)


def chips_but(z, x, y):
    found = []
    for dz in range(4):
        for dx in range(2):
            for dy in range(2):
                if dz or dx or dy:
                    found.append({"z": lax.rem(z + dz, 4), "x": (x + dx) % 2, "y": (y + dy) % 2})
    return found


def experts_call(own, cotangents, three, routed_units):
    bf16, f32 = jnp.bfloat16, jnp.float32
    rows, wide = own.shape
    width = wide - EXTRA
    units = three.shape[1]
    shared_units = units - routed_units
    tile = routed_units // 2
    assert shared_units == tile
    chunk = 4 * rows
    tokens = 4 * chunk
    cut = width // 2
    column = 1024
    half_tile = tile // 2
    keep = tile + half_tile

    def kernel(own_ref, cot_ref, three_ref, sum_ref, out_ref, dot_ref, expert_ref, shared_ref, held, weights, hidden, gate_grad, up_grad,
               part_n, part_o, dots_mine, staged, *rest):
        (g_send, g_recv, w_sem, d_send, d_recv, free, x_send, x_recv, s_sem) = rest[:9]
        n_bufs, o_bufs = rest[9:16], rest[16:23]
        z, x, y, c = positions_here()
        here = z * 2 + x
        loads = [pltpu.make_async_copy(three_ref.at[i], weights.at[i], w_sem.at[i]) for i in range(3)]
        for load in loads:
            load.start()
        others = chips_but(z, x, y)
        greet(pltpu.get_barrier_semaphore(), others + [{"c": 1 - c}])
        held[z, x, y] = own_ref[...]
        sends = Sends()
        gather = Gather(held, g_send, g_recv, cut, sends)
        sum_n = Reduce(part_n, n_bufs, cut, sends)
        sum_o = Reduce(part_o, o_bufs, cut, sends)
        lanes = lax.broadcasted_iota(jnp.int32, (16, EXTRA), 1)
        rows_of = lax.broadcasted_iota(jnp.int32, (16, EXTRA), 0)
        pick = ((rows_of == 0) & ((lanes == here) | (lanes == here + 8))) | ((rows_of == 1) & ((lanes == 16) | (lanes == 17)))
        pick = pick.astype(f32).astype(bf16)

        def units_of(step):
            plane = gather.planes[step]
            place = pl.ds(pl.multiple_of(plane * chunk, chunk), chunk)
            rows_n = held[plane, :, :, :, 0:width].reshape(chunk, width)
            rows_c = cot_ref[plane].reshape(chunk, width)
            scales = dot_nt(pick, held[plane, :, :, :, width:wide].reshape(chunk, EXTRA))

            def one(i, _):
                span = pl.ds(pl.multiple_of(i * tile, 32), tile)
                scale = jnp.where(i == 2, scales[1:2], scales[0:1])
                gate = dot_nt(weights[0, span, :], rows_n)
                up = dot_nt(weights[1, span, :], rows_n)
                down = dot_nt(weights[2, span, :], rows_c)
                sig = 1.0 / (1.0 + jnp.exp(-gate))
                active = gate * sig
                hid = active * up
                dot = jnp.sum(hid * down, 0, keepdims=True)
                hidden[span, place] = (hid * scale).astype(bf16)
                grad = down * scale
                gate_grad[span, place] = (grad * up * (sig + active * (1.0 - sig))).astype(bf16)
                up_grad[span, place] = (grad * active).astype(bf16)
                routed, shared = lax.cond(i == 2, lambda: (jnp.zeros_like(dot), dot), lambda: (dot, jnp.zeros_like(dot)))
                return (_[0] + routed, _[1] + shared)

            zero = jnp.zeros((1, chunk), f32)
            routed, shared = lax.fori_loop(0, 3, one, (zero, zero))
            row = lax.broadcasted_iota(jnp.int32, (8, chunk), 0)
            both = jnp.where(row == 0, routed, jnp.where(row == 1, shared, 0.0))
            for t in range(2):
                dots_mine[plane, t] = both[:, t * 2 * rows : (t + 1) * 2 * rows]

        def back_of(step):
            plane = gather.planes[step]
            place = pl.ds(pl.multiple_of(plane * chunk, chunk), chunk)

            def one(i, _):
                span = pl.ds(pl.multiple_of(i * column, column), column)
                value = dot_tn(gate_grad[:, place], weights[0, :, span]) + dot_tn(up_grad[:, place], weights[1, :, span])
                part_n[plane, :, :, :, span] = value.astype(bf16).reshape(2, 2, rows, column)
                return 0

            lax.fori_loop(0, width // column, one, 0)

        def out_of(step):
            plane = gather.planes[step]
            place = pl.ds(pl.multiple_of(plane * chunk, chunk), chunk)

            def one(i, _):
                span = pl.ds(pl.multiple_of(i * column, column), column)
                value = dot_tn(hidden[:, place], weights[2, :, span])
                part_o[plane, :, :, :, span] = value.astype(bf16).reshape(2, 2, rows, column)
                return 0

            lax.fori_loop(0, width // column, one, 0)

        gather.first(0)
        gather.begin()
        gather.second(0)
        gather.first(1)
        for load in loads:
            load.wait()
        for step in range(4):
            gather.whole(step)
            units_of(step)
            if step < 3:
                gather.second(step + 1)
            if step < 2:
                gather.first(step + 2)
            back_of(step)
            sum_n.first(step)
            if step:
                sum_n.second(step - 1)
            out_of(step)
            if step > 1:
                sum_n.third(step - 2)
            sum_o.first(step)
            if step:
                sum_o.second(step - 1)
        for i, other in enumerate(others):
            sends.start(dots_mine.at[other["z"], other["x"]], dot_ref.at[z, x, y], d_send.at[i], d_recv.at[z, x, y], other)
        dot_ref[z, x, y] = dots_mine[z, x]
        pl.semaphore_signal(free, inc=1, device_id={"c": 1 - c}, device_id_type=MESH_ID)

        def gradient(kind, first, count, span):
            if kind < 2:
                side = (gate_grad, up_grad)[kind]
                return dot_nn(side[pl.ds(first, count), :], held[:, :, :, :, span].reshape(tokens, column))
            return dot_nn(hidden[pl.ds(first, count), :], cot_ref[:, :, :, :, span].reshape(tokens, column))

        def away(core, kind):
            def one(i, _):
                span = pl.ds(pl.multiple_of(i * column, column), column)
                first = pl.multiple_of(core * tile, 32)
                weights[kind, 0:tile, span] = gradient(kind, first, tile, span).astype(bf16)
                first = pl.multiple_of(routed_units + core * half_tile, 16)
                weights[kind, tile:keep, span] = gradient(kind, first, half_tile, span).astype(bf16)
                return 0

            lax.fori_loop(0, width // column, one, 0)

        away(1 - c, 0)
        sum_n.second(3)
        sum_n.third(2)
        sum_o.third(1)
        pl.semaphore_wait(free, 1)
        for kind in range(3):
            if kind:
                away(1 - c, kind)
            sends.start(weights.at[kind, 0:keep], weights.at[kind, keep : 2 * keep], x_send.at[kind], x_recv.at[kind], {"c": 1 - c})
            if kind == 0:
                sum_n.third(3)
                sum_o.second(3)
                sum_o.third(2)
            if kind == 1:
                sum_o.third(3)
        sum_o.third(0)
        writes = []
        for kind in range(3):
            arrive(weights.at[kind, keep : 2 * keep], x_recv.at[kind])
            if kind > 1:
                writes[kind - 2].wait()

            def one(i, _):
                span = pl.ds(pl.multiple_of(i * column, column), column)
                first = pl.multiple_of(c * tile, 32)
                value = gradient(kind, first, tile, span)
                staged[kind % 2, :, span] = value + weights[kind, keep : keep + tile, span].astype(f32)
                first = pl.multiple_of(routed_units + c * half_tile, 16)
                value = gradient(kind, first, half_tile, span)
                shared_ref[kind, :, span] = (value + weights[kind, keep + tile : 2 * keep, span].astype(f32)).astype(bf16)
                return 0

            lax.fori_loop(0, width // column, one, 0)
            write = pltpu.make_async_copy(staged.at[kind % 2], expert_ref.at[kind], s_sem.at[kind])
            write.start()
            writes.append(write)
        sum_ref[...] = sum_n.total()
        out_ref[...] = sum_o.total()
        for other in others:
            arrive(dot_ref.at[other["z"], other["x"], other["y"]], d_recv.at[other["z"], other["x"], other["y"]])
        writes[1].wait()
        writes[2].wait()
        sends.finish()

    vmem = pl.BlockSpec(memory_space=pltpu.VMEM)
    anywhere = pl.BlockSpec(memory_space=pl.ANY)
    dma = pltpu.SemaphoreType.DMA
    flops = 2 * tokens * width * units * 9
    return pl.pallas_call(
        kernel,
        name="experts",
        out_shape=(
            jax.ShapeDtypeStruct((rows, width), f32),
            jax.ShapeDtypeStruct((rows, width), f32),
            jax.ShapeDtypeStruct((4, 2, 2, 8, 2 * rows), f32),
            jax.ShapeDtypeStruct((3, tile, width), f32),
            jax.ShapeDtypeStruct((3, half_tile, width), bf16),
        ),
        in_specs=[vmem, vmem, anywhere],
        out_specs=(vmem, vmem, vmem, anywhere, vmem),
        scratch_shapes=[
            pltpu.VMEM((4, 2, 2, rows, wide), bf16),
            pltpu.VMEM((3, units, width), bf16),
            pltpu.VMEM((units, tokens), bf16),
            pltpu.VMEM((units, tokens), bf16),
            pltpu.VMEM((units, tokens), bf16),
            pltpu.VMEM((4, 2, 2, rows, width), bf16),
            pltpu.VMEM((4, 2, 2, rows, width), bf16),
            pltpu.VMEM((4, 2, 8, 2 * rows), f32),
            pltpu.VMEM((2, tile, width), f32),
            *Gather.semaphores(),
            dma((3,)),
            dma((15,)),
            dma((4, 2, 2)),
            pltpu.SemaphoreType.REGULAR,
            dma((3,)),
            dma((3,)),
            dma((3,)),
            *Reduce.buffers(rows, width, cut),
            *Reduce.buffers(rows, width, cut),
        ],
        compiler_params=pltpu.CompilerParams(collective_id=2, has_side_effects=True, vmem_limit_bytes=VMEM_LIMIT),
        cost_estimate=pl.CostEstimate(flops=flops, bytes_accessed=40 * 1024 * 1024, transcendentals=tokens * units),
    )(own, cotangents, three)


def tree_masks(parent_rows, seg_len):
    tree_count, segment_count = parent_rows.shape
    segment_ids = jnp.arange(segment_count, dtype=jnp.int32)
    step_matrix = (
        (parent_rows[:, :, None] == segment_ids) & (segment_ids[:, None] > 0)
    )
    reached = jnp.broadcast_to(jnp.eye(segment_count, dtype=bool), step_matrix.shape)
    for _ in range(segment_count):
        reached = jnp.eye(segment_count, dtype=bool) | jnp.any(
            step_matrix[:, :, :, None] & reached[:, None, :, :], 2
        )
    expanded = jnp.repeat(jnp.repeat(reached, seg_len, 1), seg_len, 2)
    token_ids = jnp.arange(segment_count * seg_len, dtype=jnp.int32)
    return expanded & (token_ids[None, :] <= token_ids[:, None])


def turn(rows):
    half = rows.shape[-1] // 2
    return jnp.concatenate([-rows[..., half:], rows[..., :half]], -1)


def turn_back(rows):
    half = rows.shape[-1] // 2
    return jnp.concatenate([rows[..., half:], -rows[..., :half]], -1)


def chip_shards(
    layer_input,
    positions,
    parents,
    routes,
    route_slots,
    norm1_gain,
    project_weight,
    project_bias,
    output_weight,
    norm2_gain,
    router_weight,
    shared_vector,
    shared_gate,
    shared_up,
    shared_down,
    expert_gate,
    expert_up,
    expert_down,
    cotangent,
):
    f32, bf16 = jnp.float32, jnp.bfloat16
    micro_count, seq_rows, model_width = layer_input.shape
    top_count = routes.shape[2]
    expert_count = router_weight.shape[1]
    capacity = seq_rows * top_count * 5 // (4 * expert_count)
    z, x, y, c = [lax.axis_index(a) for a in AXES]
    here = z * 2 + x
    trees = expert_count
    tokens = trees * seq_rows
    blocks = (trees // 2, 2, 2, seq_rows // 2, model_width)
    own_rows = seq_rows // 2
    slice_rows = norm1_gain.shape[0]
    score_scale = HD ** (-0.5)

    def own(array):
        return lax.dynamic_slice(
            array, (c, y * own_rows, 0), (1, own_rows, model_width)
        )[0]

    own_input = own(layer_input)
    own_cotangent = own(cotangent)

    def mine(array):
        return lax.dynamic_index_in_dim(array, c, 0, keepdims=False).astype(bf16).reshape(-1)

    pieces = [
        norm1_gain,
        norm2_gain,
        shared_vector,
        router_weight.T.reshape(-1),
        project_bias.reshape(-1),
        mine(positions),
        mine(parents),
    ]
    sizes = [p.shape[0] for p in pieces]
    small = lax.all_gather(jnp.concatenate(pieces), AXES, axis=0, tiled=False)
    small = small.reshape(trees, 2, 2, -1)
    starts = [sum(sizes[:i]) for i in range(len(sizes))]

    def part(i):
        return small[..., starts[i] : starts[i] + sizes[i]]

    gain_one = part(0)[:, 0, 0].reshape(-1).astype(f32)
    gain_two = part(1)[:, 0, 0].reshape(-1).astype(f32)
    vector_full = part(2)[:, 0, 0].reshape(-1)
    router_full = (
        part(3)[:, 0, 0]
        .reshape(trees, expert_count, slice_rows)
        .transpose(1, 0, 2)
        .reshape(expert_count, model_width)
    )
    small_weights = jnp.concatenate([router_full, vector_full[None]], 0)
    bias_full = part(4).reshape(trees, 4, 3, -1).transpose(2, 1, 0, 3).reshape(3, -1)
    head = y * trees + here
    bias_head = lax.dynamic_slice(bias_full, (0, head * HD), (3, HD)).astype(f32)

    def by_tree(i):
        return lax.dynamic_index_in_dim(part(i)[:, 0], c, 1, keepdims=False)

    all_positions = by_tree(5).reshape(-1).astype(f32)
    all_parents = by_tree(6).astype(jnp.int32)

    local_heads = project_weight.shape[2] // HD
    half_rows = slice_rows // 2

    def swap_cores(array):
        return lax.all_to_all(array, "c", split_axis=0, concat_axis=0, tiled=True)

    def swap_chips(array):
        return lax.all_to_all(array, ("z", "x"), split_axis=0, concat_axis=0, tiled=True)

    def join_cores(array, axis):
        return lax.all_gather(array, "c", axis=axis, tiled=True)

    send = project_weight.transpose(1, 0, 2).reshape(3, 2, half_rows, local_heads, HD)
    send = send.transpose(1, 3, 0, 2, 4)
    send = swap_cores(send).reshape(2 * local_heads, 3, half_rows, HD)
    got = swap_chips(send)
    got = join_cores(got.transpose(1, 0, 2, 3)[:, :, None], 2)
    project_head = got.reshape(3, model_width, HD)
    send = output_weight.reshape(local_heads, HD, 2, half_rows).transpose(2, 0, 1, 3)
    send = swap_cores(send).reshape(2 * local_heads, HD, half_rows)
    got = swap_chips(send)
    got = join_cores(got.transpose(1, 0, 2)[:, :, None], 2)
    output_head = got.reshape(HD, model_width)

    sub = shared_down.shape[0] // trees
    send = jnp.stack(
        [shared_gate.T.reshape(trees, sub, -1), shared_up.T.reshape(trees, sub, -1), shared_down.reshape(trees, sub, -1)],
        1,
    )
    got = swap_chips(send).transpose(1, 2, 0, 3).reshape(3, sub, model_width)
    shared_three = join_cores(got, 1)
    expert_three = join_cores(jnp.stack([expert_gate[0].T, expert_up[0].T, expert_down[0]]), 1)
    routed_units = expert_three.shape[1]
    three = jnp.concatenate([expert_three, shared_three], 1)

    all_input = gather_call(own_input, 3).reshape(tokens, model_width).astype(f32)
    all_cotangent = gather_call(own_cotangent, 4)
    norm_one = lax.rsqrt(jnp.mean(all_input * all_input, -1, keepdims=True) + EPSILON)
    normed_one = (all_input * norm_one * gain_one).astype(bf16)
    half_size = HD // 2
    inverse = ROPE_BASE ** (-(jnp.arange(half_size, dtype=f32) * 2.0 / HD))
    angles = all_positions[:, None] * inverse[None, :]
    cosine = jnp.cos(angles)
    sine = jnp.sin(angles)
    cosine = jnp.concatenate([cosine, cosine], 1)
    sine = jnp.concatenate([sine, sine], 1)
    raw = [product(normed_one, project_head[i]) + bias_head[i] for i in range(3)]
    tree_shape = (trees, seq_rows, HD)
    queries = (raw[0] * cosine + turn(raw[0]) * sine).astype(bf16).reshape(tree_shape)
    key_rows = (raw[1] * cosine + turn(raw[1]) * sine).astype(bf16).reshape(tree_shape)
    values = raw[2].astype(bf16).reshape(tree_shape)
    allowed = tree_masks(all_parents, SEG)
    scores = (
        jnp.einsum("tqd,tkd->tqk", queries, key_rows, preferred_element_type=f32)
        * score_scale
    )
    masked = jnp.where(allowed, scores, -1e30)
    highest = jnp.max(masked, -1, keepdims=True)
    exponent = jnp.exp(masked - highest)
    attention_probs = exponent / jnp.sum(exponent, -1, keepdims=True)
    probs_low = attention_probs.astype(bf16)
    heads_out = (
        jnp.einsum("tqk,tkd->tqd", probs_low, values, preferred_element_type=f32)
        .astype(bf16)
        .reshape(tokens, HD)
    )
    attention = reduce_call(product(heads_out, output_head).astype(bf16).reshape(blocks), 5)
    own_rows_in = own_input.astype(f32)
    own_norm_one = lax.rsqrt(jnp.mean(own_rows_in * own_rows_in, -1, keepdims=True) + EPSILON)
    hidden_state = own_rows_in + attention
    norm_two = lax.rsqrt(jnp.mean(hidden_state * hidden_state, -1, keepdims=True) + EPSILON)
    own_normed_two = (hidden_state * norm_two * gain_two).astype(bf16)

    first = y * own_rows
    my_routes = lax.dynamic_slice(routes, (c, first, 0), (1, own_rows, top_count))[0]
    my_slots = lax.dynamic_slice(route_slots, (c, first, 0), (1, own_rows, top_count))[0]
    logits = product_right(own_normed_two, small_weights)
    prob = jax.nn.softmax(logits[:, :expert_count], axis=-1)
    shared_scale = jax.nn.sigmoid(logits[:, expert_count:])
    onehot = (my_routes[..., None] == jnp.arange(expert_count, dtype=jnp.int32)).astype(f32)
    kept = jnp.sum(onehot * (my_slots < capacity).astype(f32)[..., None], 1)
    onehot = jnp.sum(onehot, 1)
    picked_sum = jnp.sum(onehot * prob, -1, keepdims=True)
    every_gate = onehot * prob / picked_sum
    row_scales = jnp.concatenate([every_gate * kept, shared_scale], 1)
    high = row_scales.astype(bf16)
    low = (row_scales - high.astype(f32)).astype(bf16)
    extra = jnp.concatenate(
        [
            high[:, :expert_count],
            low[:, :expert_count],
            high[:, expert_count:],
            low[:, expert_count:],
            jnp.zeros((own_rows, EXTRA - 2 * expert_count - 2), bf16),
        ],
        1,
    )
    normed_sum, ffn_out, dots, expert_sum, shared_sum = experts_call(
        jnp.concatenate([own_normed_two, extra], 1), all_cotangent, three, routed_units
    )
    own_output = (hidden_state + ffn_out).astype(bf16)
    dots = lax.dynamic_slice(dots, (0, 0, 0, 0, first), (*dots.shape[:4], own_rows))
    dots = dots.reshape(trees, 2, 8, own_rows)
    expert_dots = (dots[:, 0, 0] + dots[:, 1, 0]).T
    shared_dot = jnp.sum(dots[:, :, 1], (0, 1))[:, None]

    kept_dots = expert_dots * kept
    picked_grad = (kept_dots - jnp.sum(kept_dots * every_gate, -1, keepdims=True)) / picked_sum
    prob_grad = picked_grad * onehot
    logit_grad = prob * (prob_grad - jnp.sum(prob * prob_grad, -1, keepdims=True))
    scale_grad = shared_dot * shared_scale * (1.0 - shared_scale)
    own_small = jnp.concatenate([logit_grad, scale_grad], 1).astype(bf16)
    grad_small = product_left(own_small, own_normed_two)
    normed_two_grad = normed_sum + product(own_small, small_weights)
    upstream = own_cotangent.astype(f32)
    grad_gain_two = jnp.sum(normed_two_grad * hidden_state * norm_two, 0)
    scaled_two = normed_two_grad * gain_two
    hidden_grad_rows = (
        upstream
        + norm_two * scaled_two
        - hidden_state * norm_two**3 * jnp.mean(scaled_two * hidden_state, -1, keepdims=True)
    )
    attention_grad = gather_call(hidden_grad_rows.astype(bf16), 6).reshape(tokens, model_width)

    output_grad = product_left(heads_out, attention_grad).astype(bf16)
    heads_grad = product_right(attention_grad, output_head).astype(bf16).reshape(tree_shape)
    value_grad = jnp.einsum("tqk,tqd->tkd", probs_low, heads_grad, preferred_element_type=f32)
    prob_grads = jnp.einsum("tqd,tkd->tqk", heads_grad, values, preferred_element_type=f32)
    score_grad = (
        attention_probs
        * (prob_grads - jnp.sum(attention_probs * prob_grads, -1, keepdims=True))
    ).astype(bf16)
    query_grad = jnp.einsum("tqk,tkd->tqd", score_grad, key_rows, preferred_element_type=f32)
    key_grad = jnp.einsum("tqk,tqd->tkd", score_grad, queries, preferred_element_type=f32)
    query_grad = (query_grad * score_scale).reshape(tokens, HD)
    key_grad = (key_grad * score_scale).reshape(tokens, HD)
    query_grad = query_grad * cosine + turn_back(query_grad * sine)
    key_grad = key_grad * cosine + turn_back(key_grad * sine)
    raw_grads = [g.astype(bf16) for g in (query_grad, key_grad, value_grad.reshape(tokens, HD))]
    bias_grad = jnp.stack([jnp.sum(g.astype(f32), 0) for g in raw_grads])
    project_grad = jnp.stack([product_left(normed_one, g) for g in raw_grads]).astype(bf16)
    normed_part = sum(product_right(g, project_head[i]) for i, g in enumerate(raw_grads))
    normed_one_grad = reduce_call(normed_part.astype(bf16).reshape(blocks), 7)
    grad_gain_one = jnp.sum(normed_one_grad * own_rows_in * own_norm_one, 0)
    scaled_one = normed_one_grad * gain_one
    own_grad = (
        hidden_grad_rows
        + own_norm_one * scaled_one
        - own_rows_in * own_norm_one**3 * jnp.mean(scaled_one * own_rows_in, -1, keepdims=True)
    )
    layer_output = lax.all_gather(own_output, ("c", "y"), axis=0, tiled=True).reshape(micro_count, seq_rows, model_width)
    input_grad = lax.all_gather(own_grad, ("c", "y"), axis=0, tiled=True).reshape(micro_count, seq_rows, model_width)

    bias_place = lax.dynamic_update_slice(jnp.zeros((3, bias_full.shape[1]), f32), bias_grad, (0, head * HD))
    vectors = jnp.concatenate([grad_small, grad_gain_one[None], grad_gain_two[None]], 0)
    vectors = lax.psum(jnp.concatenate([vectors.reshape(-1), bias_place.reshape(-1)]), AXES)
    split = (expert_count + 3) * model_width
    bias_sum = vectors[split:].reshape(3, -1)
    vectors = lax.dynamic_slice(vectors[:split].reshape(-1, model_width), (0, here * slice_rows), (expert_count + 3, slice_rows))
    bias_width = project_bias.shape[1]
    bias_out = lax.dynamic_slice(bias_sum, (0, ((y * 2 + c) * trees + here) * bias_width), (3, bias_width))

    def sum_cores(array, axis):
        return lax.psum_scatter(array, "c", scatter_dimension=axis, tiled=True)

    send = project_grad.reshape(3, trees, 2, half_rows, HD)
    send = sum_cores(send, 2).reshape(3, trees, half_rows, HD).transpose(1, 0, 2, 3)
    got = swap_chips(send).reshape(2, local_heads, 3, half_rows, HD)
    got = swap_cores(got).reshape(2, local_heads, 3, half_rows, HD)
    project_out = got.transpose(0, 3, 2, 1, 4).reshape(slice_rows, 3, local_heads * HD).astype(f32)
    send = output_grad.reshape(HD, trees, 2, half_rows)
    send = sum_cores(send, 2).reshape(HD, trees, half_rows).transpose(1, 0, 2)
    got = swap_chips(send).reshape(2, local_heads, HD, half_rows)
    got = swap_cores(got).reshape(2, local_heads, HD, half_rows)
    output_out = got.transpose(1, 2, 0, 3).reshape(local_heads * HD, slice_rows).astype(f32)
    send = shared_sum.reshape(3, sub, trees, slice_rows).transpose(2, 0, 1, 3)
    got = swap_chips(send).transpose(1, 0, 2, 3).reshape(3, trees * sub, slice_rows).astype(f32)
    return (
        layer_output,
        input_grad,
        vectors[expert_count + 1],
        project_out,
        bias_out,
        output_out,
        vectors[expert_count + 2],
        vectors[:expert_count].T,
        vectors[expert_count],
        got[0].T,
        got[1].T,
        got[2],
        expert_sum[0].T[None],
        expert_sum[1].T[None],
        expert_sum[2][None],
    )


def spread(body, mesh, rows, columns):
    def named(*dims):
        names = {"expert": rows, "tensor": columns, "both": (*columns, *rows), None: None}
        return P(*(names[d] for d in dims))

    return jax.shard_map(
        body,
        mesh=mesh,
        in_specs=(
            named(None, "expert", None),
            named(None, "expert"),
            named(None, "expert", None),
            named(None, "expert", None),
            named(None, "expert", None),
            named("expert"),
            named("expert", None, "tensor"),
            named(None, "both"),
            named("tensor", "expert"),
            named("expert"),
            named("expert", None),
            named("expert"),
            named("expert", "tensor"),
            named("expert", "tensor"),
            named("tensor", "expert"),
            named("expert", None, "tensor"),
            named("expert", None, "tensor"),
            named("expert", "tensor", None),
            named(None, "expert", None),
        ),
        out_specs=(
            named(None, "expert", None),
            named(None, "expert", None),
            named("expert"),
            named("expert", None, "tensor"),
            named(None, "both"),
            named("tensor", "expert"),
            named("expert"),
            named("expert", None),
            named("expert"),
            named("expert", "tensor"),
            named("expert", "tensor"),
            named("tensor", "expert"),
            named("expert", None, "tensor"),
            named("expert", None, "tensor"),
            named("expert", "tensor", None),
        ),
        check_vma=False,
    )


def solution(mesh):
    expert_devices, tensor_devices = mesh.shape["expert"], mesh.shape["tensor"]

    def layer(*arrays):
        heads = arrays[6].shape[2] // HD
        trees = arrays[0].shape[1] // (SEG * arrays[2].shape[2])
        if (
            tensor_devices == 4
            and expert_devices % 2 == 0
            and heads == 2 * expert_devices
            and arrays[10].shape[1] == expert_devices
            and trees == expert_devices
            and arrays[0].shape[0] == 2
        ):
            grid = Mesh(mesh.devices.reshape(expert_devices // 2, 2, 2, 2), AXES)
            body = spread(chip_shards, grid, ("z", "x"), ("y", "c"))
        else:
            body = spread(gathered_shards, mesh, ("expert",), ("tensor",))
        return body(*arrays)

    return layer
```

```python
import jax
import jax.numpy as jnp
from jax import lax
from jax.experimental import pallas as pl
from jax.experimental.pallas import tpu as pltpu
from jax.sharding import Mesh, PartitionSpec as P

HD = 128
SEG = 32


EPSILON = 1e-06
ROPE_BASE = 1000000.0


def product(left_side, right_side):
    return jnp.dot(left_side, right_side, preferred_element_type=jnp.float32)


def product_left(left_side, right_side):
    return lax.dot_general(
        left_side, right_side, (((0,), (0,)), ((), ())), preferred_element_type=jnp.float32
    )


def product_right(left_side, right_side):
    return lax.dot_general(
        left_side, right_side, (((1,), (1,)), ((), ())), preferred_element_type=jnp.float32
    )


def silu_slope(inputs):
    sigmoid_value = jax.nn.sigmoid(inputs)
    return sigmoid_value * (1.0 + inputs * (1.0 - sigmoid_value))


def rope_tables(position_row, head_size):
    half_size = head_size // 2
    inverse = ROPE_BASE ** (-(jnp.arange(half_size, dtype=jnp.float32) * 2.0 / head_size))
    angles = position_row.astype(jnp.float32)[:, None] * inverse[None, :]
    cosine = jnp.cos(angles)
    sine_table = jnp.sin(angles)
    return (jnp.concatenate([cosine, cosine], 1), jnp.concatenate([sine_table, sine_table], 1))


def rotate(vectors, cosine, sine_table):
    half_size = vectors.shape[-1] // 2
    turned = jnp.concatenate([-vectors[..., half_size:], vectors[..., :half_size]], -1)
    return vectors * cosine[:, None, :] + turned * sine_table[:, None, :]


def unrotate(gradient, cosine, sine_table):
    half_size = gradient.shape[-1] // 2
    scaled = gradient * sine_table[:, None, :]
    turned = jnp.concatenate([scaled[..., half_size:], -scaled[..., :half_size]], -1)
    return gradient * cosine[:, None, :] + turned


def tree_mask(parent_row, seg_len):
    segment_count = parent_row.shape[0]
    segment_ids = jnp.arange(segment_count, dtype=jnp.int32)
    step_matrix = (
        (parent_row[:, None] == segment_ids[None, :]) & (segment_ids[:, None] > 0)
    ).astype(jnp.float32)
    identity = jnp.eye(segment_count, dtype=jnp.float32)

    def extend(loop_index, reached):
        return jnp.minimum(
            identity + jnp.dot(step_matrix, reached, precision=lax.Precision.HIGHEST), 1.0
        )

    reached = lax.fori_loop(0, segment_count, extend, identity)
    expanded = jnp.repeat(jnp.repeat(reached, seg_len, 0), seg_len, 1) > 0.5
    token_ids = jnp.arange(segment_count * seg_len, dtype=jnp.int32)
    return expanded & (token_ids[None, :] <= token_ids[:, None])


def gathered_shards(
    layer_input,
    positions,
    parents,
    routes,
    route_slots,
    norm1_gain,
    project_weight,
    project_bias,
    output_weight,
    norm2_gain,
    router_weight,
    shared_vector,
    shared_gate,
    shared_up,
    shared_down,
    expert_gate,
    expert_up,
    expert_down,
    cotangent,
):
    micro_count, seq_rows, model_width = layer_input.shape
    top_count = routes.shape[2]
    expert_count = router_weight.shape[1]
    capacity = seq_rows * top_count * 5 // (4 * expert_count)
    slot_total = expert_count * capacity
    gathered = (
        lax.all_gather(norm1_gain, "expert", axis=0, tiled=True),
        lax.all_gather(project_weight, "expert", axis=0, tiled=True),
        lax.all_gather(project_bias, "expert", axis=1, tiled=True),
        lax.all_gather(output_weight, "expert", axis=1, tiled=True),
        lax.all_gather(norm2_gain, "expert", axis=0, tiled=True),
        lax.all_gather(router_weight, "expert", axis=0, tiled=True),
        lax.all_gather(shared_vector, "expert", axis=0, tiled=True),
        lax.all_gather(shared_gate, "expert", axis=0, tiled=True),
        lax.all_gather(shared_up, "expert", axis=0, tiled=True),
        lax.all_gather(shared_down, "expert", axis=1, tiled=True),
    )
    (
        gain_first,
        project_in,
        bias_in,
        project_out,
        gain_second,
        router_full,
        vector_full,
        shared_gates,
        shared_ups,
        shared_downs,
    ) = gathered
    local_width = project_in.shape[2]
    head_count = local_width // HD
    shared_local = shared_gates.shape[1]
    project_flat = project_in.reshape(model_width, 3 * local_width)
    bias_flat = bias_in.astype(jnp.float32).reshape(3 * local_width)
    gain_one = gain_first.astype(jnp.float32)
    gain_two = gain_second.astype(jnp.float32)
    small_weights = jnp.concatenate([router_full, vector_full[:, None]], 1)
    expert_gates = expert_gate[0]
    expert_ups = expert_up[0]
    expert_downs = expert_down[0]
    score_scale = HD ** (-0.5)
    expert_ids = jnp.arange(expert_count, dtype=jnp.int32)
    pair_ids = jnp.arange(seq_rows * top_count, dtype=jnp.int32).reshape(seq_rows, top_count)
    zero_row = jnp.zeros((1, model_width), jnp.bfloat16)
    stored = []
    layer_outputs = []
    for batch_index in range(micro_count):
        input_rows = layer_input[batch_index].astype(jnp.float32)
        norm_one = lax.rsqrt(jnp.mean(input_rows * input_rows, -1, keepdims=True) + EPSILON)
        normed_one = (input_rows * norm_one * gain_one).astype(jnp.bfloat16)
        projected = (product(normed_one, project_flat) + bias_flat).reshape(
            seq_rows, 3, head_count, HD
        )
        cosine, sine_table = rope_tables(positions[batch_index], HD)
        queries = rotate(projected[:, 0], cosine, sine_table).astype(jnp.bfloat16)
        key_rows = rotate(projected[:, 1], cosine, sine_table).astype(jnp.bfloat16)
        values = projected[:, 2].astype(jnp.bfloat16)
        allowed = tree_mask(parents[batch_index, 0], SEG)
        scores = (
            jnp.einsum("qhd,khd->hqk", queries, key_rows, preferred_element_type=jnp.float32)
            * score_scale
        )
        masked = jnp.where(allowed[None], scores, -1e30)
        highest = jnp.max(masked, -1, keepdims=True)
        exponent = jnp.exp(masked - highest)
        row_total = jnp.sum(exponent, -1, keepdims=True)
        attention_probs = exponent / row_total
        log_total = highest + jnp.log(row_total)
        heads_out = (
            jnp.einsum(
                "hqk,khd->qhd",
                attention_probs.astype(jnp.bfloat16),
                values,
                preferred_element_type=jnp.float32,
            )
            .astype(jnp.bfloat16)
            .reshape(seq_rows, local_width)
        )
        attention = lax.psum(product(heads_out, project_out), "tensor")
        hidden_state = input_rows + attention
        norm_two = lax.rsqrt(jnp.mean(hidden_state * hidden_state, -1, keepdims=True) + EPSILON)
        normed_two = (hidden_state * norm_two * gain_two).astype(jnp.bfloat16)
        small_logits = product(normed_two, small_weights)
        router_prob = jax.nn.softmax(small_logits[:, :expert_count], axis=-1)
        onehot = (routes[batch_index][..., None] == expert_ids).astype(jnp.float32)
        picked = jnp.sum(onehot * router_prob[:, None, :], -1)
        picked_sum = jnp.sum(picked, -1, keepdims=True)
        route_gates = picked / picked_sum
        shared_scale = jax.nn.sigmoid(small_logits[:, expert_count])
        gate_shared = product(normed_two, shared_gates)
        up_shared = product(normed_two, shared_ups)
        hidden_shared = (jax.nn.silu(gate_shared) * up_shared).astype(jnp.bfloat16)
        shared_part = product(hidden_shared, shared_downs)
        slot_rows = route_slots[batch_index]
        valid = slot_rows < capacity
        keep_mask = valid.astype(jnp.float32)
        slot_index = routes[batch_index] * capacity + jnp.minimum(slot_rows, capacity - 1)
        safe_index = jnp.where(valid, slot_index, 0)
        target = jnp.where(valid, slot_index, slot_total).reshape(-1)
        slot_table = (
            jnp.full((slot_total,), seq_rows * top_count, jnp.int32)
            .at[target]
            .set(pair_ids.reshape(-1), mode="drop")
        )
        padded = jnp.concatenate([normed_two, zero_row], 0)
        outgoing = padded[slot_table // top_count].reshape(expert_count, capacity, model_width)
        received = lax.all_to_all(outgoing, "expert", split_axis=0, concat_axis=0, tiled=True)
        run_owner_rows = received.reshape(-1, model_width)
        run_gate_expert = product(run_owner_rows, expert_gates)
        run_up_expert = product(run_owner_rows, expert_ups)
        run_hidden_expert = (jax.nn.silu(run_gate_expert) * run_up_expert).astype(jnp.bfloat16)
        expert_rows = product(run_hidden_expert, expert_downs).reshape(
            received.shape[0], received.shape[1], model_width
        )
        returned = lax.all_to_all(expert_rows, "expert", split_axis=0, concat_axis=0, tiled=True)
        returned, received = (returned, received)
        pair_out = returned.reshape(slot_total, -1)[safe_index] * keep_mask[..., None]
        routed = jnp.sum(route_gates[..., None] * pair_out, 1)
        shared_out, routed_full = lax.psum((shared_part, routed), "tensor")
        layer_outputs.append(
            (hidden_state + shared_scale[:, None] * shared_out + routed_full).astype(jnp.bfloat16)
        )
        stored.append(
            (
                input_rows,
                norm_one,
                normed_one,
                cosine,
                sine_table,
                queries,
                key_rows,
                values,
                allowed,
                log_total,
                heads_out,
                hidden_state,
                norm_two,
                normed_two,
                router_prob,
                onehot,
                picked_sum,
                route_gates,
                shared_scale,
                gate_shared,
                up_shared,
                hidden_shared,
                shared_out,
                pair_out,
                safe_index,
                keep_mask,
                slot_table,
                received,
            )
        )
    grad_gain_one = jnp.zeros((model_width,), jnp.float32)
    grad_gain_two = jnp.zeros((model_width,), jnp.float32)
    grad_project = jnp.zeros((model_width, 3 * local_width), jnp.float32)
    grad_bias = jnp.zeros((3 * local_width,), jnp.float32)
    grad_output = jnp.zeros((local_width, model_width), jnp.float32)
    grad_small = jnp.zeros((model_width, expert_count + 1), jnp.float32)
    grad_shared_gate = jnp.zeros((model_width, shared_local), jnp.float32)
    grad_shared_up = jnp.zeros((model_width, shared_local), jnp.float32)
    grad_shared_down = jnp.zeros((shared_local, model_width), jnp.float32)
    grad_expert_gate = jnp.zeros(expert_gates.shape, jnp.float32)
    grad_expert_up = jnp.zeros(expert_ups.shape, jnp.float32)
    grad_expert_down = jnp.zeros(expert_downs.shape, jnp.float32)
    input_grads = [None] * micro_count
    for batch_index in reversed(range(micro_count)):
        (
            input_rows,
            norm_one,
            normed_one,
            cosine,
            sine_table,
            queries,
            key_rows,
            values,
            allowed,
            log_total,
            heads_out,
            hidden_state,
            norm_two,
            normed_two,
            router_prob,
            onehot,
            picked_sum,
            route_gates,
            shared_scale,
            gate_shared,
            up_shared,
            hidden_shared,
            shared_out,
            pair_out,
            safe_index,
            keep_mask,
            slot_table,
            received,
        ) = stored[batch_index]
        upstream = cotangent[batch_index].astype(jnp.float32)
        shared_grad = (shared_scale[:, None] * upstream).astype(jnp.bfloat16)
        scale_grad = jnp.sum(upstream * shared_out, -1) * shared_scale * (1.0 - shared_scale)
        gate_part = jnp.sum(upstream[:, None, :] * pair_out, -1)
        pair_grad = (
            (route_gates[..., None] * upstream[:, None, :])
            .astype(jnp.bfloat16)
            .reshape(seq_rows * top_count, model_width)
        )
        outgoing_grad = jnp.concatenate([pair_grad, zero_row], 0)[slot_table].reshape(
            expert_count, capacity, model_width
        )
        arrived = lax.all_to_all(outgoing_grad, "expert", split_axis=0, concat_axis=0, tiled=True)
        owner_rows = received.reshape(-1, model_width)
        owner_grads = arrived.reshape(-1, model_width)
        gate_expert = product(owner_rows, expert_gates)
        up_expert = product(owner_rows, expert_ups)
        active_expert = jax.nn.silu(gate_expert)
        hidden_expert = (active_expert * up_expert).astype(jnp.bfloat16)
        hidden_expert_grad = product_right(owner_grads, expert_downs)
        grad_expert_down = grad_expert_down + product_left(hidden_expert, owner_grads)
        gate_expert_grad = (hidden_expert_grad * up_expert * silu_slope(gate_expert)).astype(
            jnp.bfloat16
        )
        up_expert_grad = (hidden_expert_grad * active_expert).astype(jnp.bfloat16)
        grad_expert_gate = grad_expert_gate + product_left(owner_rows, gate_expert_grad)
        grad_expert_up = grad_expert_up + product_left(owner_rows, up_expert_grad)
        row_grad = product_right(gate_expert_grad, expert_gates) + product_right(
            up_expert_grad, expert_ups
        )
        row_back = lax.all_to_all(
            row_grad.reshape(expert_count, capacity, model_width),
            "expert",
            split_axis=0,
            concat_axis=0,
            tiled=True,
        )
        routed_back = jnp.sum(
            row_back.reshape(slot_total, model_width)[safe_index] * keep_mask[..., None], 1
        )
        hidden_shared_grad = product_right(shared_grad, shared_downs)
        grad_shared_down = grad_shared_down + product_left(hidden_shared, shared_grad)
        gate_shared_grad = (hidden_shared_grad * up_shared * silu_slope(gate_shared)).astype(
            jnp.bfloat16
        )
        up_shared_grad = (hidden_shared_grad * jax.nn.silu(gate_shared)).astype(jnp.bfloat16)
        grad_shared_gate = grad_shared_gate + product_left(normed_two, gate_shared_grad)
        grad_shared_up = grad_shared_up + product_left(normed_two, up_shared_grad)
        normed_part = (
            product_right(gate_shared_grad, shared_gates)
            + product_right(up_shared_grad, shared_ups)
            + routed_back
        )
        normed_sum, gate_grad = lax.psum((normed_part, gate_part), "tensor")
        picked_grad = (gate_grad - jnp.sum(gate_grad * route_gates, -1, keepdims=True)) / picked_sum
        prob_grad = jnp.sum(picked_grad[..., None] * onehot, 1)
        logit_grad = router_prob * (prob_grad - jnp.sum(router_prob * prob_grad, -1, keepdims=True))
        small_grad = jnp.concatenate([logit_grad, scale_grad[:, None]], 1).astype(jnp.bfloat16)
        grad_small = grad_small + product_left(normed_two, small_grad)
        normed_two_grad = normed_sum + product_right(small_grad, small_weights)
        grad_gain_two = grad_gain_two + jnp.sum(normed_two_grad * hidden_state * norm_two, 0)
        scaled_two = normed_two_grad * gain_two
        hidden_grad = (
            upstream
            + norm_two * scaled_two
            - hidden_state * norm_two**3 * jnp.mean(scaled_two * hidden_state, -1, keepdims=True)
        )
        attention_grad = hidden_grad.astype(jnp.bfloat16)
        grad_output = grad_output + product_left(heads_out, attention_grad)
        heads_grad = (
            product_right(attention_grad, project_out)
            .astype(jnp.bfloat16)
            .reshape(seq_rows, head_count, HD)
        )
        scores = (
            jnp.einsum("qhd,khd->hqk", queries, key_rows, preferred_element_type=jnp.float32)
            * score_scale
        )
        masked = jnp.where(allowed[None], scores, -1e30)
        attention_probs = jnp.exp(masked - log_total)
        value_grad = jnp.einsum(
            "hqk,qhd->khd",
            attention_probs.astype(jnp.bfloat16),
            heads_grad,
            preferred_element_type=jnp.float32,
        )
        prob_grads = jnp.einsum(
            "qhd,khd->hqk", heads_grad, values, preferred_element_type=jnp.float32
        )
        score_grad = (
            attention_probs
            * (prob_grads - jnp.sum(attention_probs * prob_grads, -1, keepdims=True))
        ).astype(jnp.bfloat16)
        query_grad = (
            jnp.einsum("hqk,khd->qhd", score_grad, key_rows, preferred_element_type=jnp.float32)
            * score_scale
        )
        key_grad = (
            jnp.einsum("hqk,qhd->khd", score_grad, queries, preferred_element_type=jnp.float32)
            * score_scale
        )
        projected_grad = (
            jnp.stack(
                [
                    unrotate(query_grad, cosine, sine_table),
                    unrotate(key_grad, cosine, sine_table),
                    value_grad,
                ],
                1,
            )
            .astype(jnp.bfloat16)
            .reshape(seq_rows, 3 * local_width)
        )
        grad_bias = grad_bias + jnp.sum(projected_grad.astype(jnp.float32), 0)
        grad_project = grad_project + product_left(normed_one, projected_grad)
        normed_one_grad = lax.psum(
            product_right(projected_grad, project_flat).astype(jnp.bfloat16), "tensor"
        ).astype(jnp.float32)
        grad_gain_one = grad_gain_one + jnp.sum(normed_one_grad * input_rows * norm_one, 0)
        scaled_one = normed_one_grad * gain_one
        input_grads[batch_index] = (
            hidden_grad
            + norm_one * scaled_one
            - input_rows * norm_one**3 * jnp.mean(scaled_one * input_rows, -1, keepdims=True)
        )
    reduced = (
        lax.psum_scatter(
            grad_gain_one.astype(jnp.bfloat16), "expert", scatter_dimension=0, tiled=True
        ).astype(jnp.float32),
        lax.psum_scatter(
            grad_project.reshape(model_width, 3, local_width).astype(jnp.bfloat16),
            "expert",
            scatter_dimension=0,
            tiled=True,
        ).astype(jnp.float32),
        lax.psum_scatter(
            grad_bias.reshape(3, local_width).astype(jnp.bfloat16),
            "expert",
            scatter_dimension=1,
            tiled=True,
        ).astype(jnp.float32),
        lax.psum_scatter(
            grad_output.astype(jnp.bfloat16), "expert", scatter_dimension=1, tiled=True
        ).astype(jnp.float32),
        lax.psum_scatter(
            grad_gain_two.astype(jnp.bfloat16), "expert", scatter_dimension=0, tiled=True
        ).astype(jnp.float32),
        lax.psum_scatter(
            grad_small[:, :expert_count].astype(jnp.bfloat16),
            "expert",
            scatter_dimension=0,
            tiled=True,
        ).astype(jnp.float32),
        lax.psum_scatter(
            grad_small[:, expert_count].astype(jnp.bfloat16),
            "expert",
            scatter_dimension=0,
            tiled=True,
        ).astype(jnp.float32),
        lax.psum_scatter(
            grad_shared_gate.astype(jnp.bfloat16), "expert", scatter_dimension=0, tiled=True
        ).astype(jnp.float32),
        lax.psum_scatter(
            grad_shared_up.astype(jnp.bfloat16), "expert", scatter_dimension=0, tiled=True
        ).astype(jnp.float32),
        lax.psum_scatter(
            grad_shared_down.astype(jnp.bfloat16), "expert", scatter_dimension=1, tiled=True
        ).astype(jnp.float32),
    )
    return (
        jnp.stack(layer_outputs),
        jnp.stack(input_grads),
        reduced[0],
        reduced[1],
        reduced[2],
        reduced[3],
        reduced[4],
        reduced[5],
        reduced[6],
        reduced[7],
        reduced[8],
        reduced[9],
        grad_expert_gate[None],
        grad_expert_up[None],
        grad_expert_down[None],
    )


AXES = ("z", "x", "y", "c")


MESH_ID = pl.DeviceIdType.MESH
VMEM_LIMIT = 60 * 1024 * 1024


def positions_here():
    return tuple(lax.axis_index(a) for a in AXES)


def planes_from(z):
    return (z, z + 1 - 2 * (z % 2), 2 - z // 2, 3 * (1 - z // 2))


def greet(barrier, partners):
    for partner in partners:
        pl.semaphore_signal(barrier, inc=1, device_id=partner, device_id_type=MESH_ID)
    pl.semaphore_wait(barrier, len(partners))


def near_partners(z, x, y):
    planes = planes_from(z)
    return [{"x": 1 - x}, {"y": 1 - y}] + [{"z": p} for p in planes[1:]]


def run(*steps):
    for step in steps:
        step()


class Sends:
    def __init__(self):
        self.open = []

    def start(self, source, target, send, receive, where, only=None):
        copy = pltpu.make_async_remote_copy(
            src_ref=source, dst_ref=target, send_sem=send, recv_sem=receive, device_id=where, device_id_type=MESH_ID
        )
        if only is None:
            copy.start()
        else:
            pl.when(only)(copy.start)
        self.open.append((copy, only))

    def finish(self):
        for copy, only in self.open:
            if only is None:
                copy.wait_send()
            else:
                pl.when(only)(copy.wait_send)
        self.open = []


def arrive(buffer, receive):
    pltpu.make_async_copy(buffer, buffer, receive).wait()


class Gather:
    ready = (5, 8, 11, 14)

    def __init__(self, held, send, receive, cut, sends):
        self.held, self.send, self.receive, self.sends = held, send, receive, sends
        width = held.shape[-1]
        self.left, self.right = pl.ds(0, cut), pl.ds(cut, width - cut)
        self.z, self.x, self.y, _ = positions_here()
        self.planes = planes_from(self.z)
        self.inner = jnp.logical_or(self.z == 1, self.z == 2)

    def block(self, plane, x, y, columns=None):
        if columns is None:
            return self.held.at[plane, x, y]
        return self.held.at[plane, x, y, :, columns]

    def pass_on(self, plane, x, y, columns, slot, axis):
        here = self.x if axis == "x" else self.y
        ref = self.block(plane, x, y, columns)
        self.sends.start(ref, ref, self.send.at[slot, plane], self.receive.at[slot, plane], {axis: 1 - here})

    def along(self, plane, slot, to, only=None):
        ref = self.block(plane, self.x, self.y)
        self.sends.start(ref, ref, self.send.at[slot, plane], self.receive.at[6, plane], {"z": to}, only)

    def plane(self, step):
        plane = self.planes[step]
        arrive(self.block(plane, self.x, self.y), self.receive.at[6, plane])
        self.along(plane, 6, 3 - self.z if step == 1 else self.planes[1], self.inner)

    def first(self, step, part):
        plane, x, y = self.planes[step], self.x, self.y
        if part == 0:
            self.pass_on(plane, x, y, self.left, 0, "x")
            self.pass_on(plane, x, y, self.right, 1, "y")
        else:
            self.pass_on(plane, x, y, self.left, 2, "y")
            self.pass_on(plane, x, y, self.right, 3, "x")

    def second(self, step):
        plane, x, y = self.planes[step], self.x, self.y
        arrive(self.block(plane, 1 - x, y, self.left), self.receive.at[0, plane])
        self.pass_on(plane, 1 - x, y, self.left, 4, "y")
        arrive(self.block(plane, x, 1 - y, self.right), self.receive.at[1, plane])
        self.pass_on(plane, x, 1 - y, self.right, 5, "x")

    def third(self, step):
        plane, x, y = self.planes[step], self.x, self.y
        arrive(self.block(plane, x, 1 - y, self.left), self.receive.at[2, plane])
        arrive(self.block(plane, 1 - x, y, self.right), self.receive.at[3, plane])

    def fourth(self, step):
        plane, x, y = self.planes[step], self.x, self.y
        arrive(self.block(plane, 1 - x, 1 - y, self.left), self.receive.at[4, plane])
        arrive(self.block(plane, 1 - x, 1 - y, self.right), self.receive.at[5, plane])

    def steps(self):
        def begin():
            self.first(0, 0)
            self.along(self.z, 6, self.planes[1])
            self.along(self.z, 7, 3 - self.z, self.inner)
            self.first(0, 1)

        found = [begin, lambda: self.plane(1), lambda: self.second(0)]
        for step in range(4):

            def turn_over(step=step):
                if 0 < step + 2 < 4:
                    self.plane(step + 2)
                self.third(step)
                if step < 3:
                    self.first(step + 1, 0)

            def close(step=step):
                self.fourth(step)
                if step < 3:
                    self.first(step + 1, 1)

            found += [turn_over, close]
            if step < 3:
                found.append(lambda step=step: self.second(step + 1))
        return found

    @staticmethod
    def semaphores():
        return [pltpu.SemaphoreType.DMA((8, 4)), pltpu.SemaphoreType.DMA((7, 4))]


class Reduce:
    def __init__(self, parts, buffers, cut, sends):
        self.parts, self.sends = parts, sends
        self.one_left, self.one_right, self.two_left, self.two_right, self.last, self.send, self.receive = buffers
        width = parts.shape[-1]
        self.left, self.right = pl.ds(0, cut), pl.ds(cut, width - cut)
        self.z, self.x, self.y, _ = positions_here()
        self.planes = planes_from(self.z)

    @staticmethod
    def buffers(rows, width, cut):
        bf16 = jnp.bfloat16
        return [
            pltpu.VMEM((4, 2, rows, cut), bf16),
            pltpu.VMEM((4, 2, rows, width - cut), bf16),
            pltpu.VMEM((4, rows, cut), bf16),
            pltpu.VMEM((4, rows, width - cut), bf16),
            pltpu.VMEM((4, rows, width), bf16),
            pltpu.SemaphoreType.DMA((7, 4)),
            pltpu.SemaphoreType.DMA((7, 4)),
        ]

    def first(self, step, part):
        plane, x, y = self.planes[step], self.x, self.y
        its_x, its_y = (1 - x, 1 - y) if part == 0 else (x, y)
        self.sends.start(
            self.parts.at[plane, its_x, 1 - y, :, self.left], self.one_left.at[plane, part],
            self.send.at[part, plane], self.receive.at[part, plane], {"y": 1 - y},
        )
        self.sends.start(
            self.parts.at[plane, 1 - x, its_y, :, self.right], self.one_right.at[plane, part],
            self.send.at[2 + part, plane], self.receive.at[2 + part, plane], {"x": 1 - x},
        )

    def add(self, ref, other):
        ref[...] = (ref[...].astype(jnp.float32) + other[...].astype(jnp.float32)).astype(ref.dtype)

    def second(self, step):
        plane, x, y = self.planes[step], self.x, self.y
        arrive(self.one_left.at[plane, 0], self.receive.at[0, plane])
        away = self.parts.at[plane, 1 - x, y, :, self.left]
        self.add(away, self.one_left.at[plane, 0])
        self.sends.start(away, self.two_left.at[plane], self.send.at[4, plane], self.receive.at[4, plane], {"x": 1 - x})
        arrive(self.one_right.at[plane, 0], self.receive.at[2, plane])
        away = self.parts.at[plane, x, 1 - y, :, self.right]
        self.add(away, self.one_right.at[plane, 0])
        self.sends.start(away, self.two_right.at[plane], self.send.at[5, plane], self.receive.at[5, plane], {"y": 1 - y})

    def keep(self, step):
        plane, x, y = self.planes[step], self.x, self.y
        arrive(self.one_left.at[plane, 1], self.receive.at[1, plane])
        arrive(self.one_right.at[plane, 1], self.receive.at[3, plane])
        self.add(self.parts.at[plane, x, y, :, self.left], self.one_left.at[plane, 1])
        self.add(self.parts.at[plane, x, y, :, self.right], self.one_right.at[plane, 1])

    def third(self, step):
        plane, x, y = self.planes[step], self.x, self.y
        here = self.parts.at[plane, x, y]
        arrive(self.two_left.at[plane], self.receive.at[4, plane])
        arrive(self.two_right.at[plane], self.receive.at[5, plane])
        self.add(here.at[:, self.left], self.two_left.at[plane])
        self.add(here.at[:, self.right], self.two_right.at[plane])
        if step:
            self.sends.start(here, self.last.at[self.z], self.send.at[6, plane], self.receive.at[6, self.z], {"z": plane})

    def steps(self, order):
        def begin():
            self.first(order[0], 0)
            self.first(order[0], 1)

        found = [begin]
        for i in range(4):

            def keep(i=i):
                self.keep(order[i])
                if i < 3:
                    self.first(order[i + 1], 0)

            def third(i=i):
                self.third(order[i])
                if i < 3:
                    self.first(order[i + 1], 1)

            found += [lambda i=i: self.second(order[i]), keep, third]
        return found

    def total(self):
        here = self.parts[self.z, self.x, self.y].astype(jnp.float32)
        for plane in self.planes[1:]:
            arrive(self.last.at[plane], self.receive.at[6, plane])
            here = here + self.last[plane].astype(jnp.float32)
        return here


EXTRA = 128


def dot_nn(a, b):
    return lax.dot_general(a, b, (((1,), (0,)), ((), ())), preferred_element_type=jnp.float32)


def dot_nt(a, b):
    return lax.dot_general(a, b, (((1,), (1,)), ((), ())), preferred_element_type=jnp.float32)


def dot_tn(a, b):
    return lax.dot_general(a, b, (((0,), (0,)), ((), ())), preferred_element_type=jnp.float32)


def chips_but(z, x, y):
    found = []
    for dz in range(4):
        for dx in range(2):
            for dy in range(2):
                if dz or dx or dy:
                    found.append({"z": lax.rem(z + dz, 4), "x": (x + dx) % 2, "y": (y + dy) % 2})
    return found


def experts_call(own, cotangents, three, routed_units):
    bf16, f32 = jnp.bfloat16, jnp.float32
    rows, wide = own.shape
    width = wide - EXTRA
    units = three.shape[1]
    shared_units = units - routed_units
    tile = routed_units // 2
    assert shared_units == tile
    chunk = 4 * rows
    tokens = 4 * chunk
    cut = width // 2
    column = 1024
    half_tile = tile // 2
    keep = tile + half_tile

    def kernel(own_ref, cot_ref, three_ref, sum_ref, out_ref, dot_ref, expert0, expert1, expert2, shared_ref, held, weights, hidden, gate_grad, up_grad,
               part_n, part_o, dots_mine, staged, *rest):
        (g_send, g_recv, w_sem, d_send, d_recv, free, x_send, x_recv, s_sem) = rest[:9]
        n_bufs, o_bufs = rest[9:16], rest[16:23]
        z, x, y, c = positions_here()
        here = z * 2 + x
        loads = [pltpu.make_async_copy(three_ref.at[i], weights.at[i], w_sem.at[i]) for i in range(3)]
        for load in loads:
            load.start()
        others = chips_but(z, x, y)
        greet(pltpu.get_barrier_semaphore(), others + [{"c": 1 - c}])
        held[z, x, y] = own_ref[...]
        sends = Sends()
        gather = Gather(held, g_send, g_recv, cut, sends)
        sum_n = Reduce(part_n, n_bufs, cut, sends)
        sum_o = Reduce(part_o, o_bufs, cut, sends)
        lanes = lax.broadcasted_iota(jnp.int32, (16, EXTRA), 1)
        rows_of = lax.broadcasted_iota(jnp.int32, (16, EXTRA), 0)
        pick = ((rows_of == 0) & ((lanes == here) | (lanes == here + 8))) | ((rows_of == 1) & ((lanes == 16) | (lanes == 17)))
        pick = pick.astype(f32).astype(bf16)

        def units_of(step):
            plane = gather.planes[step]
            place = pl.ds(pl.multiple_of(plane * chunk, chunk), chunk)
            rows_n = held[plane, :, :, :, 0:width].reshape(chunk, width)
            rows_c = cot_ref[plane].reshape(chunk, width)
            scales = dot_nt(pick, held[plane, :, :, :, width:wide].reshape(chunk, EXTRA))

            def one(i, _):
                span = pl.ds(pl.multiple_of(i * tile, 32), tile)
                scale = jnp.where(i == 2, scales[1:2], scales[0:1])
                gate = dot_nt(weights[0, span, :], rows_n)
                up = dot_nt(weights[1, span, :], rows_n)
                down = dot_nt(weights[2, span, :], rows_c)
                sig = 1.0 / (1.0 + jnp.exp(-gate))
                active = gate * sig
                hid = active * up
                dot = jnp.sum(hid * down, 0, keepdims=True)
                hidden[span, place] = (hid * scale).astype(bf16)
                grad = down * scale
                gate_grad[span, place] = (grad * up * (sig + active * (1.0 - sig))).astype(bf16)
                up_grad[span, place] = (grad * active).astype(bf16)
                routed, shared = lax.cond(i == 2, lambda: (jnp.zeros_like(dot), dot), lambda: (dot, jnp.zeros_like(dot)))
                return (_[0] + routed, _[1] + shared)

            zero = jnp.zeros((1, chunk), f32)
            routed, shared = lax.fori_loop(0, 3, one, (zero, zero))
            row = lax.broadcasted_iota(jnp.int32, (8, chunk), 0)
            both = jnp.where(row == 0, routed, jnp.where(row == 1, shared, 0.0))
            for t in range(2):
                dots_mine[plane, t] = both[:, t * 2 * rows : (t + 1) * 2 * rows]

        def back_of(step):
            plane = gather.planes[step]
            place = pl.ds(pl.multiple_of(plane * chunk, chunk), chunk)

            def one(i, _):
                span = pl.ds(pl.multiple_of(i * column, column), column)
                value = dot_tn(gate_grad[:, place], weights[0, :, span]) + dot_tn(up_grad[:, place], weights[1, :, span])
                part_n[plane, :, :, :, span] = value.astype(bf16).reshape(2, 2, rows, column)
                return 0

            lax.fori_loop(0, width // column, one, 0)

        def out_of(step):
            plane = gather.planes[step]
            place = pl.ds(pl.multiple_of(plane * chunk, chunk), chunk)

            def one(i, _):
                span = pl.ds(pl.multiple_of(i * column, column), column)
                value = dot_tn(hidden[:, place], weights[2, :, span])
                part_o[plane, :, :, :, span] = value.astype(bf16).reshape(2, 2, rows, column)
                return 0

            lax.fori_loop(0, width // column, one, 0)

        g, n, o = gather.steps(), sum_n.steps((0, 1, 2, 3)), sum_o.steps((0, 1, 2, 3))
        run(*g[0:4])
        for load in loads:
            load.wait()
        g[4]()
        units_of(0)
        g[5]()
        back_of(0)
        run(n[0], g[6], g[7])
        units_of(1)
        run(n[1], g[8])
        back_of(1)
        run(n[2], n[3], g[9], g[10])
        units_of(2)
        run(n[4], g[11])
        back_of(2)
        run(n[5], n[6], g[12], g[13])
        units_of(3)
        n[7]()
        back_of(3)
        run(n[8], n[9])
        out_of(0)
        run(o[0], n[10])
        out_of(1)
        run(n[11], o[1], n[12], o[2], o[3])
        out_of(2)
        run(o[4], o[5])
        out_of(3)
        for i, other in enumerate(others):
            sends.start(dots_mine.at[other["z"], other["x"]], dot_ref.at[z, x, y], d_send.at[i], d_recv.at[z, x, y], other)
        dot_ref[z, x, y] = dots_mine[z, x]
        pl.semaphore_signal(free, inc=1, device_id={"c": 1 - c}, device_id_type=MESH_ID)

        def gradient(kind, first, count, span):
            if kind < 2:
                side = (gate_grad, up_grad)[kind]
                return dot_nn(side[pl.ds(first, count), :], held[:, :, :, :, span].reshape(tokens, column))
            return dot_nn(hidden[pl.ds(first, count), :], cot_ref[:, :, :, :, span].reshape(tokens, column))

        def away(core, kind):
            def one(i, _):
                span = pl.ds(pl.multiple_of(i * column, column), column)
                first = pl.multiple_of(core * tile, 32)
                weights[kind, 0:tile, span] = gradient(kind, first, tile, span).astype(bf16)
                first = pl.multiple_of(routed_units + core * half_tile, 16)
                weights[kind, tile:keep, span] = gradient(kind, first, half_tile, span).astype(bf16)
                return 0

            lax.fori_loop(0, width // column, one, 0)

        away(1 - c, 0)
        run(o[6], o[7])
        pl.semaphore_wait(free, 1)
        for kind in range(3):
            if kind:
                away(1 - c, kind)
            sends.start(weights.at[kind, 0:keep], weights.at[kind, keep : 2 * keep], x_send.at[kind], x_recv.at[kind], {"c": 1 - c})
            if kind < 2:
                run(o[8 + 2 * kind], o[9 + 2 * kind])
        o[12]()
        writes = []
        for kind in range(3):
            arrive(weights.at[kind, keep : 2 * keep], x_recv.at[kind])
            if kind > 1:
                writes[kind - 2].wait()

            def one(i, _):
                span = pl.ds(pl.multiple_of(i * column, column), column)
                first = pl.multiple_of(c * tile, 32)
                value = gradient(kind, first, tile, span)
                staged[kind % 2, :, span] = (value + weights[kind, keep : keep + tile, span].astype(f32)).astype(bf16)
                first = pl.multiple_of(routed_units + c * half_tile, 16)
                value = gradient(kind, first, half_tile, span)
                shared_ref[kind, :, span] = (value + weights[kind, keep + tile : 2 * keep, span].astype(f32)).astype(bf16)
                return 0

            lax.fori_loop(0, width // column, one, 0)
            write = pltpu.make_async_copy(staged.at[kind % 2], (expert0, expert1, expert2)[kind], s_sem.at[kind])
            write.start()
            writes.append(write)
        sum_ref[...] = sum_n.total()
        out_ref[...] = sum_o.total()
        for other in others:
            arrive(dot_ref.at[other["z"], other["x"], other["y"]], d_recv.at[other["z"], other["x"], other["y"]])
        writes[1].wait()
        writes[2].wait()
        sends.finish()

    vmem = pl.BlockSpec(memory_space=pltpu.VMEM)
    anywhere = pl.BlockSpec(memory_space=pl.ANY)
    dma = pltpu.SemaphoreType.DMA
    flops = 2 * tokens * width * units * 9
    return pl.pallas_call(
        kernel,
        name="experts",
        out_shape=(
            jax.ShapeDtypeStruct((rows, width), f32),
            jax.ShapeDtypeStruct((rows, width), f32),
            jax.ShapeDtypeStruct((4, 2, 2, 8, 2 * rows), f32),
            *[jax.ShapeDtypeStruct((tile, width), bf16)] * 3,
            jax.ShapeDtypeStruct((3, half_tile, width), bf16),
        ),
        in_specs=[vmem, vmem, anywhere],
        out_specs=(vmem, vmem, vmem, anywhere, anywhere, anywhere, vmem),
        scratch_shapes=[
            pltpu.VMEM((4, 2, 2, rows, wide), bf16),
            pltpu.VMEM((3, units, width), bf16),
            pltpu.VMEM((units, tokens), bf16),
            pltpu.VMEM((units, tokens), bf16),
            pltpu.VMEM((units, tokens), bf16),
            pltpu.VMEM((4, 2, 2, rows, width), bf16),
            pltpu.VMEM((4, 2, 2, rows, width), bf16),
            pltpu.VMEM((4, 2, 8, 2 * rows), f32),
            pltpu.VMEM((2, tile, width), bf16),
            *Gather.semaphores(),
            dma((3,)),
            dma((15,)),
            dma((4, 2, 2)),
            pltpu.SemaphoreType.REGULAR,
            dma((3,)),
            dma((3,)),
            dma((3,)),
            *Reduce.buffers(rows, width, cut),
            *Reduce.buffers(rows, width, cut),
        ],
        compiler_params=pltpu.CompilerParams(collective_id=2, has_side_effects=True, vmem_limit_bytes=VMEM_LIMIT),
        cost_estimate=pl.CostEstimate(flops=flops, bytes_accessed=40 * 1024 * 1024, transcendentals=tokens * units),
    )(own, cotangents, three)


def plane_partners(z, x, y, c):
    found = []
    for dz in range(4):
        for dx in range(2):
            for dc in range(2):
                if dz or dx or dc:
                    found.append({"z": lax.rem(z + dz, 4), "x": (x + dx) % 2, "c": (c + dc) % 2})
    return found


class Plain:
    def __init__(self):
        self.open = []

    def start(self, source, target, send, receive, where, same):
        far = pltpu.make_async_remote_copy(
            src_ref=source, dst_ref=target, send_sem=send, recv_sem=receive, device_id=where, device_id_type=MESH_ID
        )

        @pl.when(jnp.logical_not(same))
        def _():
            far.start()

        @pl.when(same)
        def _():
            pltpu.make_async_copy(source, target, receive).start()

        self.open.append((far, same))

    def finish(self):
        for far, same in self.open:

            @pl.when(jnp.logical_not(same))
            def _(far=far):
                far.wait_send()

        self.open = []


def front_call(input_rows, cotangent, project, output, gains, router, vector, positions, parents, bias, table, gate, up, down, experts):
    bf16, f32 = jnp.bfloat16, jnp.float32
    rows, width = input_rows.shape[-2:]
    chunk = 4 * rows
    tokens = 4 * chunk
    seq = 2 * rows
    trees = tokens // seq
    slice_rows = project.shape[1]
    half = slice_rows // 2
    local_heads = project.shape[2] // HD
    sub = down.shape[0] // trees
    tile = experts[0].shape[0]
    routed = 2 * tile
    units = routed + 2 * sub
    cut = width // 2
    late_cut = 3 * width // 4
    column = width // 2
    scale = HD ** (-0.5)
    lines = router.shape[0]

    def kernel(in_ref, cot_ref, project_ref, output_ref, gain1_ref, gain2_ref, router_ref, vector_ref, position_ref, parent_ref,
               bias_ref, table_ref, gate_ref, up_ref, down_ref, e0, e1, e2,
               sum_ref, normed_ref, qkv_ref, prob_ref, heads_ref, head_ref, outw_ref, smalls_ref, turns_ref, cots_ref, three_ref,
               all_ref, parts, small_f, small_v, shared_v, three_v, *rest):
        (g_send, g_recv, k_send, k_recv, w_send, w_recv, v_send, v_recv, m_send, m_recv, s_send, s_recv, c_send, c_recv, l_sem, e_send,
         e_recv, o_sem) = rest[:18]
        z, x, y, c = positions_here()
        here = z * 2 + x
        partners = plane_partners(z, x, y, c)
        other = {"c": 1 - c}
        sends, plain = Sends(), Plain()

        small_f[...] = jnp.zeros_like(small_f)
        small_f[0:1, :] = gain1_ref[...].astype(f32)
        small_f[1:2, :] = gain2_ref[...].astype(f32)
        small_f[2 : 2 + lines, :] = router_ref[...].astype(f32)
        small_f[2 + lines : 3 + lines, :] = vector_ref[...].astype(f32)
        first = c == 0
        small_f[3 + lines : 4 + lines, 0:seq] = jnp.where(first, position_ref[0:1, :], position_ref[1:2, :]).astype(f32)
        segments = parent_ref.shape[1]
        small_f[4 + lines : 5 + lines, 0:segments] = jnp.where(first, parent_ref[0:1, :], parent_ref[1:2, :]).astype(f32)
        small_f[5 + lines : 8 + lines, 0 : bias_ref.shape[1]] = bias_ref[...].astype(f32)
        small_v[...] = small_f[...].astype(bf16)

        greet(pltpu.get_barrier_semaphore(), partners + [{"y": 1 - y}])
        all_ref[z, x, y] = in_ref[c, y]
        gather = Gather(all_ref, g_send, g_recv, cut, sends)
        late = Gather(cots_ref, k_send, k_recv, late_cut, sends)
        add = Reduce(parts, rest[18:], late_cut, sends)
        a, g, r = gather.steps(), late.steps(), add.steps((3, 2, 1, 0))
        a[0]()
        for i, to in enumerate(partners):
            sends.start(small_v, smalls_ref.at[z, x, c], m_send.at[i], m_recv.at[z, x, c], to)
        smalls_ref[z, x, c] = small_v[...]
        for local in range(local_heads):
            chip = {"z": 2 * c + local // 2, "x": local % 2}
            home = jnp.logical_and(chip["z"] == z, chip["x"] == x)
            for part in range(2):
                where = {**chip, "c": part}
                same = jnp.logical_and(home, c == part)
                for i in range(3):
                    plain.start(
                        project_ref.at[i, pl.ds(part * half, half), pl.ds(local * HD, HD)],
                        head_ref.at[here, part, :, pl.ds(i * HD, HD)],
                        w_send.at[local, part, i], w_recv.at[here, i], where, same,
                    )
                plain.start(
                    output_ref.at[pl.ds(local * HD + part * HD // 2, HD // 2), :],
                    outw_ref.at[part, :, pl.ds(pl.multiple_of(here * slice_rows, slice_rows), slice_rows)],
                    w_send.at[local, part, 3], w_recv.at[here, 3], where, same,
                )
        mine = pl.ds(pl.multiple_of(c * tile, 16), tile)
        for i, ref in enumerate((e0, e1, e2)):
            sends.start(ref, three_v.at[i, mine], e_send.at[i], e_recv.at[i], other)
            pltpu.make_async_copy(ref, three_v.at[i, mine], l_sem.at[i]).start()

        def flip(i, _):
            span = pl.ds(pl.multiple_of(i * HD, HD), HD)
            shared_v[0, span, :] = gate_ref[:, span].astype(f32).T.astype(bf16)
            shared_v[1, span, :] = up_ref[:, span].astype(f32).T.astype(bf16)
            shared_v[2, span, :] = down_ref[span, :]
            return 0

        run(*a[1:3])
        lax.fori_loop(0, down.shape[0] // HD, flip, 0)
        run(*a[3:9])
        place = pl.ds(pl.multiple_of(routed + c * sub, 16), sub)
        lanes = pl.ds(pl.multiple_of(here * slice_rows, slice_rows), slice_rows)

        def share(i):
            to_z, to_x = lax.rem(z + i // 2, 4), (x + i % 2) % 2
            source = shared_v.at[:, pl.ds(pl.multiple_of((to_z * 2 + to_x) * sub, 16), sub)]
            target = three_v.at[:, place, lanes]
            if i:
                sends.start(source, target, s_send.at[i], s_recv.at[here], {"z": to_z, "x": to_x})
            else:
                pltpu.make_async_copy(source, target, s_recv.at[here]).start()

        for source in range(trees):
            for i in range(3):
                arrive(head_ref.at[source, c, :, pl.ds(i * HD, HD)], w_recv.at[source, i])
            arrive(outw_ref.at[c, :, pl.ds(source * slice_rows, slice_rows)], w_recv.at[source, 3])
        sends.start(head_ref.at[:, c], head_ref.at[:, c], v_send.at[0], v_recv.at[0], other)
        sends.start(outw_ref.at[c], outw_ref.at[c], v_send.at[1], v_recv.at[1], other)
        share(0)
        share(4)
        run(*a[9:])
        share(5)
        cots_ref[z, x, y] = cot_ref[c, y]
        g[0]()
        for to in partners:
            spot = (to["z"], to["x"], to["c"])
            arrive(smalls_ref.at[spot], m_recv.at[spot])
        gain = jnp.concatenate([smalls_ref[e // 2, e % 2, c, 0:1, :] for e in range(trees)], 1).astype(f32)
        home_z, home_c = lax.rem(here, 4), here // 4
        width_of = bias_ref.shape[1]
        biases = [smalls_ref[home_z, e, home_c, 5 + lines : 8 + lines, 0:width_of] for e in range(2)]
        row_bias = [jnp.concatenate([b[i : i + 1].astype(f32) for b in biases], 1) for i in range(3)]
        row_bias = jnp.concatenate(row_bias, 1)
        arrive(head_ref.at[:, 1 - c], v_recv.at[0])
        arrive(outw_ref.at[1 - c], v_recv.at[1])
        query_of = lax.broadcasted_iota(jnp.int32, (seq, seq), 0)
        key_of = lax.broadcasted_iota(jnp.int32, (seq, seq), 1)
        segment_of = lax.broadcasted_iota(jnp.int32, (1, seq), 1) // SEG
        lane = lax.broadcasted_iota(jnp.int32, (seq, HD), 1)

        def attend(step):
            plane = gather.planes[step]

            def norm(i, _):
                value = all_ref[plane, i // 2, i % 2].astype(f32)
                scaled = value * lax.rsqrt(jnp.mean(value * value, -1, keepdims=True) + EPSILON) * gain
                normed_ref[plane, i // 2, i % 2] = scaled.astype(bf16)
                return 0

            lax.fori_loop(0, 4, norm, 0)
            raw = dot_nn(normed_ref[plane].reshape(chunk, width), head_ref[...].reshape(width, 3 * HD)) + row_bias
            for t in range(2):
                span = slice(t * seq, (t + 1) * seq)
                notes = smalls_ref[plane, t, c].astype(f32)
                hot = (query_of == notes[3 + lines : 4 + lines, 0:seq].astype(jnp.int32)).astype(f32).astype(bf16)
                turn = dot_tn(hot, table_ref[0]) + dot_tn(hot, table_ref[1])
                swapped = pltpu.roll(turn, HD // 2, 1)
                cos = jnp.where(lane < HD // 2, turn, swapped)
                sin = jnp.where(lane < HD // 2, -swapped, turn)
                turns_ref[0, plane, span] = cos
                turns_ref[1, plane, span] = sin
                reach = []
                for s in range(segments):
                    line = (segment_of == s).astype(f32)
                    for u in range(s):
                        line = line + (notes[4 + lines : 5 + lines, s : s + 1] == u).astype(f32) * reach[u]
                    reach.append(line)
                seen = jnp.concatenate([jnp.broadcast_to(line, (SEG, seq)) for line in reach], 0)
                allowed = jnp.logical_and(seen > 0.5, key_of <= query_of)
                turned = []
                for i in range(2):
                    value = raw[span, i * HD : (i + 1) * HD]
                    turned.append((value * cos + pltpu.roll(value, HD // 2, 1) * sin).astype(bf16))
                turned.append(raw[span, 2 * HD :].astype(bf16))
                for i in range(3):
                    qkv_ref[i, plane, span] = turned[i]
                score = jnp.where(allowed, dot_nt(turned[0], turned[1]) * scale, -1e30)
                exponent = jnp.exp(score - jnp.max(score, -1, keepdims=True))
                prob = exponent / jnp.sum(exponent, -1, keepdims=True)
                prob_ref[plane, t] = prob
                heads_ref[plane, span] = dot_nn(prob.astype(bf16), turned[2]).astype(bf16)

            def spread_out(i, _):
                span = pl.ds(pl.multiple_of(i * column, column), column)
                value = dot_nn(heads_ref[plane], outw_ref[:, :, span].reshape(HD, column))
                parts[plane, :, :, :, span] = value.astype(bf16).reshape(2, 2, rows, column)
                return 0

            lax.fori_loop(0, width // column, spread_out, 0)

        attend(3)
        run(r[0], g[1], g[2])
        share(6)
        attend(2)
        run(r[1], r[2], g[3])
        share(7)
        run(r[3], g[4])
        attend(1)
        share(2)
        run(r[4], r[5], g[5])
        share(3)
        run(r[6], g[6])
        attend(0)
        share(1)
        for i in range(3):
            arrive(three_v.at[i, mine], l_sem.at[i])
            arrive(three_v.at[i, pl.ds(pl.multiple_of((1 - c) * tile, 16), tile)], e_recv.at[i])
        early = pltpu.make_async_copy(three_v.at[:, pl.ds(0, routed)], three_ref.at[:, pl.ds(0, routed)], o_sem.at[0])
        early.start()
        run(r[7], r[8], g[7], r[9], g[8], r[10], g[9], r[11], g[10], r[12], g[11], g[12])
        sum_ref[...] = add.total()
        for source in range(trees):
            arrive(three_v.at[:, place, pl.ds(source * slice_rows, slice_rows)], s_recv.at[source])
        sends.start(three_v.at[:, place], three_v.at[:, place], c_send, c_recv, other)
        g[13]()
        arrive(three_v.at[:, pl.ds(pl.multiple_of(routed + (1 - c) * sub, 16), sub)], c_recv)
        rest_of = pltpu.make_async_copy(
            three_v.at[:, pl.ds(routed, units - routed)], three_ref.at[:, pl.ds(routed, units - routed)], o_sem.at[1]
        )
        rest_of.start()
        early.wait()
        rest_of.wait()
        plain.finish()
        sends.finish()

    vmem = pl.BlockSpec(memory_space=pltpu.VMEM)
    anywhere = pl.BlockSpec(memory_space=pl.ANY)
    dma = pltpu.SemaphoreType.DMA
    shape = jax.ShapeDtypeStruct
    return pl.pallas_call(
        kernel,
        name="front",
        out_shape=(
            shape((rows, width), f32),
            shape((4, 2, 2, rows, width), bf16),
            shape((3, 4, chunk, HD), bf16),
            shape((4, 2, seq, seq), f32),
            shape((4, chunk, HD), bf16),
            shape((trees, 2, half, 3 * HD), bf16),
            shape((2, HD // 2, width), bf16),
            shape((4, 2, 2, 16, slice_rows), bf16),
            shape((2, 4, chunk, HD), f32),
            shape((4, 2, 2, rows, width), bf16),
            shape((3, units, width), bf16),
        ),
        in_specs=[vmem] * 18,
        out_specs=(vmem,) * 10 + (anywhere,),
        scratch_shapes=[
            pltpu.VMEM((4, 2, 2, rows, width), bf16),
            pltpu.VMEM((4, 2, 2, rows, width), bf16),
            pltpu.VMEM((16, slice_rows), f32),
            pltpu.VMEM((16, slice_rows), bf16),
            pltpu.VMEM((3, *down.shape), bf16),
            pltpu.VMEM((3, units, width), bf16),
            *Gather.semaphores(),
            *Gather.semaphores(),
            dma((local_heads, 2, 4)),
            dma((trees, 4)),
            dma((2,)),
            dma((2,)),
            dma((15,)),
            dma((4, 2, 2)),
            dma((trees,)),
            dma((trees,)),
            dma,
            dma,
            dma((3,)),
            dma((3,)),
            dma((3,)),
            dma((2,)),
            *Reduce.buffers(rows, width, late_cut),
        ],
        compiler_params=pltpu.CompilerParams(collective_id=8, has_side_effects=True, vmem_limit_bytes=VMEM_LIMIT),
    )(input_rows, cotangent, project, output, *gains, router, vector, positions, parents, bias, table, gate, up, down, *experts)


def all_but(z, x, y, c):
    found = []
    for dz in range(4):
        for dx in range(2):
            for dy in range(2):
                for dc in range(2):
                    if dz or dx or dy or dc:
                        found.append(
                            {"z": lax.rem(z + dz, 4), "x": (x + dx) % 2, "y": (y + dy) % 2, "c": (c + dc) % 2}
                        )
    return found


def attention_back_call(own_grad, normed, qkv, probs, heads, head, out_head, turns, input_rows, hidden_grad, gain, lines,
                        own_output, vectors, shared):
    bf16, f32 = jnp.bfloat16, jnp.float32
    rows, width = own_grad.shape
    chunk = 4 * rows
    tokens = 4 * chunk
    seq = 2 * rows
    trees, _, half, _ = head.shape
    slice_rows = 2 * half
    sub = shared.shape[1]
    cut = 3 * width // 4
    column = width // 2
    scale = HD ** (-0.5)
    local_heads = trees // 2

    def kernel(grad_ref, normed_ref, qkv_ref, prob_ref, heads_ref, head_ref, outw_ref, turns_ref, in_ref, hg_ref, gain_ref,
               result_ref, vec_ref, shared_ref,
               layer_ref, ig, pgrad_ref, ograd_ref, gate_ref, up_ref, down_ref, gain1_ref, gain2_ref, router_ref, vector_ref, bias_ref,
               sgrad_ref,               held, parts, raw_grad, dwp, dwp_got, dwp_sum, dwo, dwo_got, dwo_sum, message, got, bias_sum, *rest):
        (g_send, g_recv, l_send, l_recv, i_send, i_recv, m_send, m_recv, s_send, s_recv, c_send, c_recv, w_send,
         w_recv) = rest[:14]
        z, x, y, c = positions_here()
        here = z * 2 + x
        everyone = all_but(z, x, y, c)
        greet(pltpu.get_barrier_semaphore(), everyone)
        sends = Sends()
        plain = Plain()
        other, across = {"c": 1 - c}, {"y": 1 - y}
        held[z, x, y] = grad_ref[...]
        gather = Gather(held, g_send, g_recv, cut, sends)
        add = Reduce(parts, rest[14:], cut, sends)
        g, r = gather.steps(), add.steps((0, 1, 2, 3))
        g[0]()
        layer_ref[c, y] = result_ref[...]
        sends.start(layer_ref.at[c, y], layer_ref.at[c, y], l_send.at[0], l_recv.at[0], across)
        sends.start(layer_ref.at[c, y], layer_ref.at[c, y], l_send.at[1], l_recv.at[1], other)

        def lanes_of(e):
            return pl.ds(pl.multiple_of(e * slice_rows, slice_rows), slice_rows)

        bias_sum[...] = jnp.zeros_like(bias_sum)

        def attend(step):
            plane = gather.planes[step]
            grads = dot_nt(held[plane].reshape(chunk, width), outw_ref[...].reshape(HD, width)).astype(bf16)
            cos, sin = turns_ref[0, plane], turns_ref[1, plane]
            for t in range(2):
                span = slice(t * seq, (t + 1) * seq)
                prob = prob_ref[plane, t]
                out_grad = grads[span]
                query, key, value = (qkv_ref[i, plane, span] for i in range(3))
                value_grad = dot_tn(prob.astype(bf16), out_grad)
                prob_grad = dot_nt(out_grad, value)
                score_grad = (prob * (prob_grad - jnp.sum(prob * prob_grad, -1, keepdims=True))).astype(bf16)
                sides = [dot_nn(score_grad, key) * scale, dot_tn(score_grad, query) * scale]
                sides = [s * cos[span] - pltpu.roll(s, HD // 2, 1) * sin[span] for s in sides] + [value_grad]
                for i in range(3):
                    side = sides[i].astype(bf16)
                    raw_grad[plane, span, i * HD : (i + 1) * HD] = side
                    bias_sum[0:1, i * HD : (i + 1) * HD] += jnp.sum(side.astype(f32), 0, keepdims=True)

            def back(i, _):
                span = pl.ds(pl.multiple_of(i * column, column), column)
                weight = head_ref[pl.ds(i * (trees // 2), trees // 2)].reshape(column, 3 * HD)
                parts[plane, :, :, :, span] = dot_nt(raw_grad[plane], weight).astype(bf16).reshape(2, 2, rows, column)
                return 0

            lax.fori_loop(0, 2, back, 0)

        def share(i):
            to_z, to_x = lax.rem(z + i // 2, 4), (x + i % 2) % 2
            source = shared_ref.at[:, :, lanes_of(to_z * 2 + to_x)]
            target = sgrad_ref.at[:, pl.ds(pl.multiple_of(here * sub, 16), sub)]
            if i:
                sends.start(source, target, s_send.at[i], s_recv.at[here], {"z": to_z, "x": to_x})
            else:
                pltpu.make_async_copy(source, target, s_recv.at[here]).start()

        share(0)
        share(4)
        run(*g[1:3])
        share(5)
        run(*g[3:5])
        attend(0)
        run(g[5], r[0], g[6], g[7])
        share(6)
        attend(1)
        run(r[1], g[8], r[2], r[3])
        share(7)
        run(g[9], g[10])
        attend(2)
        share(2)
        run(r[4], g[11], r[5])
        share(3)
        run(r[6], g[12], g[13])
        share(1)
        attend(3)
        run(r[7], r[8], r[9])
        arrive(layer_ref.at[c, 1 - y], l_recv.at[0])
        sends.start(layer_ref.at[c, 1 - y], layer_ref.at[c, 1 - y], l_send.at[2], l_recv.at[2], other)

        def project(e, _):
            rows_n = normed_ref[:, :, :, :, lanes_of(e)].reshape(tokens, slice_rows)
            value = dot_tn(rows_n, raw_grad[...].reshape(tokens, 3 * HD))
            dwp[e] = value.astype(bf16).reshape(2, half, 3 * HD)
            return 0

        lax.fori_loop(0, trees, project, 0)
        sends.start(dwp.at[:, 1 - c], dwp_got, c_send.at[0], c_recv.at[0], other)
        run(r[10], r[11])

        def output(i, _):
            span = pl.ds(pl.multiple_of(i * column, column), column)
            rows_g = held[:, :, :, :, span].reshape(tokens, column)
            value = dot_tn(heads_ref[...].reshape(tokens, HD), rows_g)
            dwo[:, :, span] = value.astype(bf16).reshape(2, HD // 2, column)
            return 0

        lax.fori_loop(0, 2, output, 0)
        sends.start(dwo.at[1 - c], dwo_got, c_send.at[1], c_recv.at[1], other)
        r[12]()
        arrive(dwp_got, c_recv.at[0])
        dwp_sum[...] = (dwp[:, c].astype(f32) + dwp_got[...].astype(f32)).astype(bf16)
        arrive(dwo_got, c_recv.at[1])
        dwo_sum[...] = (dwo[c].astype(f32) + dwo_got[...].astype(f32)).astype(bf16)
        holder = z // 2
        place = lax.rem(z, 2) * 2 + x
        for e in range(trees):
            same = jnp.logical_and(here == e, c == holder)
            where = {"z": e // 2, "x": e % 2, "c": holder}
            for i in range(3):
                plain.start(
                    dwp_sum.at[e, :, pl.ds(i * HD, HD)],
                    pgrad_ref.at[i, pl.ds(pl.multiple_of(c * half, 16), half), pl.ds(pl.multiple_of(place * HD, HD), HD)],
                    w_send.at[e, i], w_recv.at[place, c, i], where, same,
                )
            plain.start(
                dwo_sum.at[:, pl.ds(e * slice_rows, slice_rows)],
                ograd_ref.at[pl.ds(pl.multiple_of(place * HD + c * (HD // 2), 16), HD // 2), :],
                w_send.at[e, 3], w_recv.at[place, c, 3], where, same,
            )

        for source in range(trees):
            arrive(sgrad_ref.at[:, pl.ds(source * sub, sub)], s_recv.at[source])

        def flip(i, _):
            span = pl.ds(pl.multiple_of(i * HD, HD), HD)
            gate_ref[:, span] = sgrad_ref[0, span, :].astype(f32).T.astype(bf16)
            up_ref[:, span] = sgrad_ref[1, span, :].astype(f32).T.astype(bf16)
            down_ref[span, :] = sgrad_ref[2, span, :]
            return 0

        lax.fori_loop(0, trees * sub // HD, flip, 0)

        total = add.total()
        value = in_ref[c, y].astype(f32)
        norm = lax.rsqrt(jnp.mean(value * value, -1, keepdims=True) + EPSILON)
        gain_part = jnp.sum(total * value * norm, 0, keepdims=True)
        scaled = total * gain_ref[...]
        ig[c, y] = (
            hg_ref[...] + norm * scaled - value * norm**3 * jnp.mean(scaled * value, -1, keepdims=True)
        ).astype(bf16)
        sends.start(ig.at[c, y], ig.at[c, y], i_send.at[0], i_recv.at[0], across)
        sends.start(ig.at[c, y], ig.at[c, y], i_send.at[1], i_recv.at[1], other)
        row = lax.broadcasted_iota(jnp.int32, (16, slice_rows), 0)
        bias = [
            jnp.concatenate([bias_sum[0:1, i * HD : (i + 1) * HD], jnp.zeros((1, slice_rows - HD), f32)], 1) for i in range(3)
        ]
        for e in range(trees):
            block = vec_ref[:, e * slice_rows : (e + 1) * slice_rows].astype(f32)
            block = jnp.where(row == lines + 2, gain_part[:, e * slice_rows : (e + 1) * slice_rows], block)
            for i in range(3):
                block = jnp.where(row == lines + 3 + i, bias[i], block)
            message[e] = block.astype(bf16)
        for i, to in enumerate(everyone):
            sends.start(message.at[to["z"] * 2 + to["x"]], got.at[z, x, y, c], m_send.at[i], m_recv.at[z, x, y, c], to)
        got[z, x, y, c] = message[here]
        arrive(ig.at[c, 1 - y], i_recv.at[0])
        sends.start(ig.at[c, 1 - y], ig.at[c, 1 - y], i_send.at[2], i_recv.at[2], other)

        for l in range(local_heads):
            for part in range(2):
                for i in range(3):
                    arrive(pgrad_ref.at[i, pl.ds(part * half, half), pl.ds(l * HD, HD)], w_recv.at[l, part, i])
                arrive(ograd_ref.at[pl.ds(l * HD + part * (HD // 2), HD // 2), :], w_recv.at[l, part, 3])
        arrive(layer_ref.at[1 - c, y], l_recv.at[1])
        arrive(layer_ref.at[1 - c, 1 - y], l_recv.at[2])
        for to in everyone:
            spot = (to["z"], to["x"], to["y"], to["c"])
            arrive(got.at[spot], m_recv.at[spot])
        small = jnp.sum(got[...].reshape(32, 16, slice_rows).astype(f32), 0)
        router_ref[...] = small[0:lines]
        vector_ref[...] = small[lines : lines + 1]
        gain2_ref[...] = small[lines + 1 : lines + 2]
        gain1_ref[...] = small[lines + 2 : lines + 3]
        source_z, source_x = 2 * c + z // 2, lax.rem(z, 2)
        both = got[source_z, source_x, y, 0].astype(f32) + got[source_z, source_x, y, 1].astype(f32)
        both = both[:, 0:HD]
        both = jnp.where(x == 1, pltpu.roll(both, HD // 2, 1), both)
        bias_ref[...] = both[lines + 3 : lines + 6, 0 : HD // 2]
        arrive(ig.at[1 - c, y], i_recv.at[1])
        arrive(ig.at[1 - c, 1 - y], i_recv.at[2])
        plain.finish()
        sends.finish()

    vmem = pl.BlockSpec(memory_space=pltpu.VMEM)
    dma = pltpu.SemaphoreType.DMA
    shape = jax.ShapeDtypeStruct
    return pl.pallas_call(
        kernel,
        name="attention_back",
        out_shape=(
            shape((2, 2, rows, width), bf16),
            shape((2, 2, rows, width), bf16),
            shape((3, slice_rows, local_heads * HD), bf16),
            shape((local_heads * HD, slice_rows), bf16),
            shape((slice_rows, trees * sub), bf16),
            shape((slice_rows, trees * sub), bf16),
            shape((trees * sub, slice_rows), bf16),
            shape((1, slice_rows), f32),
            shape((1, slice_rows), f32),
            shape((lines, slice_rows), f32),
            shape((1, slice_rows), f32),
            shape((3, HD // 2), f32),
        ),
        in_specs=[vmem] * 14,
        out_specs=(vmem,) * 12,
        scratch_shapes=[
            pltpu.VMEM((3, trees * sub, slice_rows), bf16),
            pltpu.VMEM((4, 2, 2, rows, width), bf16),
            pltpu.VMEM((4, 2, 2, rows, width), bf16),
            pltpu.VMEM((4, chunk, 3 * HD), bf16),
            pltpu.VMEM((trees, 2, half, 3 * HD), bf16),
            pltpu.VMEM((trees, half, 3 * HD), bf16),
            pltpu.VMEM((trees, half, 3 * HD), bf16),
            pltpu.VMEM((2, HD // 2, width), bf16),
            pltpu.VMEM((HD // 2, width), bf16),
            pltpu.VMEM((HD // 2, width), bf16),
            pltpu.VMEM((trees, 16, slice_rows), bf16),
            pltpu.VMEM((4, 2, 2, 2, 16, slice_rows), bf16),
            pltpu.VMEM((8, 3 * HD), f32),
            *Gather.semaphores(),
            dma((3,)),
            dma((3,)),
            dma((3,)),
            dma((3,)),
            dma((31,)),
            dma((4, 2, 2, 2)),
            dma((trees,)),
            dma((trees,)),
            dma((2,)),
            dma((2,)),
            dma((trees, 4)),
            dma((local_heads, 2, 4)),
            *Reduce.buffers(rows, width, cut),
        ],
        compiler_params=pltpu.CompilerParams(collective_id=10, has_side_effects=True, vmem_limit_bytes=VMEM_LIMIT),
    )(own_grad, normed, qkv, probs, heads, head, out_head, turns, input_rows, hidden_grad, gain, own_output, vectors, shared)


def chip_shards(
    layer_input,
    positions,
    parents,
    routes,
    route_slots,
    norm1_gain,
    project_weight,
    project_bias,
    output_weight,
    norm2_gain,
    router_weight,
    shared_vector,
    shared_gate,
    shared_up,
    shared_down,
    expert_gate,
    expert_up,
    expert_down,
    cotangent,
):
    f32, bf16 = jnp.float32, jnp.bfloat16
    micro_count, seq_rows, model_width = layer_input.shape
    top_count = routes.shape[2]
    expert_count = router_weight.shape[1]
    capacity = seq_rows * top_count * 5 // (4 * expert_count)
    z, x, y, c = [lax.axis_index(a) for a in AXES]
    here = z * 2 + x
    trees = expert_count
    tokens = trees * seq_rows
    blocks = (trees // 2, 2, 2, seq_rows // 2, model_width)
    own_rows = seq_rows // 2
    slice_rows = norm1_gain.shape[0]
    score_scale = HD ** (-0.5)

    def own(array):
        return lax.dynamic_slice(
            array, (c, y * own_rows, 0), (1, own_rows, model_width)
        )[0]

    own_input = own(layer_input)
    own_cotangent = own(cotangent)
    by_rows = (2, 2, own_rows, model_width)

    half_size = HD // 2
    inverse = ROPE_BASE ** (-(jnp.arange(half_size, dtype=f32) * 2.0 / HD))
    angles = jnp.arange(seq_rows, dtype=f32)[:, None] * inverse[None, :]
    table = jnp.concatenate([jnp.cos(angles), jnp.sin(angles)], 1)
    coarse = lax.reduce_precision(table, 8, 7)
    table = jnp.stack([coarse, table - coarse]).astype(bf16)
    (
        attention,
        normed_one,
        qkv,
        attention_probs,
        heads_out,
        head_weight,
        out_weight,
        smalls,
        turns,
        all_cotangent,
        three,
    ) = front_call(
        layer_input.reshape(by_rows),
        cotangent.reshape(by_rows),
        project_weight.transpose(1, 0, 2),
        output_weight,
        [norm1_gain[None], norm2_gain[None]],
        router_weight.T,
        shared_vector[None],
        positions,
        parents[:, 0],
        project_bias,
        table,
        shared_gate,
        shared_up,
        shared_down,
        [expert_gate[0].T, expert_up[0].T, expert_down[0]],
    )
    of_core = lax.dynamic_index_in_dim(smalls.reshape(trees, 2, -1, slice_rows), c, 1, keepdims=False)
    full = of_core[:, : expert_count + 3].transpose(1, 0, 2).reshape(expert_count + 3, model_width)
    gain_one, gain_two = full[0].astype(f32), full[1].astype(f32)
    small_weights = full[2:]
    routed_units = 2 * expert_down.shape[1]
    own_rows_in = own_input.astype(f32)
    hidden_state = own_rows_in + attention
    norm_two = lax.rsqrt(jnp.mean(hidden_state * hidden_state, -1, keepdims=True) + EPSILON)
    own_normed_two = (hidden_state * norm_two * gain_two).astype(bf16)

    first = y * own_rows
    my_routes = lax.dynamic_slice(routes, (c, first, 0), (1, own_rows, top_count))[0]
    my_slots = lax.dynamic_slice(route_slots, (c, first, 0), (1, own_rows, top_count))[0]
    logits = product_right(own_normed_two, small_weights)
    prob = jax.nn.softmax(logits[:, :expert_count], axis=-1)
    shared_scale = jax.nn.sigmoid(logits[:, expert_count:])
    onehot = (my_routes[..., None] == jnp.arange(expert_count, dtype=jnp.int32)).astype(f32)
    kept = jnp.sum(onehot * (my_slots < capacity).astype(f32)[..., None], 1)
    onehot = jnp.sum(onehot, 1)
    picked_sum = jnp.sum(onehot * prob, -1, keepdims=True)
    every_gate = onehot * prob / picked_sum
    row_scales = jnp.concatenate([every_gate * kept, shared_scale], 1)
    high = row_scales.astype(bf16)
    low = (row_scales - high.astype(f32)).astype(bf16)
    extra = jnp.concatenate(
        [
            high[:, :expert_count],
            low[:, :expert_count],
            high[:, expert_count:],
            low[:, expert_count:],
            jnp.zeros((own_rows, EXTRA - 2 * expert_count - 2), bf16),
        ],
        1,
    )
    normed_sum, ffn_out, dots, *expert_sum, shared_sum = experts_call(
        jnp.concatenate([own_normed_two, extra], 1), all_cotangent, three, routed_units
    )
    own_output = (hidden_state + ffn_out).astype(bf16)
    dots = lax.dynamic_slice(dots, (0, 0, 0, 0, first), (*dots.shape[:4], own_rows))
    dots = dots.reshape(trees, 2, 8, own_rows)
    expert_dots = (dots[:, 0, 0] + dots[:, 1, 0]).T
    shared_dot = jnp.sum(dots[:, :, 1], (0, 1))[:, None]

    kept_dots = expert_dots * kept
    picked_grad = (kept_dots - jnp.sum(kept_dots * every_gate, -1, keepdims=True)) / picked_sum
    prob_grad = picked_grad * onehot
    logit_grad = prob * (prob_grad - jnp.sum(prob * prob_grad, -1, keepdims=True))
    scale_grad = shared_dot * shared_scale * (1.0 - shared_scale)
    own_small = jnp.concatenate([logit_grad, scale_grad], 1).astype(bf16)
    grad_small = product_left(own_small, own_normed_two)
    normed_two_grad = normed_sum + product(own_small, small_weights)
    upstream = own_cotangent.astype(f32)
    grad_gain_two = jnp.sum(normed_two_grad * hidden_state * norm_two, 0)
    scaled_two = normed_two_grad * gain_two
    hidden_grad_rows = (
        upstream
        + norm_two * scaled_two
        - hidden_state * norm_two**3 * jnp.mean(scaled_two * hidden_state, -1, keepdims=True)
    )
    vectors = jnp.concatenate([grad_small, grad_gain_two[None]], 0)
    vectors = jnp.pad(vectors, ((0, -vectors.shape[0] % 16), (0, 0))).astype(bf16)
    (
        layer_output,
        input_grad,
        project_out,
        output_out,
        gate_out,
        up_out,
        down_out,
        gain_one_out,
        gain_two_out,
        router_out,
        vector_out,
        bias_out,
    ) = attention_back_call(
        hidden_grad_rows.astype(bf16),
        normed_one,
        qkv,
        attention_probs,
        heads_out,
        head_weight,
        out_weight,
        turns,
        layer_input.reshape(by_rows),
        hidden_grad_rows,
        gain_one[None],
        expert_count,
        own_output,
        vectors,
        shared_sum,
    )
    return (
        layer_output.reshape(layer_input.shape),
        input_grad.reshape(layer_input.shape).astype(f32),
        gain_one_out[0],
        project_out.astype(f32).transpose(1, 0, 2),
        bias_out,
        output_out.astype(f32),
        gain_two_out[0],
        router_out.T,
        vector_out[0],
        gate_out.astype(f32),
        up_out.astype(f32),
        down_out.astype(f32),
        expert_sum[0].astype(f32).T[None],
        expert_sum[1].astype(f32).T[None],
        expert_sum[2].astype(f32)[None],
    )


def spread(body, mesh, rows, columns):
    def named(*dims):
        names = {"expert": rows, "tensor": columns, "both": (*columns, *rows), None: None}
        return P(*(names[d] for d in dims))

    return jax.shard_map(
        body,
        mesh=mesh,
        in_specs=(
            named(None, "expert", None),
            named(None, "expert"),
            named(None, "expert", None),
            named(None, "expert", None),
            named(None, "expert", None),
            named("expert"),
            named("expert", None, "tensor"),
            named(None, "both"),
            named("tensor", "expert"),
            named("expert"),
            named("expert", None),
            named("expert"),
            named("expert", "tensor"),
            named("expert", "tensor"),
            named("tensor", "expert"),
            named("expert", None, "tensor"),
            named("expert", None, "tensor"),
            named("expert", "tensor", None),
            named(None, "expert", None),
        ),
        out_specs=(
            named(None, "expert", None),
            named(None, "expert", None),
            named("expert"),
            named("expert", None, "tensor"),
            named(None, "both"),
            named("tensor", "expert"),
            named("expert"),
            named("expert", None),
            named("expert"),
            named("expert", "tensor"),
            named("expert", "tensor"),
            named("tensor", "expert"),
            named("expert", None, "tensor"),
            named("expert", None, "tensor"),
            named("expert", "tensor", None),
        ),
        check_vma=False,
    )


def solution(mesh):
    expert_devices, tensor_devices = mesh.shape["expert"], mesh.shape["tensor"]

    def layer(*arrays):
        heads = arrays[6].shape[2] // HD
        trees = arrays[0].shape[1] // (SEG * arrays[2].shape[2])
        if (
            tensor_devices == 4
            and expert_devices % 2 == 0
            and heads == 2 * expert_devices
            and arrays[10].shape[1] == expert_devices
            and trees == expert_devices
            and arrays[0].shape[0] == 2
        ):
            grid = Mesh(mesh.devices.reshape(expert_devices // 2, 2, 2, 2), AXES)
            body = spread(chip_shards, grid, ("z", "x"), ("y", "c"))
        else:
            body = spread(gathered_shards, mesh, ("expert",), ("tensor",))
        return body(*arrays)

    return layer
```

```python
import jax
import jax.numpy as jnp
from jax import lax
from jax.experimental import pallas as pl
from jax.experimental.pallas import tpu as pltpu
from jax.sharding import Mesh, PartitionSpec as P

HD = 128
SEG = 32


EPSILON = 1e-06
ROPE_BASE = 1000000.0


def product(left_side, right_side):
    return jnp.dot(left_side, right_side, preferred_element_type=jnp.float32)


def product_left(left_side, right_side):
    return lax.dot_general(
        left_side, right_side, (((0,), (0,)), ((), ())), preferred_element_type=jnp.float32
    )


def product_right(left_side, right_side):
    return lax.dot_general(
        left_side, right_side, (((1,), (1,)), ((), ())), preferred_element_type=jnp.float32
    )


def silu_slope(inputs):
    sigmoid_value = jax.nn.sigmoid(inputs)
    return sigmoid_value * (1.0 + inputs * (1.0 - sigmoid_value))


def rope_tables(position_row, head_size):
    half_size = head_size // 2
    inverse = ROPE_BASE ** (-(jnp.arange(half_size, dtype=jnp.float32) * 2.0 / head_size))
    angles = position_row.astype(jnp.float32)[:, None] * inverse[None, :]
    cosine = jnp.cos(angles)
    sine_table = jnp.sin(angles)
    return (jnp.concatenate([cosine, cosine], 1), jnp.concatenate([sine_table, sine_table], 1))


def rotate(vectors, cosine, sine_table):
    half_size = vectors.shape[-1] // 2
    turned = jnp.concatenate([-vectors[..., half_size:], vectors[..., :half_size]], -1)
    return vectors * cosine[:, None, :] + turned * sine_table[:, None, :]


def unrotate(gradient, cosine, sine_table):
    half_size = gradient.shape[-1] // 2
    scaled = gradient * sine_table[:, None, :]
    turned = jnp.concatenate([scaled[..., half_size:], -scaled[..., :half_size]], -1)
    return gradient * cosine[:, None, :] + turned


def tree_mask(parent_row, seg_len):
    segment_count = parent_row.shape[0]
    segment_ids = jnp.arange(segment_count, dtype=jnp.int32)
    step_matrix = (
        (parent_row[:, None] == segment_ids[None, :]) & (segment_ids[:, None] > 0)
    ).astype(jnp.float32)
    identity = jnp.eye(segment_count, dtype=jnp.float32)

    def extend(loop_index, reached):
        return jnp.minimum(
            identity + jnp.dot(step_matrix, reached, precision=lax.Precision.HIGHEST), 1.0
        )

    reached = lax.fori_loop(0, segment_count, extend, identity)
    expanded = jnp.repeat(jnp.repeat(reached, seg_len, 0), seg_len, 1) > 0.5
    token_ids = jnp.arange(segment_count * seg_len, dtype=jnp.int32)
    return expanded & (token_ids[None, :] <= token_ids[:, None])


def gathered_shards(
    layer_input,
    positions,
    parents,
    routes,
    route_slots,
    norm1_gain,
    project_weight,
    project_bias,
    output_weight,
    norm2_gain,
    router_weight,
    shared_vector,
    shared_gate,
    shared_up,
    shared_down,
    expert_gate,
    expert_up,
    expert_down,
    cotangent,
):
    micro_count, seq_rows, model_width = layer_input.shape
    top_count = routes.shape[2]
    expert_count = router_weight.shape[1]
    capacity = seq_rows * top_count * 5 // (4 * expert_count)
    slot_total = expert_count * capacity
    gathered = (
        lax.all_gather(norm1_gain, "expert", axis=0, tiled=True),
        lax.all_gather(project_weight, "expert", axis=0, tiled=True),
        lax.all_gather(project_bias, "expert", axis=1, tiled=True),
        lax.all_gather(output_weight, "expert", axis=1, tiled=True),
        lax.all_gather(norm2_gain, "expert", axis=0, tiled=True),
        lax.all_gather(router_weight, "expert", axis=0, tiled=True),
        lax.all_gather(shared_vector, "expert", axis=0, tiled=True),
        lax.all_gather(shared_gate, "expert", axis=0, tiled=True),
        lax.all_gather(shared_up, "expert", axis=0, tiled=True),
        lax.all_gather(shared_down, "expert", axis=1, tiled=True),
    )
    (
        gain_first,
        project_in,
        bias_in,
        project_out,
        gain_second,
        router_full,
        vector_full,
        shared_gates,
        shared_ups,
        shared_downs,
    ) = gathered
    local_width = project_in.shape[2]
    head_count = local_width // HD
    shared_local = shared_gates.shape[1]
    project_flat = project_in.reshape(model_width, 3 * local_width)
    bias_flat = bias_in.astype(jnp.float32).reshape(3 * local_width)
    gain_one = gain_first.astype(jnp.float32)
    gain_two = gain_second.astype(jnp.float32)
    small_weights = jnp.concatenate([router_full, vector_full[:, None]], 1)
    expert_gates = expert_gate[0]
    expert_ups = expert_up[0]
    expert_downs = expert_down[0]
    score_scale = HD ** (-0.5)
    expert_ids = jnp.arange(expert_count, dtype=jnp.int32)
    pair_ids = jnp.arange(seq_rows * top_count, dtype=jnp.int32).reshape(seq_rows, top_count)
    zero_row = jnp.zeros((1, model_width), jnp.bfloat16)
    stored = []
    layer_outputs = []
    for batch_index in range(micro_count):
        input_rows = layer_input[batch_index].astype(jnp.float32)
        norm_one = lax.rsqrt(jnp.mean(input_rows * input_rows, -1, keepdims=True) + EPSILON)
        normed_one = (input_rows * norm_one * gain_one).astype(jnp.bfloat16)
        projected = (product(normed_one, project_flat) + bias_flat).reshape(
            seq_rows, 3, head_count, HD
        )
        cosine, sine_table = rope_tables(positions[batch_index], HD)
        queries = rotate(projected[:, 0], cosine, sine_table).astype(jnp.bfloat16)
        key_rows = rotate(projected[:, 1], cosine, sine_table).astype(jnp.bfloat16)
        values = projected[:, 2].astype(jnp.bfloat16)
        allowed = tree_mask(parents[batch_index, 0], SEG)
        scores = (
            jnp.einsum("qhd,khd->hqk", queries, key_rows, preferred_element_type=jnp.float32)
            * score_scale
        )
        masked = jnp.where(allowed[None], scores, -1e30)
        highest = jnp.max(masked, -1, keepdims=True)
        exponent = jnp.exp(masked - highest)
        row_total = jnp.sum(exponent, -1, keepdims=True)
        attention_probs = exponent / row_total
        log_total = highest + jnp.log(row_total)
        heads_out = (
            jnp.einsum(
                "hqk,khd->qhd",
                attention_probs.astype(jnp.bfloat16),
                values,
                preferred_element_type=jnp.float32,
            )
            .astype(jnp.bfloat16)
            .reshape(seq_rows, local_width)
        )
        attention = lax.psum(product(heads_out, project_out), "tensor")
        hidden_state = input_rows + attention
        norm_two = lax.rsqrt(jnp.mean(hidden_state * hidden_state, -1, keepdims=True) + EPSILON)
        normed_two = (hidden_state * norm_two * gain_two).astype(jnp.bfloat16)
        small_logits = product(normed_two, small_weights)
        router_prob = jax.nn.softmax(small_logits[:, :expert_count], axis=-1)
        onehot = (routes[batch_index][..., None] == expert_ids).astype(jnp.float32)
        picked = jnp.sum(onehot * router_prob[:, None, :], -1)
        picked_sum = jnp.sum(picked, -1, keepdims=True)
        route_gates = picked / picked_sum
        shared_scale = jax.nn.sigmoid(small_logits[:, expert_count])
        gate_shared = product(normed_two, shared_gates)
        up_shared = product(normed_two, shared_ups)
        hidden_shared = (jax.nn.silu(gate_shared) * up_shared).astype(jnp.bfloat16)
        shared_part = product(hidden_shared, shared_downs)
        slot_rows = route_slots[batch_index]
        valid = slot_rows < capacity
        keep_mask = valid.astype(jnp.float32)
        slot_index = routes[batch_index] * capacity + jnp.minimum(slot_rows, capacity - 1)
        safe_index = jnp.where(valid, slot_index, 0)
        target = jnp.where(valid, slot_index, slot_total).reshape(-1)
        slot_table = (
            jnp.full((slot_total,), seq_rows * top_count, jnp.int32)
            .at[target]
            .set(pair_ids.reshape(-1), mode="drop")
        )
        padded = jnp.concatenate([normed_two, zero_row], 0)
        outgoing = padded[slot_table // top_count].reshape(expert_count, capacity, model_width)
        received = lax.all_to_all(outgoing, "expert", split_axis=0, concat_axis=0, tiled=True)
        run_owner_rows = received.reshape(-1, model_width)
        run_gate_expert = product(run_owner_rows, expert_gates)
        run_up_expert = product(run_owner_rows, expert_ups)
        run_hidden_expert = (jax.nn.silu(run_gate_expert) * run_up_expert).astype(jnp.bfloat16)
        expert_rows = product(run_hidden_expert, expert_downs).reshape(
            received.shape[0], received.shape[1], model_width
        )
        returned = lax.all_to_all(expert_rows, "expert", split_axis=0, concat_axis=0, tiled=True)
        returned, received = (returned, received)
        pair_out = returned.reshape(slot_total, -1)[safe_index] * keep_mask[..., None]
        routed = jnp.sum(route_gates[..., None] * pair_out, 1)
        shared_out, routed_full = lax.psum((shared_part, routed), "tensor")
        layer_outputs.append(
            (hidden_state + shared_scale[:, None] * shared_out + routed_full).astype(jnp.bfloat16)
        )
        stored.append(
            (
                input_rows,
                norm_one,
                normed_one,
                cosine,
                sine_table,
                queries,
                key_rows,
                values,
                allowed,
                log_total,
                heads_out,
                hidden_state,
                norm_two,
                normed_two,
                router_prob,
                onehot,
                picked_sum,
                route_gates,
                shared_scale,
                gate_shared,
                up_shared,
                hidden_shared,
                shared_out,
                pair_out,
                safe_index,
                keep_mask,
                slot_table,
                received,
            )
        )
    grad_gain_one = jnp.zeros((model_width,), jnp.float32)
    grad_gain_two = jnp.zeros((model_width,), jnp.float32)
    grad_project = jnp.zeros((model_width, 3 * local_width), jnp.float32)
    grad_bias = jnp.zeros((3 * local_width,), jnp.float32)
    grad_output = jnp.zeros((local_width, model_width), jnp.float32)
    grad_small = jnp.zeros((model_width, expert_count + 1), jnp.float32)
    grad_shared_gate = jnp.zeros((model_width, shared_local), jnp.float32)
    grad_shared_up = jnp.zeros((model_width, shared_local), jnp.float32)
    grad_shared_down = jnp.zeros((shared_local, model_width), jnp.float32)
    grad_expert_gate = jnp.zeros(expert_gates.shape, jnp.float32)
    grad_expert_up = jnp.zeros(expert_ups.shape, jnp.float32)
    grad_expert_down = jnp.zeros(expert_downs.shape, jnp.float32)
    input_grads = [None] * micro_count
    for batch_index in reversed(range(micro_count)):
        (
            input_rows,
            norm_one,
            normed_one,
            cosine,
            sine_table,
            queries,
            key_rows,
            values,
            allowed,
            log_total,
            heads_out,
            hidden_state,
            norm_two,
            normed_two,
            router_prob,
            onehot,
            picked_sum,
            route_gates,
            shared_scale,
            gate_shared,
            up_shared,
            hidden_shared,
            shared_out,
            pair_out,
            safe_index,
            keep_mask,
            slot_table,
            received,
        ) = stored[batch_index]
        upstream = cotangent[batch_index].astype(jnp.float32)
        shared_grad = (shared_scale[:, None] * upstream).astype(jnp.bfloat16)
        scale_grad = jnp.sum(upstream * shared_out, -1) * shared_scale * (1.0 - shared_scale)
        gate_part = jnp.sum(upstream[:, None, :] * pair_out, -1)
        pair_grad = (
            (route_gates[..., None] * upstream[:, None, :])
            .astype(jnp.bfloat16)
            .reshape(seq_rows * top_count, model_width)
        )
        outgoing_grad = jnp.concatenate([pair_grad, zero_row], 0)[slot_table].reshape(
            expert_count, capacity, model_width
        )
        arrived = lax.all_to_all(outgoing_grad, "expert", split_axis=0, concat_axis=0, tiled=True)
        owner_rows = received.reshape(-1, model_width)
        owner_grads = arrived.reshape(-1, model_width)
        gate_expert = product(owner_rows, expert_gates)
        up_expert = product(owner_rows, expert_ups)
        active_expert = jax.nn.silu(gate_expert)
        hidden_expert = (active_expert * up_expert).astype(jnp.bfloat16)
        hidden_expert_grad = product_right(owner_grads, expert_downs)
        grad_expert_down = grad_expert_down + product_left(hidden_expert, owner_grads)
        gate_expert_grad = (hidden_expert_grad * up_expert * silu_slope(gate_expert)).astype(
            jnp.bfloat16
        )
        up_expert_grad = (hidden_expert_grad * active_expert).astype(jnp.bfloat16)
        grad_expert_gate = grad_expert_gate + product_left(owner_rows, gate_expert_grad)
        grad_expert_up = grad_expert_up + product_left(owner_rows, up_expert_grad)
        row_grad = product_right(gate_expert_grad, expert_gates) + product_right(
            up_expert_grad, expert_ups
        )
        row_back = lax.all_to_all(
            row_grad.reshape(expert_count, capacity, model_width),
            "expert",
            split_axis=0,
            concat_axis=0,
            tiled=True,
        )
        routed_back = jnp.sum(
            row_back.reshape(slot_total, model_width)[safe_index] * keep_mask[..., None], 1
        )
        hidden_shared_grad = product_right(shared_grad, shared_downs)
        grad_shared_down = grad_shared_down + product_left(hidden_shared, shared_grad)
        gate_shared_grad = (hidden_shared_grad * up_shared * silu_slope(gate_shared)).astype(
            jnp.bfloat16
        )
        up_shared_grad = (hidden_shared_grad * jax.nn.silu(gate_shared)).astype(jnp.bfloat16)
        grad_shared_gate = grad_shared_gate + product_left(normed_two, gate_shared_grad)
        grad_shared_up = grad_shared_up + product_left(normed_two, up_shared_grad)
        normed_part = (
            product_right(gate_shared_grad, shared_gates)
            + product_right(up_shared_grad, shared_ups)
            + routed_back
        )
        normed_sum, gate_grad = lax.psum((normed_part, gate_part), "tensor")
        picked_grad = (gate_grad - jnp.sum(gate_grad * route_gates, -1, keepdims=True)) / picked_sum
        prob_grad = jnp.sum(picked_grad[..., None] * onehot, 1)
        logit_grad = router_prob * (prob_grad - jnp.sum(router_prob * prob_grad, -1, keepdims=True))
        small_grad = jnp.concatenate([logit_grad, scale_grad[:, None]], 1).astype(jnp.bfloat16)
        grad_small = grad_small + product_left(normed_two, small_grad)
        normed_two_grad = normed_sum + product_right(small_grad, small_weights)
        grad_gain_two = grad_gain_two + jnp.sum(normed_two_grad * hidden_state * norm_two, 0)
        scaled_two = normed_two_grad * gain_two
        hidden_grad = (
            upstream
            + norm_two * scaled_two
            - hidden_state * norm_two**3 * jnp.mean(scaled_two * hidden_state, -1, keepdims=True)
        )
        attention_grad = hidden_grad.astype(jnp.bfloat16)
        grad_output = grad_output + product_left(heads_out, attention_grad)
        heads_grad = (
            product_right(attention_grad, project_out)
            .astype(jnp.bfloat16)
            .reshape(seq_rows, head_count, HD)
        )
        scores = (
            jnp.einsum("qhd,khd->hqk", queries, key_rows, preferred_element_type=jnp.float32)
            * score_scale
        )
        masked = jnp.where(allowed[None], scores, -1e30)
        attention_probs = jnp.exp(masked - log_total)
        value_grad = jnp.einsum(
            "hqk,qhd->khd",
            attention_probs.astype(jnp.bfloat16),
            heads_grad,
            preferred_element_type=jnp.float32,
        )
        prob_grads = jnp.einsum(
            "qhd,khd->hqk", heads_grad, values, preferred_element_type=jnp.float32
        )
        score_grad = (
            attention_probs
            * (prob_grads - jnp.sum(attention_probs * prob_grads, -1, keepdims=True))
        ).astype(jnp.bfloat16)
        query_grad = (
            jnp.einsum("hqk,khd->qhd", score_grad, key_rows, preferred_element_type=jnp.float32)
            * score_scale
        )
        key_grad = (
            jnp.einsum("hqk,qhd->khd", score_grad, queries, preferred_element_type=jnp.float32)
            * score_scale
        )
        projected_grad = (
            jnp.stack(
                [
                    unrotate(query_grad, cosine, sine_table),
                    unrotate(key_grad, cosine, sine_table),
                    value_grad,
                ],
                1,
            )
            .astype(jnp.bfloat16)
            .reshape(seq_rows, 3 * local_width)
        )
        grad_bias = grad_bias + jnp.sum(projected_grad.astype(jnp.float32), 0)
        grad_project = grad_project + product_left(normed_one, projected_grad)
        normed_one_grad = lax.psum(
            product_right(projected_grad, project_flat).astype(jnp.bfloat16), "tensor"
        ).astype(jnp.float32)
        grad_gain_one = grad_gain_one + jnp.sum(normed_one_grad * input_rows * norm_one, 0)
        scaled_one = normed_one_grad * gain_one
        input_grads[batch_index] = (
            hidden_grad
            + norm_one * scaled_one
            - input_rows * norm_one**3 * jnp.mean(scaled_one * input_rows, -1, keepdims=True)
        )
    reduced = (
        lax.psum_scatter(
            grad_gain_one.astype(jnp.bfloat16), "expert", scatter_dimension=0, tiled=True
        ).astype(jnp.float32),
        lax.psum_scatter(
            grad_project.reshape(model_width, 3, local_width).astype(jnp.bfloat16),
            "expert",
            scatter_dimension=0,
            tiled=True,
        ).astype(jnp.float32),
        lax.psum_scatter(
            grad_bias.reshape(3, local_width).astype(jnp.bfloat16),
            "expert",
            scatter_dimension=1,
            tiled=True,
        ).astype(jnp.float32),
        lax.psum_scatter(
            grad_output.astype(jnp.bfloat16), "expert", scatter_dimension=1, tiled=True
        ).astype(jnp.float32),
        lax.psum_scatter(
            grad_gain_two.astype(jnp.bfloat16), "expert", scatter_dimension=0, tiled=True
        ).astype(jnp.float32),
        lax.psum_scatter(
            grad_small[:, :expert_count].astype(jnp.bfloat16),
            "expert",
            scatter_dimension=0,
            tiled=True,
        ).astype(jnp.float32),
        lax.psum_scatter(
            grad_small[:, expert_count].astype(jnp.bfloat16),
            "expert",
            scatter_dimension=0,
            tiled=True,
        ).astype(jnp.float32),
        lax.psum_scatter(
            grad_shared_gate.astype(jnp.bfloat16), "expert", scatter_dimension=0, tiled=True
        ).astype(jnp.float32),
        lax.psum_scatter(
            grad_shared_up.astype(jnp.bfloat16), "expert", scatter_dimension=0, tiled=True
        ).astype(jnp.float32),
        lax.psum_scatter(
            grad_shared_down.astype(jnp.bfloat16), "expert", scatter_dimension=1, tiled=True
        ).astype(jnp.float32),
    )
    return (
        jnp.stack(layer_outputs),
        jnp.stack(input_grads),
        reduced[0],
        reduced[1],
        reduced[2],
        reduced[3],
        reduced[4],
        reduced[5],
        reduced[6],
        reduced[7],
        reduced[8],
        reduced[9],
        grad_expert_gate[None],
        grad_expert_up[None],
        grad_expert_down[None],
    )


AXES = ("z", "x", "y", "c")


MESH_ID = pl.DeviceIdType.MESH
VMEM_LIMIT = 60 * 1024 * 1024


def positions_here():
    return tuple(lax.axis_index(a) for a in AXES)


def planes_from(z):
    return (z, z + 1 - 2 * (z % 2), 2 - z // 2, 3 * (1 - z // 2))


def greet(barrier, partners):
    for partner in partners:
        pl.semaphore_signal(barrier, inc=1, device_id=partner, device_id_type=MESH_ID)
    pl.semaphore_wait(barrier, len(partners))


def near_partners(z, x, y):
    planes = planes_from(z)
    return [{"x": 1 - x}, {"y": 1 - y}] + [{"z": p} for p in planes[1:]]


def run(*steps):
    for step in steps:
        step()


class Sends:
    def __init__(self):
        self.open = []

    def start(self, source, target, send, receive, where, only=None):
        copy = pltpu.make_async_remote_copy(
            src_ref=source, dst_ref=target, send_sem=send, recv_sem=receive, device_id=where, device_id_type=MESH_ID
        )
        if only is None:
            copy.start()
        else:
            pl.when(only)(copy.start)
        self.open.append((copy, only))

    def finish(self):
        for copy, only in self.open:
            if only is None:
                copy.wait_send()
            else:
                pl.when(only)(copy.wait_send)
        self.open = []


def arrive(buffer, receive):
    pltpu.make_async_copy(buffer, buffer, receive).wait()


class Gather:
    ready = (5, 8, 11, 14)

    def __init__(self, held, send, receive, cut, sends, twice=False):
        self.held, self.send, self.receive, self.sends, self.twice = held, send, receive, sends, twice
        width = held.shape[-1]
        self.left, self.right = pl.ds(0, cut), pl.ds(cut, width - cut)
        self.z, self.x, self.y, _ = positions_here()
        self.planes = planes_from(self.z)
        self.inner = jnp.logical_or(self.z == 1, self.z == 2)

    def block(self, plane, x, y, columns=None):
        if columns is None:
            return self.held.at[plane, x, y]
        return self.held.at[plane, x, y, :, columns]

    def pass_on(self, plane, x, y, columns, slot, axis):
        here = self.x if axis == "x" else self.y
        ref = self.block(plane, x, y, columns)
        self.sends.start(ref, ref, self.send.at[slot, plane], self.receive.at[slot, plane], {axis: 1 - here})

    def along(self, plane, slot, to, only=None):
        ref = self.block(plane, self.x, self.y)
        self.sends.start(ref, ref, self.send.at[slot, plane], self.receive.at[6, plane], {"z": to}, only)

    def plane(self, step):
        plane = self.planes[step]
        arrive(self.block(plane, self.x, self.y), self.receive.at[6, plane])
        self.along(plane, 6, 3 - self.z if step == 1 else self.planes[1], self.inner)

    def first(self, step, part):
        plane, x, y = self.planes[step], self.x, self.y
        if part == 0:
            self.pass_on(plane, x, y, self.left, 0, "x")
            if step or not self.twice:
                self.pass_on(plane, x, y, self.right, 1, "y")
        else:
            if step or not self.twice:
                self.pass_on(plane, x, y, self.left, 2, "y")
            self.pass_on(plane, x, y, self.right, 3, "x")

    def second(self, step):
        plane, x, y = self.planes[step], self.x, self.y
        arrive(self.block(plane, 1 - x, y, self.left), self.receive.at[0, plane])
        self.pass_on(plane, 1 - x, y, self.left, 4, "y")
        if step or not self.twice:
            arrive(self.block(plane, x, 1 - y, self.right), self.receive.at[1, plane])
        self.pass_on(plane, x, 1 - y, self.right, 5, "x")

    def third(self, step):
        plane, x, y = self.planes[step], self.x, self.y
        if step or not self.twice:
            arrive(self.block(plane, x, 1 - y, self.left), self.receive.at[2, plane])
        arrive(self.block(plane, 1 - x, y, self.right), self.receive.at[3, plane])

    def fourth(self, step):
        plane, x, y = self.planes[step], self.x, self.y
        arrive(self.block(plane, 1 - x, 1 - y, self.left), self.receive.at[4, plane])
        arrive(self.block(plane, 1 - x, 1 - y, self.right), self.receive.at[5, plane])

    def steps(self):
        def begin():
            self.first(0, 0)
            self.along(self.z, 6, self.planes[1])
            self.along(self.z, 7, 3 - self.z, self.inner)
            self.first(0, 1)

        found = [begin, lambda: self.plane(1), lambda: self.second(0)]
        for step in range(4):

            def turn_over(step=step):
                if 0 < step + 2 < 4:
                    self.plane(step + 2)
                self.third(step)
                if step < 3:
                    self.first(step + 1, 0)

            def close(step=step):
                self.fourth(step)
                if step < 3:
                    self.first(step + 1, 1)

            found += [turn_over, close]
            if step < 3:
                found.append(lambda step=step: self.second(step + 1))
        return found

    @staticmethod
    def semaphores():
        return [pltpu.SemaphoreType.DMA((8, 4)), pltpu.SemaphoreType.DMA((7, 4))]


class Reduce:
    def __init__(self, parts, buffers, cut, sends):
        self.parts, self.sends = parts, sends
        self.one_left, self.one_right, self.two_left, self.two_right, self.last, self.send, self.receive = buffers
        width = parts.shape[-1]
        self.left, self.right = pl.ds(0, cut), pl.ds(cut, width - cut)
        self.z, self.x, self.y, _ = positions_here()
        self.planes = planes_from(self.z)

    @staticmethod
    def buffers(rows, width, cut):
        bf16 = jnp.bfloat16
        return [
            pltpu.VMEM((4, 2, rows, cut), bf16),
            pltpu.VMEM((4, 2, rows, width - cut), bf16),
            pltpu.VMEM((4, rows, cut), bf16),
            pltpu.VMEM((4, rows, width - cut), bf16),
            pltpu.VMEM((4, rows, width), bf16),
            pltpu.SemaphoreType.DMA((7, 4)),
            pltpu.SemaphoreType.DMA((7, 4)),
        ]

    def first(self, step, part):
        plane, x, y = self.planes[step], self.x, self.y
        its_x, its_y = (1 - x, 1 - y) if part == 0 else (x, y)
        self.sends.start(
            self.parts.at[plane, its_x, 1 - y, :, self.left], self.one_left.at[plane, part],
            self.send.at[part, plane], self.receive.at[part, plane], {"y": 1 - y},
        )
        self.sends.start(
            self.parts.at[plane, 1 - x, its_y, :, self.right], self.one_right.at[plane, part],
            self.send.at[2 + part, plane], self.receive.at[2 + part, plane], {"x": 1 - x},
        )

    def add(self, ref, other):
        ref[...] = (ref[...].astype(jnp.float32) + other[...].astype(jnp.float32)).astype(ref.dtype)

    def second(self, step):
        plane, x, y = self.planes[step], self.x, self.y
        arrive(self.one_left.at[plane, 0], self.receive.at[0, plane])
        away = self.parts.at[plane, 1 - x, y, :, self.left]
        self.add(away, self.one_left.at[plane, 0])
        self.sends.start(away, self.two_left.at[plane], self.send.at[4, plane], self.receive.at[4, plane], {"x": 1 - x})
        arrive(self.one_right.at[plane, 0], self.receive.at[2, plane])
        away = self.parts.at[plane, x, 1 - y, :, self.right]
        self.add(away, self.one_right.at[plane, 0])
        self.sends.start(away, self.two_right.at[plane], self.send.at[5, plane], self.receive.at[5, plane], {"y": 1 - y})

    def keep(self, step):
        plane, x, y = self.planes[step], self.x, self.y
        arrive(self.one_left.at[plane, 1], self.receive.at[1, plane])
        arrive(self.one_right.at[plane, 1], self.receive.at[3, plane])
        self.add(self.parts.at[plane, x, y, :, self.left], self.one_left.at[plane, 1])
        self.add(self.parts.at[plane, x, y, :, self.right], self.one_right.at[plane, 1])

    def third(self, step):
        plane, x, y = self.planes[step], self.x, self.y
        here = self.parts.at[plane, x, y]
        arrive(self.two_left.at[plane], self.receive.at[4, plane])
        arrive(self.two_right.at[plane], self.receive.at[5, plane])
        self.add(here.at[:, self.left], self.two_left.at[plane])
        self.add(here.at[:, self.right], self.two_right.at[plane])
        if step:
            self.sends.start(here, self.last.at[self.z], self.send.at[6, plane], self.receive.at[6, self.z], {"z": plane})

    def steps(self, order):
        def begin():
            self.first(order[0], 0)
            self.first(order[0], 1)

        found = [begin]
        for i in range(4):

            def keep(i=i):
                self.keep(order[i])
                if i < 3:
                    self.first(order[i + 1], 0)

            def third(i=i):
                self.third(order[i])
                if i < 3:
                    self.first(order[i + 1], 1)

            found += [lambda i=i: self.second(order[i]), keep, third]
        return found

    def total(self):
        here = self.parts[self.z, self.x, self.y].astype(jnp.float32)
        for plane in self.planes[1:]:
            arrive(self.last.at[plane], self.receive.at[6, plane])
            here = here + self.last[plane].astype(jnp.float32)
        return here


EXTRA = 128


def dot_nn(a, b):
    return lax.dot_general(a, b, (((1,), (0,)), ((), ())), preferred_element_type=jnp.float32)


def dot_nt(a, b):
    return lax.dot_general(a, b, (((1,), (1,)), ((), ())), preferred_element_type=jnp.float32)


def dot_tn(a, b):
    return lax.dot_general(a, b, (((0,), (0,)), ((), ())), preferred_element_type=jnp.float32)


def chips_but(z, x, y):
    found = []
    for dz in range(4):
        for dx in range(2):
            for dy in range(2):
                if dz or dx or dy:
                    found.append({"z": lax.rem(z + dz, 4), "x": (x + dx) % 2, "y": (y + dy) % 2})
    return found


def experts_call(own, cotangents, three, routed_units):
    bf16, f32 = jnp.bfloat16, jnp.float32
    rows, wide = own.shape
    width = wide - EXTRA
    units = three.shape[1]
    shared_units = units - routed_units
    tile = routed_units // 2
    assert shared_units == tile
    chunk = 4 * rows
    tokens = 4 * chunk
    cut = width // 2
    column = 1024
    half_tile = tile // 2
    keep = tile + half_tile

    def kernel(own_ref, cot_in, three_ref, sum_ref, out_ref, dot_ref, expert0, expert1, expert2, shared_ref, cot_ref, held, weights, hidden, gate_grad, up_grad,
               part_n, part_o, dots_mine, staged, *rest):
        (g_send, g_recv, w_sem, d_send, d_recv, free, x_send, x_recv, s_sem) = rest[:9]
        n_bufs, o_bufs = rest[9:16], rest[16:23]
        z, x, y, c = positions_here()
        here = z * 2 + x
        loads = [pltpu.make_async_copy(three_ref.at[i], weights.at[i], w_sem.at[i]) for i in range(3)]
        loads.append(pltpu.make_async_copy(cot_in, cot_ref, w_sem.at[3]))
        for load in loads:
            load.start()
        others = chips_but(z, x, y)
        greet(pltpu.get_barrier_semaphore(), others + [{"c": 1 - c}])
        held[z, x, y] = own_ref[...]
        sends = Sends()
        gather = Gather(held, g_send, g_recv, cut, sends)
        sum_n = Reduce(part_n, n_bufs, cut, sends)
        sum_o = Reduce(part_o, o_bufs, cut, sends)
        lanes = lax.broadcasted_iota(jnp.int32, (16, EXTRA), 1)
        rows_of = lax.broadcasted_iota(jnp.int32, (16, EXTRA), 0)
        pick = ((rows_of == 0) & ((lanes == here) | (lanes == here + 8))) | ((rows_of == 1) & ((lanes == 16) | (lanes == 17)))
        pick = pick.astype(f32).astype(bf16)

        def units_of(step):
            plane = gather.planes[step]
            place = pl.ds(pl.multiple_of(plane * chunk, chunk), chunk)
            rows_n = held[plane, :, :, :, 0:width].reshape(chunk, width)
            rows_c = cot_ref[plane].reshape(chunk, width)
            scales = dot_nt(pick, held[plane, :, :, :, width:wide].reshape(chunk, EXTRA))

            def one(i, _):
                span = pl.ds(pl.multiple_of(i * tile, 32), tile)
                scale = jnp.where(i == 2, scales[1:2], scales[0:1])
                gate = dot_nt(weights[0, span, :], rows_n)
                up = dot_nt(weights[1, span, :], rows_n)
                down = dot_nt(weights[2, span, :], rows_c)
                sig = 1.0 / (1.0 + jnp.exp(-gate))
                active = gate * sig
                hid = active * up
                dot = jnp.sum(hid * down, 0, keepdims=True)
                hidden[span, place] = (hid * scale).astype(bf16)
                grad = down * scale
                gate_grad[span, place] = (grad * up * (sig + active * (1.0 - sig))).astype(bf16)
                up_grad[span, place] = (grad * active).astype(bf16)
                routed, shared = lax.cond(i == 2, lambda: (jnp.zeros_like(dot), dot), lambda: (dot, jnp.zeros_like(dot)))
                return (_[0] + routed, _[1] + shared)

            zero = jnp.zeros((1, chunk), f32)
            routed, shared = lax.fori_loop(0, 3, one, (zero, zero))
            row = lax.broadcasted_iota(jnp.int32, (8, chunk), 0)
            both = jnp.where(row == 0, routed, jnp.where(row == 1, shared, 0.0))
            for t in range(2):
                dots_mine[plane, t] = both[:, t * 2 * rows : (t + 1) * 2 * rows]

        def back_of(step):
            plane = gather.planes[step]
            place = pl.ds(pl.multiple_of(plane * chunk, chunk), chunk)

            def one(i, _):
                span = pl.ds(pl.multiple_of(i * column, column), column)
                value = dot_tn(gate_grad[:, place], weights[0, :, span]) + dot_tn(up_grad[:, place], weights[1, :, span])
                part_n[plane, :, :, :, span] = value.astype(bf16).reshape(2, 2, rows, column)
                return 0

            lax.fori_loop(0, width // column, one, 0)

        def out_of(step):
            plane = gather.planes[step]
            place = pl.ds(pl.multiple_of(plane * chunk, chunk), chunk)

            def one(i, _):
                span = pl.ds(pl.multiple_of(i * column, column), column)
                value = dot_tn(hidden[:, place], weights[2, :, span])
                part_o[plane, :, :, :, span] = value.astype(bf16).reshape(2, 2, rows, column)
                return 0

            lax.fori_loop(0, width // column, one, 0)

        g, n, o = gather.steps(), sum_n.steps((0, 1, 2, 3)), sum_o.steps((0, 1, 2, 3))
        run(*g[0:4])
        for load in loads:
            load.wait()
        g[4]()
        units_of(0)
        g[5]()
        back_of(0)
        run(n[0], g[6], g[7])
        units_of(1)
        run(n[1], g[8])
        back_of(1)
        run(n[2], n[3], g[9], g[10])
        units_of(2)
        run(n[4], g[11])
        back_of(2)
        run(n[5], n[6], g[12], g[13])
        units_of(3)
        n[7]()
        back_of(3)
        n[8]()
        out_of(0)
        run(o[0], n[9])
        out_of(1)
        n[10]()
        out_of(2)
        run(o[1], n[11])
        out_of(3)
        for i, other in enumerate(others):
            sends.start(dots_mine.at[other["z"], other["x"]], dot_ref.at[z, x, y], d_send.at[i], d_recv.at[z, x, y], other)
        dot_ref[z, x, y] = dots_mine[z, x]
        pl.semaphore_signal(free, inc=1, device_id={"c": 1 - c}, device_id_type=MESH_ID)

        def gradient(kind, first, count, span):
            if kind < 2:
                side = (gate_grad, up_grad)[kind]
                return dot_nn(side[pl.ds(first, count), :], held[:, :, :, :, span].reshape(tokens, column))
            return dot_nn(hidden[pl.ds(first, count), :], cot_ref[:, :, :, :, span].reshape(tokens, column))

        def away(kind, i):
            span = pl.ds(i * column, column)
            first = pl.multiple_of((1 - c) * tile, 32)
            weights[kind, 0:tile, span] = gradient(kind, first, tile, span).astype(bf16)
            first = pl.multiple_of(routed_units + (1 - c) * half_tile, 16)
            weights[kind, tile:keep, span] = gradient(kind, first, half_tile, span).astype(bf16)

        def stay(kind, i):
            span = pl.ds(i * column, column)
            first = pl.multiple_of(c * tile, 32)
            value = gradient(kind, first, tile, span)
            staged[kind % 2, :, span] = (value + weights[kind, keep : keep + tile, span].astype(f32)).astype(bf16)
            first = pl.multiple_of(routed_units + c * half_tile, 16)
            value = gradient(kind, first, half_tile, span)
            shared_ref[kind, :, span] = (value + weights[kind, keep + tile : 2 * keep, span].astype(f32)).astype(bf16)

        def hand_over(kind):
            sends.start(weights.at[kind, 0:keep], weights.at[kind, keep : 2 * keep], x_send.at[kind], x_recv.at[kind], {"c": 1 - c})

        away(0, 0)
        run(o[2], n[12])
        away(0, 1)
        o[3]()
        pl.semaphore_wait(free, 1)
        hand_over(0)
        for kind in (1, 2):
            away(kind, 0)
            o[2 + 2 * kind]()
            away(kind, 1)
            o[3 + 2 * kind]()
            hand_over(kind)
        writes = []
        for kind in range(3):
            arrive(weights.at[kind, keep : 2 * keep], x_recv.at[kind])
            if kind > 1:
                writes[kind - 2].wait()
            stay(kind, 0)
            o[8 + 2 * kind]()
            stay(kind, 1)
            if kind < 2:
                o[9 + 2 * kind]()
            write = pltpu.make_async_copy(staged.at[kind % 2], (expert0, expert1, expert2)[kind], s_sem.at[kind])
            write.start()
            writes.append(write)
        sum_ref[...] = sum_n.total()
        out_ref[...] = sum_o.total()
        for other in others:
            arrive(dot_ref.at[other["z"], other["x"], other["y"]], d_recv.at[other["z"], other["x"], other["y"]])
        writes[1].wait()
        writes[2].wait()
        sends.finish()

    vmem = pl.BlockSpec(memory_space=pltpu.VMEM)
    anywhere = pl.BlockSpec(memory_space=pl.ANY)
    dma = pltpu.SemaphoreType.DMA
    flops = 2 * tokens * width * units * 9
    return pl.pallas_call(
        kernel,
        name="experts",
        out_shape=(
            jax.ShapeDtypeStruct((rows, width), f32),
            jax.ShapeDtypeStruct((rows, width), f32),
            jax.ShapeDtypeStruct((4, 2, 2, 8, 2 * rows), f32),
            *[jax.ShapeDtypeStruct((tile, width), bf16)] * 3,
            jax.ShapeDtypeStruct((3, half_tile, width), bf16),
        ),
        in_specs=[vmem, anywhere, anywhere],
        out_specs=(vmem, vmem, vmem, anywhere, anywhere, anywhere, vmem),
        scratch_shapes=[
            pltpu.VMEM((4, 2, 2, rows, width), bf16),
            pltpu.VMEM((4, 2, 2, rows, wide), bf16),
            pltpu.VMEM((3, units, width), bf16),
            pltpu.VMEM((units, tokens), bf16),
            pltpu.VMEM((units, tokens), bf16),
            pltpu.VMEM((units, tokens), bf16),
            pltpu.VMEM((4, 2, 2, rows, width), bf16),
            pltpu.VMEM((4, 2, 2, rows, width), bf16),
            pltpu.VMEM((4, 2, 8, 2 * rows), f32),
            pltpu.VMEM((2, tile, width), bf16),
            *Gather.semaphores(),
            dma((4,)),
            dma((15,)),
            dma((4, 2, 2)),
            pltpu.SemaphoreType.REGULAR,
            dma((3,)),
            dma((3,)),
            dma((3,)),
            *Reduce.buffers(rows, width, cut),
            *Reduce.buffers(rows, width, cut),
        ],
        compiler_params=pltpu.CompilerParams(collective_id=2, has_side_effects=True, vmem_limit_bytes=VMEM_LIMIT),
        cost_estimate=pl.CostEstimate(flops=flops, bytes_accessed=40 * 1024 * 1024, transcendentals=tokens * units),
    )(own, cotangents, three)


def plane_partners(z, x, y, c):
    found = []
    for dz in range(4):
        for dx in range(2):
            for dc in range(2):
                if dz or dx or dc:
                    found.append({"z": lax.rem(z + dz, 4), "x": (x + dx) % 2, "c": (c + dc) % 2})
    return found


class Plain:
    def __init__(self):
        self.open = []

    def start(self, source, target, send, receive, where, same):
        far = pltpu.make_async_remote_copy(
            src_ref=source, dst_ref=target, send_sem=send, recv_sem=receive, device_id=where, device_id_type=MESH_ID
        )

        @pl.when(jnp.logical_not(same))
        def _():
            far.start()

        @pl.when(same)
        def _():
            pltpu.make_async_copy(source, target, receive).start()

        self.open.append((far, same))

    def finish(self):
        for far, same in self.open:

            @pl.when(jnp.logical_not(same))
            def _(far=far):
                far.wait_send()

        self.open = []


def front_call(input_rows, cotangent, project, output, gains, router, vector, positions, parents, bias, table, gate, up, down, experts):
    bf16, f32 = jnp.bfloat16, jnp.float32
    rows, width = input_rows.shape[-2:]
    chunk = 4 * rows
    tokens = 4 * chunk
    seq = 2 * rows
    trees = tokens // seq
    slice_rows = project.shape[1]
    half = slice_rows // 2
    local_heads = project.shape[2] // HD
    sub = down.shape[0] // trees
    tile = experts[0].shape[0]
    routed = 2 * tile
    units = routed + 2 * sub
    cut = width // 2
    late_cut = 3 * width // 4
    column = width // 2
    scale = HD ** (-0.5)
    lines = router.shape[0]

    def kernel(in_ref, cot_ref, project_ref, output_ref, gain1_ref, gain2_ref, router_ref, vector_ref, position_ref, parent_ref,
               bias_ref, table_ref, gate_ref, up_ref, down_ref, e0, e1, e2,
               sum_ref, normed_out, qkv_ref, prob_ref, heads_ref, head_ref, outw_ref, smalls_ref, turns_ref, cots_out, three_ref,
               all_ref, parts, small_f, small_v, shared_v, three_v, cots_ref, normed_ref, *rest):
        (g_send, g_recv, k_send, k_recv, w_send, w_recv, v_send, v_recv, m_send, m_recv, s_send, s_recv, c_send, c_recv, l_sem, e_send,
         e_recv, o_sem, n_sem, k_sem) = rest[:20]
        z, x, y, c = positions_here()
        here = z * 2 + x
        partners = plane_partners(z, x, y, c)
        other = {"c": 1 - c}
        sends, plain = Sends(), Plain()

        small_f[...] = jnp.zeros_like(small_f)
        small_f[0:1, :] = gain1_ref[...].astype(f32)
        small_f[1:2, :] = gain2_ref[...].astype(f32)
        small_f[2 : 2 + lines, :] = router_ref[...].astype(f32)
        small_f[2 + lines : 3 + lines, :] = vector_ref[...].astype(f32)
        first = c == 0
        small_f[3 + lines : 4 + lines, 0:seq] = jnp.where(first, position_ref[0:1, :], position_ref[1:2, :]).astype(f32)
        segments = parent_ref.shape[1]
        small_f[4 + lines : 5 + lines, 0:segments] = jnp.where(first, parent_ref[0:1, :], parent_ref[1:2, :]).astype(f32)
        small_f[5 + lines : 8 + lines, 0 : bias_ref.shape[1]] = bias_ref[...].astype(f32)
        small_v[...] = small_f[...].astype(bf16)

        greet(pltpu.get_barrier_semaphore(), partners + [{"y": 1 - y}])
        all_ref[z, x, y] = in_ref[c, y]
        all_ref[z, x, 1 - y] = in_ref[c, 1 - y]
        gather = Gather(all_ref, g_send, g_recv, cut, sends, True)
        late = Gather(cots_ref, k_send, k_recv, late_cut, sends, True)
        add = Reduce(parts, rest[20:], late_cut, sends)
        a, g, r = gather.steps(), late.steps(), add.steps((3, 2, 1, 0))
        a[0]()
        for i, to in enumerate(partners):
            sends.start(small_v, smalls_ref.at[z, x, c], m_send.at[i], m_recv.at[z, x, c], to)
        smalls_ref[z, x, c] = small_v[...]
        for local in range(local_heads):
            chip = {"z": 2 * c + local // 2, "x": local % 2}
            home = jnp.logical_and(chip["z"] == z, chip["x"] == x)
            for part in range(2):
                where = {**chip, "c": part}
                same = jnp.logical_and(home, c == part)
                for i in range(3):
                    plain.start(
                        project_ref.at[i, pl.ds(part * half, half), pl.ds(local * HD, HD)],
                        head_ref.at[here, part, :, pl.ds(i * HD, HD)],
                        w_send.at[local, part, i], w_recv.at[here, i], where, same,
                    )
                plain.start(
                    output_ref.at[pl.ds(local * HD + part * HD // 2, HD // 2), :],
                    outw_ref.at[part, :, pl.ds(pl.multiple_of(here * slice_rows, slice_rows), slice_rows)],
                    w_send.at[local, part, 3], w_recv.at[here, 3], where, same,
                )
        mine = pl.ds(pl.multiple_of(c * tile, 16), tile)
        for i, ref in enumerate((e0, e1, e2)):
            sends.start(ref, three_v.at[i, mine], e_send.at[i], e_recv.at[i], other)
            pltpu.make_async_copy(ref, three_v.at[i, mine], l_sem.at[i]).start()

        def flip(i, _):
            span = pl.ds(pl.multiple_of(i * HD, HD), HD)
            shared_v[0, span, :] = gate_ref[:, span].astype(f32).T.astype(bf16)
            shared_v[1, span, :] = up_ref[:, span].astype(f32).T.astype(bf16)
            shared_v[2, span, :] = down_ref[span, :]
            return 0

        flips = down.shape[0] // HD
        for i in range(8):
            lax.fori_loop(i * flips // 8, (i + 1) * flips // 8, flip, 0)
            a[i + 1]()
        place = pl.ds(pl.multiple_of(routed + c * sub, 16), sub)
        lanes = pl.ds(pl.multiple_of(here * slice_rows, slice_rows), slice_rows)

        def share(i):
            to_z, to_x = lax.rem(z + i // 2, 4), (x + i % 2) % 2
            source = shared_v.at[:, pl.ds(pl.multiple_of((to_z * 2 + to_x) * sub, 16), sub)]
            target = three_v.at[:, place, lanes]
            if i:
                sends.start(source, target, s_send.at[i], s_recv.at[here], {"z": to_z, "x": to_x})
            else:
                pltpu.make_async_copy(source, target, s_recv.at[here]).start()

        def hand_on(i):
            from_z, from_x = lax.rem(z + 4 - i // 2, 4), (x + i % 2) % 2
            source = from_z * 2 + from_x
            span = pl.ds(pl.multiple_of(source * slice_rows, slice_rows), slice_rows)
            piece = three_v.at[:, place, span]
            arrive(piece, s_recv.at[source])
            sends.start(piece, piece, c_send.at[i], c_recv.at[source], other)

        for source in range(trees):
            for i in range(3):
                arrive(head_ref.at[source, c, :, pl.ds(i * HD, HD)], w_recv.at[source, i])
            arrive(outw_ref.at[c, :, pl.ds(source * slice_rows, slice_rows)], w_recv.at[source, 3])
        sends.start(head_ref.at[:, c], head_ref.at[:, c], v_send.at[0], v_recv.at[0], other)
        sends.start(outw_ref.at[c], outw_ref.at[c], v_send.at[1], v_recv.at[1], other)
        share(0)
        share(4)
        run(*a[9:])
        share(5)
        cots_ref[z, x, y] = cot_ref[c, y]
        cots_ref[z, x, 1 - y] = cot_ref[c, 1 - y]
        g[0]()
        for to in partners:
            spot = (to["z"], to["x"], to["c"])
            arrive(smalls_ref.at[spot], m_recv.at[spot])
        gain = jnp.concatenate([smalls_ref[e // 2, e % 2, c, 0:1, :] for e in range(trees)], 1).astype(f32)
        home_z, home_c = lax.rem(here, 4), here // 4
        width_of = bias_ref.shape[1]
        biases = [smalls_ref[home_z, e, home_c, 5 + lines : 8 + lines, 0:width_of] for e in range(2)]
        row_bias = [jnp.concatenate([b[i : i + 1].astype(f32) for b in biases], 1) for i in range(3)]
        row_bias = jnp.concatenate(row_bias, 1)
        arrive(head_ref.at[:, 1 - c], v_recv.at[0])
        arrive(outw_ref.at[1 - c], v_recv.at[1])
        query_of = lax.broadcasted_iota(jnp.int32, (seq, seq), 0)
        key_of = lax.broadcasted_iota(jnp.int32, (seq, seq), 1)
        segment_of = lax.broadcasted_iota(jnp.int32, (1, seq), 1) // SEG
        lane = lax.broadcasted_iota(jnp.int32, (seq, HD), 1)

        def attend(step):
            plane = gather.planes[step]

            def norm(i, _):
                value = all_ref[plane, i // 2, i % 2].astype(f32)
                scaled = value * lax.rsqrt(jnp.mean(value * value, -1, keepdims=True) + EPSILON) * gain
                normed_ref[plane, i // 2, i % 2] = scaled.astype(bf16)
                return 0

            lax.fori_loop(0, 4, norm, 0)
            raw = dot_nn(normed_ref[plane].reshape(chunk, width), head_ref[...].reshape(width, 3 * HD)) + row_bias
            for t in range(2):
                span = slice(t * seq, (t + 1) * seq)
                notes = smalls_ref[plane, t, c].astype(f32)
                hot = (query_of == notes[3 + lines : 4 + lines, 0:seq].astype(jnp.int32)).astype(f32).astype(bf16)
                turn = dot_tn(hot, table_ref[0]) + dot_tn(hot, table_ref[1])
                swapped = pltpu.roll(turn, HD // 2, 1)
                cos = jnp.where(lane < HD // 2, turn, swapped)
                sin = jnp.where(lane < HD // 2, -swapped, turn)
                turns_ref[0, plane, span] = cos
                turns_ref[1, plane, span] = sin
                reach = []
                for s in range(segments):
                    line = (segment_of == s).astype(f32)
                    for u in range(s):
                        line = line + (notes[4 + lines : 5 + lines, s : s + 1] == u).astype(f32) * reach[u]
                    reach.append(line)
                seen = jnp.concatenate([jnp.broadcast_to(line, (SEG, seq)) for line in reach], 0)
                allowed = jnp.logical_and(seen > 0.5, key_of <= query_of)
                turned = []
                for i in range(2):
                    value = raw[span, i * HD : (i + 1) * HD]
                    turned.append((value * cos + pltpu.roll(value, HD // 2, 1) * sin).astype(bf16))
                turned.append(raw[span, 2 * HD :].astype(bf16))
                for i in range(3):
                    qkv_ref[i, plane, span] = turned[i]
                score = jnp.where(allowed, dot_nt(turned[0], turned[1]) * scale, -1e30)
                exponent = jnp.exp(score - jnp.max(score, -1, keepdims=True))
                prob = exponent / jnp.sum(exponent, -1, keepdims=True)
                prob_ref[plane, t] = prob
                heads_ref[plane, span] = dot_nn(prob.astype(bf16), turned[2]).astype(bf16)

            def spread_out(i, _):
                span = pl.ds(pl.multiple_of(i * column, column), column)
                value = dot_nn(heads_ref[plane], outw_ref[:, :, span].reshape(HD, column))
                parts[plane, :, :, :, span] = value.astype(bf16).reshape(2, 2, rows, column)
                return 0

            lax.fori_loop(0, width // column, spread_out, 0)
            copy = pltpu.make_async_copy(normed_ref.at[plane], normed_out.at[plane], n_sem.at[step])
            copy.start()
            saved.append(copy)

        def save(step):
            plane = gather.planes[step]
            copy = pltpu.make_async_copy(cots_ref.at[plane], cots_out.at[plane], k_sem.at[step])
            copy.start()
            saved.append(copy)

        saved = []

        attend(3)
        run(r[0], g[1], g[2])
        share(6)
        attend(2)
        run(r[1], r[2], g[3])
        share(7)
        hand_on(0)
        hand_on(4)
        run(r[3], g[4])
        save(0)
        attend(1)
        share(2)
        run(r[4], r[5], g[5])
        hand_on(5)
        share(3)
        run(r[6], g[6])
        hand_on(6)
        attend(0)
        share(1)
        for i in range(3):
            arrive(three_v.at[i, mine], l_sem.at[i])
            arrive(three_v.at[i, pl.ds(pl.multiple_of((1 - c) * tile, 16), tile)], e_recv.at[i])
        early = pltpu.make_async_copy(three_v.at[:, pl.ds(0, routed)], three_ref.at[:, pl.ds(0, routed)], o_sem.at[0])
        early.start()
        run(r[7], r[8], g[7])
        save(1)
        hand_on(7)
        run(r[9], g[8])
        hand_on(2)
        run(r[10], g[9], r[11], g[10])
        save(2)
        hand_on(3)
        run(r[12], g[11], g[12])
        hand_on(1)
        sum_ref[...] = add.total()
        g[13]()
        save(3)
        theirs = pl.ds(pl.multiple_of(routed + (1 - c) * sub, 16), sub)
        for source in range(trees):
            arrive(three_v.at[:, theirs, pl.ds(source * slice_rows, slice_rows)], c_recv.at[source])
        rest_of = pltpu.make_async_copy(
            three_v.at[:, pl.ds(routed, units - routed)], three_ref.at[:, pl.ds(routed, units - routed)], o_sem.at[1]
        )
        rest_of.start()
        for copy in saved:
            copy.wait()
        early.wait()
        rest_of.wait()
        plain.finish()
        sends.finish()

    vmem = pl.BlockSpec(memory_space=pltpu.VMEM)
    anywhere = pl.BlockSpec(memory_space=pl.ANY)
    dma = pltpu.SemaphoreType.DMA
    shape = jax.ShapeDtypeStruct
    return pl.pallas_call(
        kernel,
        name="front",
        out_shape=(
            shape((rows, width), f32),
            shape((4, 2, 2, rows, width), bf16),
            shape((3, 4, chunk, HD), bf16),
            shape((4, 2, seq, seq), f32),
            shape((4, chunk, HD), bf16),
            shape((trees, 2, half, 3 * HD), bf16),
            shape((2, HD // 2, width), bf16),
            shape((4, 2, 2, 16, slice_rows), bf16),
            shape((2, 4, chunk, HD), f32),
            shape((4, 2, 2, rows, width), bf16),
            shape((3, units, width), bf16),
        ),
        in_specs=[vmem] * 18,
        out_specs=(vmem, anywhere) + (vmem,) * 7 + (anywhere,) * 2,
        scratch_shapes=[
            pltpu.VMEM((4, 2, 2, rows, width), bf16),
            pltpu.VMEM((4, 2, 2, rows, width), bf16),
            pltpu.VMEM((16, slice_rows), f32),
            pltpu.VMEM((16, slice_rows), bf16),
            pltpu.VMEM((3, *down.shape), bf16),
            pltpu.VMEM((3, units, width), bf16),
            pltpu.VMEM((4, 2, 2, rows, width), bf16),
            pltpu.VMEM((4, 2, 2, rows, width), bf16),
            *Gather.semaphores(),
            *Gather.semaphores(),
            dma((local_heads, 2, 4)),
            dma((trees, 4)),
            dma((2,)),
            dma((2,)),
            dma((15,)),
            dma((4, 2, 2)),
            dma((trees,)),
            dma((trees,)),
            dma((trees,)),
            dma((trees,)),
            dma((3,)),
            dma((3,)),
            dma((3,)),
            dma((2,)),
            dma((4,)),
            dma((4,)),
            *Reduce.buffers(rows, width, late_cut),
        ],
        compiler_params=pltpu.CompilerParams(collective_id=8, has_side_effects=True, vmem_limit_bytes=VMEM_LIMIT),
    )(input_rows, cotangent, project, output, *gains, router, vector, positions, parents, bias, table, gate, up, down, *experts)


def all_but(z, x, y, c):
    found = []
    for dz in range(4):
        for dx in range(2):
            for dy in range(2):
                for dc in range(2):
                    if dz or dx or dy or dc:
                        found.append(
                            {"z": lax.rem(z + dz, 4), "x": (x + dx) % 2, "y": (y + dy) % 2, "c": (c + dc) % 2}
                        )
    return found


def attention_back_call(own_grad, normed, qkv, probs, heads, head, out_head, turns, input_rows, hidden_grad, gain, lines,
                        own_output, vectors, shared):
    bf16, f32 = jnp.bfloat16, jnp.float32
    rows, width = own_grad.shape
    chunk = 4 * rows
    tokens = 4 * chunk
    seq = 2 * rows
    trees, _, half, _ = head.shape
    slice_rows = 2 * half
    sub = shared.shape[1]
    cut = 3 * width // 4
    column = width // 2
    scale = HD ** (-0.5)
    local_heads = trees // 2

    def kernel(grad_ref, normed_in, qkv_ref, prob_ref, heads_ref, head_ref, outw_ref, turns_ref, in_ref, hg_ref, gain_ref,
               result_ref, vec_ref, shared_ref,
               layer_ref, ig, pgrad_ref, ograd_ref, gate_ref, up_ref, down_ref, gain1_ref, gain2_ref, router_ref, vector_ref, bias_ref,
               sgrad_ref, normed_ref,               held, parts, raw_grad, dwp, dwp_got, dwp_sum, dwo, dwo_got, dwo_sum, message, got, bias_sum, *rest):
        (g_send, g_recv, l_send, l_recv, i_send, i_recv, m_send, m_recv, s_send, s_recv, c_send, c_recv, w_send,
         w_recv, n_sem) = rest[:15]
        z, x, y, c = positions_here()
        here = z * 2 + x
        everyone = all_but(z, x, y, c)
        load = pltpu.make_async_copy(normed_in, normed_ref, n_sem)
        load.start()
        greet(pltpu.get_barrier_semaphore(), everyone)
        sends = Sends()
        plain = Plain()
        other, across = {"c": 1 - c}, {"y": 1 - y}
        held[z, x, y] = grad_ref[...]
        gather = Gather(held, g_send, g_recv, cut, sends)
        add = Reduce(parts, rest[15:], cut, sends)
        g, r = gather.steps(), add.steps((0, 1, 2, 3))
        g[0]()
        layer_ref[c, y] = result_ref[...]
        sends.start(layer_ref.at[c, y], layer_ref.at[c, y], l_send.at[0], l_recv.at[0], across)
        sends.start(layer_ref.at[c, y], layer_ref.at[c, y], l_send.at[1], l_recv.at[1], other)

        def lanes_of(e):
            return pl.ds(pl.multiple_of(e * slice_rows, slice_rows), slice_rows)

        bias_sum[...] = jnp.zeros_like(bias_sum)

        def attend(step):
            plane = gather.planes[step]
            grads = dot_nt(held[plane].reshape(chunk, width), outw_ref[...].reshape(HD, width)).astype(bf16)
            cos, sin = turns_ref[0, plane], turns_ref[1, plane]
            for t in range(2):
                span = slice(t * seq, (t + 1) * seq)
                prob = prob_ref[plane, t]
                out_grad = grads[span]
                query, key, value = (qkv_ref[i, plane, span] for i in range(3))
                value_grad = dot_tn(prob.astype(bf16), out_grad)
                prob_grad = dot_nt(out_grad, value)
                score_grad = (prob * (prob_grad - jnp.sum(prob * prob_grad, -1, keepdims=True))).astype(bf16)
                sides = [dot_nn(score_grad, key) * scale, dot_tn(score_grad, query) * scale]
                sides = [s * cos[span] - pltpu.roll(s, HD // 2, 1) * sin[span] for s in sides] + [value_grad]
                for i in range(3):
                    side = sides[i].astype(bf16)
                    raw_grad[plane, span, i * HD : (i + 1) * HD] = side
                    bias_sum[0:1, i * HD : (i + 1) * HD] += jnp.sum(side.astype(f32), 0, keepdims=True)

            def back(i, _):
                span = pl.ds(pl.multiple_of(i * column, column), column)
                weight = head_ref[pl.ds(i * (trees // 2), trees // 2)].reshape(column, 3 * HD)
                parts[plane, :, :, :, span] = dot_nt(raw_grad[plane], weight).astype(bf16).reshape(2, 2, rows, column)
                return 0

            lax.fori_loop(0, 2, back, 0)

        def share(i):
            to_z, to_x = lax.rem(z + i // 2, 4), (x + i % 2) % 2
            source = shared_ref.at[:, :, lanes_of(to_z * 2 + to_x)]
            target = sgrad_ref.at[:, pl.ds(pl.multiple_of(here * sub, 16), sub)]
            if i:
                sends.start(source, target, s_send.at[i], s_recv.at[here], {"z": to_z, "x": to_x})
            else:
                pltpu.make_async_copy(source, target, s_recv.at[here]).start()

        share(0)
        share(4)
        run(*g[1:3])
        share(5)
        run(*g[3:5])
        attend(0)
        run(g[5], r[0], g[6], g[7])
        share(6)
        attend(1)
        run(r[1], g[8], r[2], r[3])
        share(7)
        run(g[9], g[10])
        attend(2)
        share(2)
        run(r[4], g[11], r[5])
        share(3)
        run(r[6], g[12], g[13])
        share(1)
        attend(3)
        run(r[7], r[8], r[9])
        arrive(layer_ref.at[c, 1 - y], l_recv.at[0])
        sends.start(layer_ref.at[c, 1 - y], layer_ref.at[c, 1 - y], l_send.at[2], l_recv.at[2], other)

        def project(e, _):
            rows_n = normed_ref[:, :, :, :, lanes_of(e)].reshape(tokens, slice_rows)
            value = dot_tn(rows_n, raw_grad[...].reshape(tokens, 3 * HD))
            dwp[e] = value.astype(bf16).reshape(2, half, 3 * HD)
            return 0

        load.wait()
        lax.fori_loop(0, trees, project, 0)
        sends.start(dwp.at[:, 1 - c], dwp_got, c_send.at[0], c_recv.at[0], other)
        run(r[10], r[11])

        def output(i, _):
            span = pl.ds(pl.multiple_of(i * column, column), column)
            rows_g = held[:, :, :, :, span].reshape(tokens, column)
            value = dot_tn(heads_ref[...].reshape(tokens, HD), rows_g)
            dwo[:, :, span] = value.astype(bf16).reshape(2, HD // 2, column)
            return 0

        lax.fori_loop(0, 2, output, 0)
        sends.start(dwo.at[1 - c], dwo_got, c_send.at[1], c_recv.at[1], other)
        r[12]()
        arrive(dwp_got, c_recv.at[0])
        dwp_sum[...] = (dwp[:, c].astype(f32) + dwp_got[...].astype(f32)).astype(bf16)
        arrive(dwo_got, c_recv.at[1])
        dwo_sum[...] = (dwo[c].astype(f32) + dwo_got[...].astype(f32)).astype(bf16)
        holder = z // 2
        place = lax.rem(z, 2) * 2 + x
        for e in range(trees):
            same = jnp.logical_and(here == e, c == holder)
            where = {"z": e // 2, "x": e % 2, "c": holder}
            for i in range(3):
                plain.start(
                    dwp_sum.at[e, :, pl.ds(i * HD, HD)],
                    pgrad_ref.at[i, pl.ds(pl.multiple_of(c * half, 16), half), pl.ds(pl.multiple_of(place * HD, HD), HD)],
                    w_send.at[e, i], w_recv.at[place, c, i], where, same,
                )
            plain.start(
                dwo_sum.at[:, pl.ds(e * slice_rows, slice_rows)],
                ograd_ref.at[pl.ds(pl.multiple_of(place * HD + c * (HD // 2), 16), HD // 2), :],
                w_send.at[e, 3], w_recv.at[place, c, 3], where, same,
            )

        total = add.total()
        value = in_ref[c, y].astype(f32)
        norm = lax.rsqrt(jnp.mean(value * value, -1, keepdims=True) + EPSILON)
        gain_part = jnp.sum(total * value * norm, 0, keepdims=True)
        scaled = total * gain_ref[...]
        ig[c, y] = (
            hg_ref[...] + norm * scaled - value * norm**3 * jnp.mean(scaled * value, -1, keepdims=True)
        ).astype(bf16)
        sends.start(ig.at[c, y], ig.at[c, y], i_send.at[0], i_recv.at[0], across)
        sends.start(ig.at[c, y], ig.at[c, y], i_send.at[1], i_recv.at[1], other)
        row = lax.broadcasted_iota(jnp.int32, (16, slice_rows), 0)
        bias = [
            jnp.concatenate([bias_sum[0:1, i * HD : (i + 1) * HD], jnp.zeros((1, slice_rows - HD), f32)], 1) for i in range(3)
        ]
        for e in range(trees):
            block = vec_ref[:, e * slice_rows : (e + 1) * slice_rows].astype(f32)
            block = jnp.where(row == lines + 2, gain_part[:, e * slice_rows : (e + 1) * slice_rows], block)
            for i in range(3):
                block = jnp.where(row == lines + 3 + i, bias[i], block)
            message[e] = block.astype(bf16)
        for i, to in enumerate(everyone):
            sends.start(message.at[to["z"] * 2 + to["x"]], got.at[z, x, y, c], m_send.at[i], m_recv.at[z, x, y, c], to)
        got[z, x, y, c] = message[here]
        for source in range(trees):
            arrive(sgrad_ref.at[:, pl.ds(source * sub, sub)], s_recv.at[source])

        def flip(i, _):
            span = pl.ds(pl.multiple_of(i * HD, HD), HD)
            gate_ref[:, span] = sgrad_ref[0, span, :].astype(f32).T.astype(bf16)
            up_ref[:, span] = sgrad_ref[1, span, :].astype(f32).T.astype(bf16)
            down_ref[span, :] = sgrad_ref[2, span, :]
            return 0

        lax.fori_loop(0, trees * sub // HD, flip, 0)
        arrive(ig.at[c, 1 - y], i_recv.at[0])
        sends.start(ig.at[c, 1 - y], ig.at[c, 1 - y], i_send.at[2], i_recv.at[2], other)

        for l in range(local_heads):
            for part in range(2):
                for i in range(3):
                    arrive(pgrad_ref.at[i, pl.ds(part * half, half), pl.ds(l * HD, HD)], w_recv.at[l, part, i])
                arrive(ograd_ref.at[pl.ds(l * HD + part * (HD // 2), HD // 2), :], w_recv.at[l, part, 3])
        arrive(layer_ref.at[1 - c, y], l_recv.at[1])
        arrive(layer_ref.at[1 - c, 1 - y], l_recv.at[2])
        for to in everyone:
            spot = (to["z"], to["x"], to["y"], to["c"])
            arrive(got.at[spot], m_recv.at[spot])
        small = jnp.sum(got[...].reshape(32, 16, slice_rows).astype(f32), 0)
        router_ref[...] = small[0:lines]
        vector_ref[...] = small[lines : lines + 1]
        gain2_ref[...] = small[lines + 1 : lines + 2]
        gain1_ref[...] = small[lines + 2 : lines + 3]
        source_z, source_x = 2 * c + z // 2, lax.rem(z, 2)
        both = got[source_z, source_x, y, 0].astype(f32) + got[source_z, source_x, y, 1].astype(f32)
        both = both[:, 0:HD]
        both = jnp.where(x == 1, pltpu.roll(both, HD // 2, 1), both)
        bias_ref[...] = both[lines + 3 : lines + 6, 0 : HD // 2]
        arrive(ig.at[1 - c, y], i_recv.at[1])
        arrive(ig.at[1 - c, 1 - y], i_recv.at[2])
        plain.finish()
        sends.finish()

    vmem = pl.BlockSpec(memory_space=pltpu.VMEM)
    dma = pltpu.SemaphoreType.DMA
    shape = jax.ShapeDtypeStruct
    return pl.pallas_call(
        kernel,
        name="attention_back",
        out_shape=(
            shape((2, 2, rows, width), bf16),
            shape((2, 2, rows, width), bf16),
            shape((3, slice_rows, local_heads * HD), bf16),
            shape((local_heads * HD, slice_rows), bf16),
            shape((slice_rows, trees * sub), bf16),
            shape((slice_rows, trees * sub), bf16),
            shape((trees * sub, slice_rows), bf16),
            shape((1, slice_rows), f32),
            shape((1, slice_rows), f32),
            shape((lines, slice_rows), f32),
            shape((1, slice_rows), f32),
            shape((3, HD // 2), f32),
        ),
        in_specs=[vmem, pl.BlockSpec(memory_space=pl.ANY)] + [vmem] * 12,
        out_specs=(vmem,) * 12,
        scratch_shapes=[
            pltpu.VMEM((3, trees * sub, slice_rows), bf16),
            pltpu.VMEM((4, 2, 2, rows, width), bf16),
            pltpu.VMEM((4, 2, 2, rows, width), bf16),
            pltpu.VMEM((4, 2, 2, rows, width), bf16),
            pltpu.VMEM((4, chunk, 3 * HD), bf16),
            pltpu.VMEM((trees, 2, half, 3 * HD), bf16),
            pltpu.VMEM((trees, half, 3 * HD), bf16),
            pltpu.VMEM((trees, half, 3 * HD), bf16),
            pltpu.VMEM((2, HD // 2, width), bf16),
            pltpu.VMEM((HD // 2, width), bf16),
            pltpu.VMEM((HD // 2, width), bf16),
            pltpu.VMEM((trees, 16, slice_rows), bf16),
            pltpu.VMEM((4, 2, 2, 2, 16, slice_rows), bf16),
            pltpu.VMEM((8, 3 * HD), f32),
            *Gather.semaphores(),
            dma((3,)),
            dma((3,)),
            dma((3,)),
            dma((3,)),
            dma((31,)),
            dma((4, 2, 2, 2)),
            dma((trees,)),
            dma((trees,)),
            dma((2,)),
            dma((2,)),
            dma((trees, 4)),
            dma((local_heads, 2, 4)),
            dma,
            *Reduce.buffers(rows, width, cut),
        ],
        compiler_params=pltpu.CompilerParams(collective_id=10, has_side_effects=True, vmem_limit_bytes=VMEM_LIMIT),
    )(own_grad, normed, qkv, probs, heads, head, out_head, turns, input_rows, hidden_grad, gain, own_output, vectors, shared)


def finish_call(arrays, kinds):
    count = len(arrays)

    def kernel(*refs):
        sources, targets = refs[:count], refs[count : 2 * count]
        narrow, wide = refs[2 * count : 3 * count], refs[3 * count : 4 * count]
        in_sem, out_sem = refs[4 * count :]
        reads = [pltpu.make_async_copy(sources[i], narrow[i], in_sem.at[i]) for i in range(count)]
        for read in reads:
            read.start()
        writes = []
        for i in range(count):
            reads[i].wait()
            wide[i][...] = narrow[i][...].astype(kinds[i])
            write = pltpu.make_async_copy(wide[i], targets[i], out_sem.at[i])
            write.start()
            writes.append(write)
        for write in writes:
            write.wait()

    anywhere = pl.BlockSpec(memory_space=pl.ANY)
    return pl.pallas_call(
        kernel,
        name="finish",
        out_shape=tuple(jax.ShapeDtypeStruct(a.shape, kind) for a, kind in zip(arrays, kinds)),
        in_specs=[anywhere] * count,
        out_specs=(anywhere,) * count,
        scratch_shapes=[
            *[pltpu.VMEM(a.shape, a.dtype) for a in arrays],
            *[pltpu.VMEM(a.shape, kind) for a, kind in zip(arrays, kinds)],
            pltpu.SemaphoreType.DMA((count,)),
            pltpu.SemaphoreType.DMA((count,)),
        ],
        compiler_params=pltpu.CompilerParams(vmem_limit_bytes=VMEM_LIMIT),
    )(*arrays)


def chip_shards(
    layer_input,
    positions,
    parents,
    routes,
    route_slots,
    norm1_gain,
    project_weight,
    project_bias,
    output_weight,
    norm2_gain,
    router_weight,
    shared_vector,
    shared_gate,
    shared_up,
    shared_down,
    expert_gate,
    expert_up,
    expert_down,
    cotangent,
):
    f32, bf16 = jnp.float32, jnp.bfloat16
    micro_count, seq_rows, model_width = layer_input.shape
    top_count = routes.shape[2]
    expert_count = router_weight.shape[1]
    capacity = seq_rows * top_count * 5 // (4 * expert_count)
    z, x, y, c = [lax.axis_index(a) for a in AXES]
    here = z * 2 + x
    trees = expert_count
    tokens = trees * seq_rows
    blocks = (trees // 2, 2, 2, seq_rows // 2, model_width)
    own_rows = seq_rows // 2
    slice_rows = norm1_gain.shape[0]
    score_scale = HD ** (-0.5)

    def own(array):
        return lax.dynamic_slice(
            array, (c, y * own_rows, 0), (1, own_rows, model_width)
        )[0]

    own_input = own(layer_input)
    own_cotangent = own(cotangent)
    by_rows = (2, 2, own_rows, model_width)

    half_size = HD // 2
    inverse = ROPE_BASE ** (-(jnp.arange(half_size, dtype=f32) * 2.0 / HD))
    angles = jnp.arange(seq_rows, dtype=f32)[:, None] * inverse[None, :]
    table = jnp.concatenate([jnp.cos(angles), jnp.sin(angles)], 1)
    coarse = lax.reduce_precision(table, 8, 7)
    table = jnp.stack([coarse, table - coarse]).astype(bf16)
    (
        attention,
        normed_one,
        qkv,
        attention_probs,
        heads_out,
        head_weight,
        out_weight,
        smalls,
        turns,
        all_cotangent,
        three,
    ) = front_call(
        layer_input.reshape(by_rows),
        cotangent.reshape(by_rows),
        project_weight.transpose(1, 0, 2),
        output_weight,
        [norm1_gain[None], norm2_gain[None]],
        router_weight.T,
        shared_vector[None],
        positions,
        parents[:, 0],
        project_bias,
        table,
        shared_gate,
        shared_up,
        shared_down,
        [expert_gate[0].T, expert_up[0].T, expert_down[0]],
    )
    of_core = lax.dynamic_index_in_dim(smalls.reshape(trees, 2, -1, slice_rows), c, 1, keepdims=False)
    full = of_core[:, : expert_count + 3].transpose(1, 0, 2).reshape(expert_count + 3, model_width)
    gain_one, gain_two = full[0].astype(f32), full[1].astype(f32)
    small_weights = full[2:]
    routed_units = 2 * expert_down.shape[1]
    own_rows_in = own_input.astype(f32)
    hidden_state = own_rows_in + attention
    norm_two = lax.rsqrt(jnp.mean(hidden_state * hidden_state, -1, keepdims=True) + EPSILON)
    own_normed_two = (hidden_state * norm_two * gain_two).astype(bf16)

    first = y * own_rows
    my_routes = lax.dynamic_slice(routes, (c, first, 0), (1, own_rows, top_count))[0]
    my_slots = lax.dynamic_slice(route_slots, (c, first, 0), (1, own_rows, top_count))[0]
    logits = product_right(own_normed_two, small_weights)
    prob = jax.nn.softmax(logits[:, :expert_count], axis=-1)
    shared_scale = jax.nn.sigmoid(logits[:, expert_count:])
    onehot = (my_routes[..., None] == jnp.arange(expert_count, dtype=jnp.int32)).astype(f32)
    kept = jnp.sum(onehot * (my_slots < capacity).astype(f32)[..., None], 1)
    onehot = jnp.sum(onehot, 1)
    picked_sum = jnp.sum(onehot * prob, -1, keepdims=True)
    every_gate = onehot * prob / picked_sum
    row_scales = jnp.concatenate([every_gate * kept, shared_scale], 1)
    high = row_scales.astype(bf16)
    low = (row_scales - high.astype(f32)).astype(bf16)
    extra = jnp.concatenate(
        [
            high[:, :expert_count],
            low[:, :expert_count],
            high[:, expert_count:],
            low[:, expert_count:],
            jnp.zeros((own_rows, EXTRA - 2 * expert_count - 2), bf16),
        ],
        1,
    )
    normed_sum, ffn_out, dots, *expert_sum, shared_sum = experts_call(
        jnp.concatenate([own_normed_two, extra], 1), all_cotangent, three, routed_units
    )
    own_output = (hidden_state + ffn_out).astype(bf16)
    dots = lax.dynamic_slice(dots, (0, 0, 0, 0, first), (*dots.shape[:4], own_rows))
    dots = dots.reshape(trees, 2, 8, own_rows)
    expert_dots = (dots[:, 0, 0] + dots[:, 1, 0]).T
    shared_dot = jnp.sum(dots[:, :, 1], (0, 1))[:, None]

    kept_dots = expert_dots * kept
    picked_grad = (kept_dots - jnp.sum(kept_dots * every_gate, -1, keepdims=True)) / picked_sum
    prob_grad = picked_grad * onehot
    logit_grad = prob * (prob_grad - jnp.sum(prob * prob_grad, -1, keepdims=True))
    scale_grad = shared_dot * shared_scale * (1.0 - shared_scale)
    own_small = jnp.concatenate([logit_grad, scale_grad], 1).astype(bf16)
    grad_small = product_left(own_small, own_normed_two)
    normed_two_grad = normed_sum + product(own_small, small_weights)
    upstream = own_cotangent.astype(f32)
    grad_gain_two = jnp.sum(normed_two_grad * hidden_state * norm_two, 0)
    scaled_two = normed_two_grad * gain_two
    hidden_grad_rows = (
        upstream
        + norm_two * scaled_two
        - hidden_state * norm_two**3 * jnp.mean(scaled_two * hidden_state, -1, keepdims=True)
    )
    vectors = jnp.concatenate([grad_small, grad_gain_two[None]], 0)
    vectors = jnp.pad(vectors, ((0, -vectors.shape[0] % 16), (0, 0))).astype(bf16)
    (
        layer_output,
        input_grad,
        project_out,
        output_out,
        gate_out,
        up_out,
        down_out,
        gain_one_out,
        gain_two_out,
        router_out,
        vector_out,
        bias_out,
    ) = attention_back_call(
        hidden_grad_rows.astype(bf16),
        normed_one,
        qkv,
        attention_probs,
        heads_out,
        head_weight,
        out_weight,
        turns,
        layer_input.reshape(by_rows),
        hidden_grad_rows,
        gain_one[None],
        expert_count,
        own_output,
        vectors,
        shared_sum,
    )
    (
        expert_gate_out,
        expert_up_out,
        expert_down_out,
        gate_out,
        up_out,
        down_out,
        project_out,
        output_out,
        input_grad,
        layer_output,
        gain_one_out,
        gain_two_out,
        router_out,
        vector_out,
        bias_out,
    ) = finish_call(
        [
            *expert_sum,
            gate_out,
            up_out,
            down_out,
            project_out,
            output_out,
            input_grad,
            layer_output,
            gain_one_out,
            gain_two_out,
            router_out,
            vector_out,
            bias_out,
        ],
        [f32] * 9 + [bf16] + [f32] * 5,
    )
    return (
        layer_output.reshape(layer_input.shape),
        input_grad.reshape(layer_input.shape),
        gain_one_out[0],
        project_out.transpose(1, 0, 2),
        bias_out,
        output_out,
        gain_two_out[0],
        router_out.T,
        vector_out[0],
        gate_out,
        up_out,
        down_out,
        expert_gate_out.T[None],
        expert_up_out.T[None],
        expert_down_out[None],
    )


def spread(body, mesh, rows, columns):
    def named(*dims):
        names = {"expert": rows, "tensor": columns, "both": (*columns, *rows), None: None}
        return P(*(names[d] for d in dims))

    return jax.shard_map(
        body,
        mesh=mesh,
        in_specs=(
            named(None, "expert", None),
            named(None, "expert"),
            named(None, "expert", None),
            named(None, "expert", None),
            named(None, "expert", None),
            named("expert"),
            named("expert", None, "tensor"),
            named(None, "both"),
            named("tensor", "expert"),
            named("expert"),
            named("expert", None),
            named("expert"),
            named("expert", "tensor"),
            named("expert", "tensor"),
            named("tensor", "expert"),
            named("expert", None, "tensor"),
            named("expert", None, "tensor"),
            named("expert", "tensor", None),
            named(None, "expert", None),
        ),
        out_specs=(
            named(None, "expert", None),
            named(None, "expert", None),
            named("expert"),
            named("expert", None, "tensor"),
            named(None, "both"),
            named("tensor", "expert"),
            named("expert"),
            named("expert", None),
            named("expert"),
            named("expert", "tensor"),
            named("expert", "tensor"),
            named("tensor", "expert"),
            named("expert", None, "tensor"),
            named("expert", None, "tensor"),
            named("expert", "tensor", None),
        ),
        check_vma=False,
    )


def solution(mesh):
    expert_devices, tensor_devices = mesh.shape["expert"], mesh.shape["tensor"]

    def layer(*arrays):
        heads = arrays[6].shape[2] // HD
        trees = arrays[0].shape[1] // (SEG * arrays[2].shape[2])
        if (
            tensor_devices == 4
            and expert_devices % 2 == 0
            and heads == 2 * expert_devices
            and arrays[10].shape[1] == expert_devices
            and trees == expert_devices
            and arrays[0].shape[0] == 2
        ):
            grid = Mesh(mesh.devices.reshape(expert_devices // 2, 2, 2, 2), AXES)
            body = spread(chip_shards, grid, ("z", "x"), ("y", "c"))
        else:
            body = spread(gathered_shards, mesh, ("expert",), ("tensor",))
        return body(*arrays)

    return layer
```

```python
import jax
import jax.numpy as jnp
from jax import lax
from jax.experimental import pallas as pl
from jax.experimental.pallas import tpu as pltpu
from jax.sharding import Mesh, PartitionSpec as P

HD = 128
SEG = 32


EPSILON = 1e-06
ROPE_BASE = 1000000.0


def product(left_side, right_side):
    return jnp.dot(left_side, right_side, preferred_element_type=jnp.float32)


def product_left(left_side, right_side):
    return lax.dot_general(
        left_side, right_side, (((0,), (0,)), ((), ())), preferred_element_type=jnp.float32
    )


def product_right(left_side, right_side):
    return lax.dot_general(
        left_side, right_side, (((1,), (1,)), ((), ())), preferred_element_type=jnp.float32
    )


def silu_slope(inputs):
    sigmoid_value = jax.nn.sigmoid(inputs)
    return sigmoid_value * (1.0 + inputs * (1.0 - sigmoid_value))


def rope_tables(position_row, head_size):
    half_size = head_size // 2
    inverse = ROPE_BASE ** (-(jnp.arange(half_size, dtype=jnp.float32) * 2.0 / head_size))
    angles = position_row.astype(jnp.float32)[:, None] * inverse[None, :]
    cosine = jnp.cos(angles)
    sine_table = jnp.sin(angles)
    return (jnp.concatenate([cosine, cosine], 1), jnp.concatenate([sine_table, sine_table], 1))


def rotate(vectors, cosine, sine_table):
    half_size = vectors.shape[-1] // 2
    turned = jnp.concatenate([-vectors[..., half_size:], vectors[..., :half_size]], -1)
    return vectors * cosine[:, None, :] + turned * sine_table[:, None, :]


def unrotate(gradient, cosine, sine_table):
    half_size = gradient.shape[-1] // 2
    scaled = gradient * sine_table[:, None, :]
    turned = jnp.concatenate([scaled[..., half_size:], -scaled[..., :half_size]], -1)
    return gradient * cosine[:, None, :] + turned


def tree_mask(parent_row, seg_len):
    segment_count = parent_row.shape[0]
    segment_ids = jnp.arange(segment_count, dtype=jnp.int32)
    step_matrix = (
        (parent_row[:, None] == segment_ids[None, :]) & (segment_ids[:, None] > 0)
    ).astype(jnp.float32)
    identity = jnp.eye(segment_count, dtype=jnp.float32)

    def extend(loop_index, reached):
        return jnp.minimum(
            identity + jnp.dot(step_matrix, reached, precision=lax.Precision.HIGHEST), 1.0
        )

    reached = lax.fori_loop(0, segment_count, extend, identity)
    expanded = jnp.repeat(jnp.repeat(reached, seg_len, 0), seg_len, 1) > 0.5
    token_ids = jnp.arange(segment_count * seg_len, dtype=jnp.int32)
    return expanded & (token_ids[None, :] <= token_ids[:, None])


def gathered_shards(
    layer_input,
    positions,
    parents,
    routes,
    route_slots,
    norm1_gain,
    project_weight,
    project_bias,
    output_weight,
    norm2_gain,
    router_weight,
    shared_vector,
    shared_gate,
    shared_up,
    shared_down,
    expert_gate,
    expert_up,
    expert_down,
    cotangent,
):
    micro_count, seq_rows, model_width = layer_input.shape
    top_count = routes.shape[2]
    expert_count = router_weight.shape[1]
    capacity = seq_rows * top_count * 5 // (4 * expert_count)
    slot_total = expert_count * capacity
    gathered = (
        lax.all_gather(norm1_gain, "expert", axis=0, tiled=True),
        lax.all_gather(project_weight, "expert", axis=0, tiled=True),
        lax.all_gather(project_bias, "expert", axis=1, tiled=True),
        lax.all_gather(output_weight, "expert", axis=1, tiled=True),
        lax.all_gather(norm2_gain, "expert", axis=0, tiled=True),
        lax.all_gather(router_weight, "expert", axis=0, tiled=True),
        lax.all_gather(shared_vector, "expert", axis=0, tiled=True),
        lax.all_gather(shared_gate, "expert", axis=0, tiled=True),
        lax.all_gather(shared_up, "expert", axis=0, tiled=True),
        lax.all_gather(shared_down, "expert", axis=1, tiled=True),
    )
    (
        gain_first,
        project_in,
        bias_in,
        project_out,
        gain_second,
        router_full,
        vector_full,
        shared_gates,
        shared_ups,
        shared_downs,
    ) = gathered
    local_width = project_in.shape[2]
    head_count = local_width // HD
    shared_local = shared_gates.shape[1]
    project_flat = project_in.reshape(model_width, 3 * local_width)
    bias_flat = bias_in.astype(jnp.float32).reshape(3 * local_width)
    gain_one = gain_first.astype(jnp.float32)
    gain_two = gain_second.astype(jnp.float32)
    small_weights = jnp.concatenate([router_full, vector_full[:, None]], 1)
    expert_gates = expert_gate[0]
    expert_ups = expert_up[0]
    expert_downs = expert_down[0]
    score_scale = HD ** (-0.5)
    expert_ids = jnp.arange(expert_count, dtype=jnp.int32)
    pair_ids = jnp.arange(seq_rows * top_count, dtype=jnp.int32).reshape(seq_rows, top_count)
    zero_row = jnp.zeros((1, model_width), jnp.bfloat16)
    stored = []
    layer_outputs = []
    for batch_index in range(micro_count):
        input_rows = layer_input[batch_index].astype(jnp.float32)
        norm_one = lax.rsqrt(jnp.mean(input_rows * input_rows, -1, keepdims=True) + EPSILON)
        normed_one = (input_rows * norm_one * gain_one).astype(jnp.bfloat16)
        projected = (product(normed_one, project_flat) + bias_flat).reshape(
            seq_rows, 3, head_count, HD
        )
        cosine, sine_table = rope_tables(positions[batch_index], HD)
        queries = rotate(projected[:, 0], cosine, sine_table).astype(jnp.bfloat16)
        key_rows = rotate(projected[:, 1], cosine, sine_table).astype(jnp.bfloat16)
        values = projected[:, 2].astype(jnp.bfloat16)
        allowed = tree_mask(parents[batch_index, 0], SEG)
        scores = (
            jnp.einsum("qhd,khd->hqk", queries, key_rows, preferred_element_type=jnp.float32)
            * score_scale
        )
        masked = jnp.where(allowed[None], scores, -1e30)
        highest = jnp.max(masked, -1, keepdims=True)
        exponent = jnp.exp(masked - highest)
        row_total = jnp.sum(exponent, -1, keepdims=True)
        attention_probs = exponent / row_total
        log_total = highest + jnp.log(row_total)
        heads_out = (
            jnp.einsum(
                "hqk,khd->qhd",
                attention_probs.astype(jnp.bfloat16),
                values,
                preferred_element_type=jnp.float32,
            )
            .astype(jnp.bfloat16)
            .reshape(seq_rows, local_width)
        )
        attention = lax.psum(product(heads_out, project_out), "tensor")
        hidden_state = input_rows + attention
        norm_two = lax.rsqrt(jnp.mean(hidden_state * hidden_state, -1, keepdims=True) + EPSILON)
        normed_two = (hidden_state * norm_two * gain_two).astype(jnp.bfloat16)
        small_logits = product(normed_two, small_weights)
        router_prob = jax.nn.softmax(small_logits[:, :expert_count], axis=-1)
        onehot = (routes[batch_index][..., None] == expert_ids).astype(jnp.float32)
        picked = jnp.sum(onehot * router_prob[:, None, :], -1)
        picked_sum = jnp.sum(picked, -1, keepdims=True)
        route_gates = picked / picked_sum
        shared_scale = jax.nn.sigmoid(small_logits[:, expert_count])
        gate_shared = product(normed_two, shared_gates)
        up_shared = product(normed_two, shared_ups)
        hidden_shared = (jax.nn.silu(gate_shared) * up_shared).astype(jnp.bfloat16)
        shared_part = product(hidden_shared, shared_downs)
        slot_rows = route_slots[batch_index]
        valid = slot_rows < capacity
        keep_mask = valid.astype(jnp.float32)
        slot_index = routes[batch_index] * capacity + jnp.minimum(slot_rows, capacity - 1)
        safe_index = jnp.where(valid, slot_index, 0)
        target = jnp.where(valid, slot_index, slot_total).reshape(-1)
        slot_table = (
            jnp.full((slot_total,), seq_rows * top_count, jnp.int32)
            .at[target]
            .set(pair_ids.reshape(-1), mode="drop")
        )
        padded = jnp.concatenate([normed_two, zero_row], 0)
        outgoing = padded[slot_table // top_count].reshape(expert_count, capacity, model_width)
        received = lax.all_to_all(outgoing, "expert", split_axis=0, concat_axis=0, tiled=True)
        run_owner_rows = received.reshape(-1, model_width)
        run_gate_expert = product(run_owner_rows, expert_gates)
        run_up_expert = product(run_owner_rows, expert_ups)
        run_hidden_expert = (jax.nn.silu(run_gate_expert) * run_up_expert).astype(jnp.bfloat16)
        expert_rows = product(run_hidden_expert, expert_downs).reshape(
            received.shape[0], received.shape[1], model_width
        )
        returned = lax.all_to_all(expert_rows, "expert", split_axis=0, concat_axis=0, tiled=True)
        returned, received = (returned, received)
        pair_out = returned.reshape(slot_total, -1)[safe_index] * keep_mask[..., None]
        routed = jnp.sum(route_gates[..., None] * pair_out, 1)
        shared_out, routed_full = lax.psum((shared_part, routed), "tensor")
        layer_outputs.append(
            (hidden_state + shared_scale[:, None] * shared_out + routed_full).astype(jnp.bfloat16)
        )
        stored.append(
            (
                input_rows,
                norm_one,
                normed_one,
                cosine,
                sine_table,
                queries,
                key_rows,
                values,
                allowed,
                log_total,
                heads_out,
                hidden_state,
                norm_two,
                normed_two,
                router_prob,
                onehot,
                picked_sum,
                route_gates,
                shared_scale,
                gate_shared,
                up_shared,
                hidden_shared,
                shared_out,
                pair_out,
                safe_index,
                keep_mask,
                slot_table,
                received,
            )
        )
    grad_gain_one = jnp.zeros((model_width,), jnp.float32)
    grad_gain_two = jnp.zeros((model_width,), jnp.float32)
    grad_project = jnp.zeros((model_width, 3 * local_width), jnp.float32)
    grad_bias = jnp.zeros((3 * local_width,), jnp.float32)
    grad_output = jnp.zeros((local_width, model_width), jnp.float32)
    grad_small = jnp.zeros((model_width, expert_count + 1), jnp.float32)
    grad_shared_gate = jnp.zeros((model_width, shared_local), jnp.float32)
    grad_shared_up = jnp.zeros((model_width, shared_local), jnp.float32)
    grad_shared_down = jnp.zeros((shared_local, model_width), jnp.float32)
    grad_expert_gate = jnp.zeros(expert_gates.shape, jnp.float32)
    grad_expert_up = jnp.zeros(expert_ups.shape, jnp.float32)
    grad_expert_down = jnp.zeros(expert_downs.shape, jnp.float32)
    input_grads = [None] * micro_count
    for batch_index in reversed(range(micro_count)):
        (
            input_rows,
            norm_one,
            normed_one,
            cosine,
            sine_table,
            queries,
            key_rows,
            values,
            allowed,
            log_total,
            heads_out,
            hidden_state,
            norm_two,
            normed_two,
            router_prob,
            onehot,
            picked_sum,
            route_gates,
            shared_scale,
            gate_shared,
            up_shared,
            hidden_shared,
            shared_out,
            pair_out,
            safe_index,
            keep_mask,
            slot_table,
            received,
        ) = stored[batch_index]
        upstream = cotangent[batch_index].astype(jnp.float32)
        shared_grad = (shared_scale[:, None] * upstream).astype(jnp.bfloat16)
        scale_grad = jnp.sum(upstream * shared_out, -1) * shared_scale * (1.0 - shared_scale)
        gate_part = jnp.sum(upstream[:, None, :] * pair_out, -1)
        pair_grad = (
            (route_gates[..., None] * upstream[:, None, :])
            .astype(jnp.bfloat16)
            .reshape(seq_rows * top_count, model_width)
        )
        outgoing_grad = jnp.concatenate([pair_grad, zero_row], 0)[slot_table].reshape(
            expert_count, capacity, model_width
        )
        arrived = lax.all_to_all(outgoing_grad, "expert", split_axis=0, concat_axis=0, tiled=True)
        owner_rows = received.reshape(-1, model_width)
        owner_grads = arrived.reshape(-1, model_width)
        gate_expert = product(owner_rows, expert_gates)
        up_expert = product(owner_rows, expert_ups)
        active_expert = jax.nn.silu(gate_expert)
        hidden_expert = (active_expert * up_expert).astype(jnp.bfloat16)
        hidden_expert_grad = product_right(owner_grads, expert_downs)
        grad_expert_down = grad_expert_down + product_left(hidden_expert, owner_grads)
        gate_expert_grad = (hidden_expert_grad * up_expert * silu_slope(gate_expert)).astype(
            jnp.bfloat16
        )
        up_expert_grad = (hidden_expert_grad * active_expert).astype(jnp.bfloat16)
        grad_expert_gate = grad_expert_gate + product_left(owner_rows, gate_expert_grad)
        grad_expert_up = grad_expert_up + product_left(owner_rows, up_expert_grad)
        row_grad = product_right(gate_expert_grad, expert_gates) + product_right(
            up_expert_grad, expert_ups
        )
        row_back = lax.all_to_all(
            row_grad.reshape(expert_count, capacity, model_width),
            "expert",
            split_axis=0,
            concat_axis=0,
            tiled=True,
        )
        routed_back = jnp.sum(
            row_back.reshape(slot_total, model_width)[safe_index] * keep_mask[..., None], 1
        )
        hidden_shared_grad = product_right(shared_grad, shared_downs)
        grad_shared_down = grad_shared_down + product_left(hidden_shared, shared_grad)
        gate_shared_grad = (hidden_shared_grad * up_shared * silu_slope(gate_shared)).astype(
            jnp.bfloat16
        )
        up_shared_grad = (hidden_shared_grad * jax.nn.silu(gate_shared)).astype(jnp.bfloat16)
        grad_shared_gate = grad_shared_gate + product_left(normed_two, gate_shared_grad)
        grad_shared_up = grad_shared_up + product_left(normed_two, up_shared_grad)
        normed_part = (
            product_right(gate_shared_grad, shared_gates)
            + product_right(up_shared_grad, shared_ups)
            + routed_back
        )
        normed_sum, gate_grad = lax.psum((normed_part, gate_part), "tensor")
        picked_grad = (gate_grad - jnp.sum(gate_grad * route_gates, -1, keepdims=True)) / picked_sum
        prob_grad = jnp.sum(picked_grad[..., None] * onehot, 1)
        logit_grad = router_prob * (prob_grad - jnp.sum(router_prob * prob_grad, -1, keepdims=True))
        small_grad = jnp.concatenate([logit_grad, scale_grad[:, None]], 1).astype(jnp.bfloat16)
        grad_small = grad_small + product_left(normed_two, small_grad)
        normed_two_grad = normed_sum + product_right(small_grad, small_weights)
        grad_gain_two = grad_gain_two + jnp.sum(normed_two_grad * hidden_state * norm_two, 0)
        scaled_two = normed_two_grad * gain_two
        hidden_grad = (
            upstream
            + norm_two * scaled_two
            - hidden_state * norm_two**3 * jnp.mean(scaled_two * hidden_state, -1, keepdims=True)
        )
        attention_grad = hidden_grad.astype(jnp.bfloat16)
        grad_output = grad_output + product_left(heads_out, attention_grad)
        heads_grad = (
            product_right(attention_grad, project_out)
            .astype(jnp.bfloat16)
            .reshape(seq_rows, head_count, HD)
        )
        scores = (
            jnp.einsum("qhd,khd->hqk", queries, key_rows, preferred_element_type=jnp.float32)
            * score_scale
        )
        masked = jnp.where(allowed[None], scores, -1e30)
        attention_probs = jnp.exp(masked - log_total)
        value_grad = jnp.einsum(
            "hqk,qhd->khd",
            attention_probs.astype(jnp.bfloat16),
            heads_grad,
            preferred_element_type=jnp.float32,
        )
        prob_grads = jnp.einsum(
            "qhd,khd->hqk", heads_grad, values, preferred_element_type=jnp.float32
        )
        score_grad = (
            attention_probs
            * (prob_grads - jnp.sum(attention_probs * prob_grads, -1, keepdims=True))
        ).astype(jnp.bfloat16)
        query_grad = (
            jnp.einsum("hqk,khd->qhd", score_grad, key_rows, preferred_element_type=jnp.float32)
            * score_scale
        )
        key_grad = (
            jnp.einsum("hqk,qhd->khd", score_grad, queries, preferred_element_type=jnp.float32)
            * score_scale
        )
        projected_grad = (
            jnp.stack(
                [
                    unrotate(query_grad, cosine, sine_table),
                    unrotate(key_grad, cosine, sine_table),
                    value_grad,
                ],
                1,
            )
            .astype(jnp.bfloat16)
            .reshape(seq_rows, 3 * local_width)
        )
        grad_bias = grad_bias + jnp.sum(projected_grad.astype(jnp.float32), 0)
        grad_project = grad_project + product_left(normed_one, projected_grad)
        normed_one_grad = lax.psum(
            product_right(projected_grad, project_flat).astype(jnp.bfloat16), "tensor"
        ).astype(jnp.float32)
        grad_gain_one = grad_gain_one + jnp.sum(normed_one_grad * input_rows * norm_one, 0)
        scaled_one = normed_one_grad * gain_one
        input_grads[batch_index] = (
            hidden_grad
            + norm_one * scaled_one
            - input_rows * norm_one**3 * jnp.mean(scaled_one * input_rows, -1, keepdims=True)
        )
    reduced = (
        lax.psum_scatter(
            grad_gain_one.astype(jnp.bfloat16), "expert", scatter_dimension=0, tiled=True
        ).astype(jnp.float32),
        lax.psum_scatter(
            grad_project.reshape(model_width, 3, local_width).astype(jnp.bfloat16),
            "expert",
            scatter_dimension=0,
            tiled=True,
        ).astype(jnp.float32),
        lax.psum_scatter(
            grad_bias.reshape(3, local_width).astype(jnp.bfloat16),
            "expert",
            scatter_dimension=1,
            tiled=True,
        ).astype(jnp.float32),
        lax.psum_scatter(
            grad_output.astype(jnp.bfloat16), "expert", scatter_dimension=1, tiled=True
        ).astype(jnp.float32),
        lax.psum_scatter(
            grad_gain_two.astype(jnp.bfloat16), "expert", scatter_dimension=0, tiled=True
        ).astype(jnp.float32),
        lax.psum_scatter(
            grad_small[:, :expert_count].astype(jnp.bfloat16),
            "expert",
            scatter_dimension=0,
            tiled=True,
        ).astype(jnp.float32),
        lax.psum_scatter(
            grad_small[:, expert_count].astype(jnp.bfloat16),
            "expert",
            scatter_dimension=0,
            tiled=True,
        ).astype(jnp.float32),
        lax.psum_scatter(
            grad_shared_gate.astype(jnp.bfloat16), "expert", scatter_dimension=0, tiled=True
        ).astype(jnp.float32),
        lax.psum_scatter(
            grad_shared_up.astype(jnp.bfloat16), "expert", scatter_dimension=0, tiled=True
        ).astype(jnp.float32),
        lax.psum_scatter(
            grad_shared_down.astype(jnp.bfloat16), "expert", scatter_dimension=1, tiled=True
        ).astype(jnp.float32),
    )
    return (
        jnp.stack(layer_outputs),
        jnp.stack(input_grads),
        reduced[0],
        reduced[1],
        reduced[2],
        reduced[3],
        reduced[4],
        reduced[5],
        reduced[6],
        reduced[7],
        reduced[8],
        reduced[9],
        grad_expert_gate[None],
        grad_expert_up[None],
        grad_expert_down[None],
    )


AXES = ("z", "x", "y", "c")


MESH_ID = pl.DeviceIdType.MESH
VMEM_LIMIT = 60 * 1024 * 1024


def positions_here():
    return tuple(lax.axis_index(a) for a in AXES)


def planes_from(z):
    return (z, z + 1 - 2 * (z % 2), 2 - z // 2, 3 * (1 - z // 2))


def mirror(z, which):
    return (z, z + 1 - 2 * (z % 2), lax.rem(z + 2, 4), 3 - z)[which]


def greet(barrier, partners):
    for partner in partners:
        pl.semaphore_signal(barrier, inc=1, device_id=partner, device_id_type=MESH_ID)
    pl.semaphore_wait(barrier, len(partners))


def near_partners(z, x, y):
    planes = planes_from(z)
    return [{"x": 1 - x}, {"y": 1 - y}] + [{"z": p} for p in planes[1:]]


def run(*steps):
    for step in steps:
        step()


class Sends:
    def __init__(self):
        self.open = []

    def start(self, source, target, send, receive, where, only=None):
        copy = pltpu.make_async_remote_copy(
            src_ref=source, dst_ref=target, send_sem=send, recv_sem=receive, device_id=where, device_id_type=MESH_ID
        )
        if only is None:
            copy.start()
        else:
            pl.when(only)(copy.start)
        self.open.append((copy, only))

    def finish(self):
        for copy, only in self.open:
            if only is None:
                copy.wait_send()
            else:
                pl.when(only)(copy.wait_send)
        self.open = []


def arrive(buffer, receive):
    pltpu.make_async_copy(buffer, buffer, receive).wait()


class Gather:
    ready = (5, 8, 11, 14)

    def __init__(self, held, send, receive, cut, sends, twice=False):
        self.held, self.send, self.receive, self.sends, self.twice = held, send, receive, sends, twice
        width = held.shape[-1]
        self.left, self.right = pl.ds(0, cut), pl.ds(cut, width - cut)
        self.z, self.x, self.y, _ = positions_here()
        self.planes = planes_from(self.z)
        self.inner = jnp.logical_or(self.z == 1, self.z == 2)

    def block(self, plane, x, y, columns=None):
        if columns is None:
            return self.held.at[plane, x, y]
        return self.held.at[plane, x, y, :, columns]

    def pass_on(self, plane, x, y, columns, slot, axis):
        here = self.x if axis == "x" else self.y
        ref = self.block(plane, x, y, columns)
        self.sends.start(ref, ref, self.send.at[slot, plane], self.receive.at[slot, plane], {axis: 1 - here})

    def along(self, plane, slot, to, only=None):
        ref = self.block(plane, self.x, self.y)
        self.sends.start(ref, ref, self.send.at[slot, plane], self.receive.at[6, plane], {"z": to}, only)

    def plane(self, step):
        plane = self.planes[step]
        arrive(self.block(plane, self.x, self.y), self.receive.at[6, plane])
        self.along(plane, 6, 3 - self.z if step == 1 else self.planes[1], self.inner)

    def first(self, step, part):
        plane, x, y = self.planes[step], self.x, self.y
        if part == 0:
            self.pass_on(plane, x, y, self.left, 0, "x")
            if step or not self.twice:
                self.pass_on(plane, x, y, self.right, 1, "y")
        else:
            if step or not self.twice:
                self.pass_on(plane, x, y, self.left, 2, "y")
            self.pass_on(plane, x, y, self.right, 3, "x")

    def second(self, step):
        plane, x, y = self.planes[step], self.x, self.y
        arrive(self.block(plane, 1 - x, y, self.left), self.receive.at[0, plane])
        self.pass_on(plane, 1 - x, y, self.left, 4, "y")
        if step or not self.twice:
            arrive(self.block(plane, x, 1 - y, self.right), self.receive.at[1, plane])
        self.pass_on(plane, x, 1 - y, self.right, 5, "x")

    def third(self, step):
        plane, x, y = self.planes[step], self.x, self.y
        if step or not self.twice:
            arrive(self.block(plane, x, 1 - y, self.left), self.receive.at[2, plane])
        arrive(self.block(plane, 1 - x, y, self.right), self.receive.at[3, plane])

    def fourth(self, step):
        plane, x, y = self.planes[step], self.x, self.y
        arrive(self.block(plane, 1 - x, 1 - y, self.left), self.receive.at[4, plane])
        arrive(self.block(plane, 1 - x, 1 - y, self.right), self.receive.at[5, plane])

    def steps(self):
        def begin():
            self.first(0, 0)
            self.along(self.z, 6, self.planes[1])
            self.along(self.z, 7, 3 - self.z, self.inner)
            self.first(0, 1)

        found = [begin, lambda: self.plane(1), lambda: self.second(0)]
        for step in range(4):

            def turn_over(step=step):
                if 0 < step + 2 < 4:
                    self.plane(step + 2)
                self.third(step)
                if step < 3:
                    self.first(step + 1, 0)

            def close(step=step):
                self.fourth(step)
                if step < 3:
                    self.first(step + 1, 1)

            found += [turn_over, close]
            if step < 3:
                found.append(lambda step=step: self.second(step + 1))
        return found

    @staticmethod
    def semaphores():
        return [pltpu.SemaphoreType.DMA((8, 4)), pltpu.SemaphoreType.DMA((7, 4))]


class Reduce:
    def __init__(self, parts, buffers, cut, sends):
        self.parts, self.sends = parts, sends
        self.one_left, self.one_right, self.two_left, self.two_right, self.last, self.send, self.receive = buffers
        width = parts.shape[-1]
        self.left, self.right = pl.ds(0, cut), pl.ds(cut, width - cut)
        self.z, self.x, self.y, _ = positions_here()
        self.planes = planes_from(self.z)

    @staticmethod
    def buffers(rows, width, cut):
        bf16 = jnp.bfloat16
        return [
            pltpu.VMEM((4, 2, rows, cut), bf16),
            pltpu.VMEM((4, 2, rows, width - cut), bf16),
            pltpu.VMEM((4, rows, cut), bf16),
            pltpu.VMEM((4, rows, width - cut), bf16),
            pltpu.VMEM((4, rows, width), bf16),
            pltpu.SemaphoreType.DMA((7, 4)),
            pltpu.SemaphoreType.DMA((7, 4)),
        ]

    def first(self, step, part):
        plane, x, y = self.planes[step], self.x, self.y
        its_x, its_y = (1 - x, 1 - y) if part == 0 else (x, y)
        self.sends.start(
            self.parts.at[plane, its_x, 1 - y, :, self.left], self.one_left.at[plane, part],
            self.send.at[part, plane], self.receive.at[part, plane], {"y": 1 - y},
        )
        self.sends.start(
            self.parts.at[plane, 1 - x, its_y, :, self.right], self.one_right.at[plane, part],
            self.send.at[2 + part, plane], self.receive.at[2 + part, plane], {"x": 1 - x},
        )

    def add(self, ref, other):
        ref[...] = (ref[...].astype(jnp.float32) + other[...].astype(jnp.float32)).astype(ref.dtype)

    def second(self, step):
        plane, x, y = self.planes[step], self.x, self.y
        arrive(self.one_left.at[plane, 0], self.receive.at[0, plane])
        away = self.parts.at[plane, 1 - x, y, :, self.left]
        self.add(away, self.one_left.at[plane, 0])
        self.sends.start(away, self.two_left.at[plane], self.send.at[4, plane], self.receive.at[4, plane], {"x": 1 - x})
        arrive(self.one_right.at[plane, 0], self.receive.at[2, plane])
        away = self.parts.at[plane, x, 1 - y, :, self.right]
        self.add(away, self.one_right.at[plane, 0])
        self.sends.start(away, self.two_right.at[plane], self.send.at[5, plane], self.receive.at[5, plane], {"y": 1 - y})

    def keep(self, step):
        plane, x, y = self.planes[step], self.x, self.y
        arrive(self.one_left.at[plane, 1], self.receive.at[1, plane])
        arrive(self.one_right.at[plane, 1], self.receive.at[3, plane])
        self.add(self.parts.at[plane, x, y, :, self.left], self.one_left.at[plane, 1])
        self.add(self.parts.at[plane, x, y, :, self.right], self.one_right.at[plane, 1])

    def third(self, step):
        plane, x, y = self.planes[step], self.x, self.y
        here = self.parts.at[plane, x, y]
        arrive(self.two_left.at[plane], self.receive.at[4, plane])
        arrive(self.two_right.at[plane], self.receive.at[5, plane])
        self.add(here.at[:, self.left], self.two_left.at[plane])
        self.add(here.at[:, self.right], self.two_right.at[plane])
        if step:
            self.sends.start(here, self.last.at[self.z], self.send.at[6, plane], self.receive.at[6, self.z], {"z": plane})

    def steps(self, order):
        def begin():
            self.first(order[0], 0)
            self.first(order[0], 1)

        found = [begin]
        for i in range(4):

            def keep(i=i):
                self.keep(order[i])
                if i < 3:
                    self.first(order[i + 1], 0)

            def third(i=i):
                self.third(order[i])
                if i < 3:
                    self.first(order[i + 1], 1)

            found += [lambda i=i: self.second(order[i]), keep, third]
        return found

    def total(self):
        here = self.parts[self.z, self.x, self.y].astype(jnp.float32)
        for plane in self.planes[1:]:
            arrive(self.last.at[plane], self.receive.at[6, plane])
            here = here + self.last[plane].astype(jnp.float32)
        return here


EXTRA = 128


def dot_nn(a, b):
    return lax.dot_general(a, b, (((1,), (0,)), ((), ())), preferred_element_type=jnp.float32)


def dot_nt(a, b):
    return lax.dot_general(a, b, (((1,), (1,)), ((), ())), preferred_element_type=jnp.float32)


def dot_tn(a, b):
    return lax.dot_general(a, b, (((0,), (0,)), ((), ())), preferred_element_type=jnp.float32)


def chips_but(z, x, y):
    found = []
    for dz in range(4):
        for dx in range(2):
            for dy in range(2):
                if dz or dx or dy:
                    found.append({"z": lax.rem(z + dz, 4), "x": (x + dx) % 2, "y": (y + dy) % 2})
    return found


def experts_call(own, cotangents, three, routed_units):
    bf16, f32 = jnp.bfloat16, jnp.float32
    rows, wide = own.shape
    width = wide - EXTRA
    units = three.shape[1]
    shared_units = units - routed_units
    tile = routed_units // 2
    assert shared_units == tile
    chunk = 4 * rows
    tokens = 4 * chunk
    cut = width // 2
    column = 1024
    half_tile = tile // 2
    keep = tile + half_tile

    def kernel(own_ref, cot_in, three_ref, sum_ref, out_ref, dot_ref, expert0, expert1, expert2, shared_ref, cot_ref, held, weights, hidden, gate_grad, up_grad,
               part_n, part_o, dots_mine, staged, *rest):
        (g_send, g_recv, w_sem, d_send, d_recv, free, x_send, x_recv, s_sem) = rest[:9]
        n_bufs, o_bufs = rest[9:16], rest[16:23]
        z, x, y, c = positions_here()
        here = z * 2 + x
        loads = [pltpu.make_async_copy(three_ref.at[i], weights.at[i], w_sem.at[i]) for i in range(3)]
        loads.append(pltpu.make_async_copy(cot_in, cot_ref, w_sem.at[3]))
        for load in loads:
            load.start()
        others = chips_but(z, x, y)
        greet(pltpu.get_barrier_semaphore(), others + [{"c": 1 - c}])
        held[z, x, y] = own_ref[...]
        sends = Sends()
        gather = Gather(held, g_send, g_recv, cut, sends)
        sum_n = Reduce(part_n, n_bufs, cut, sends)
        sum_o = Reduce(part_o, o_bufs, cut, sends)
        lanes = lax.broadcasted_iota(jnp.int32, (16, EXTRA), 1)
        rows_of = lax.broadcasted_iota(jnp.int32, (16, EXTRA), 0)
        pick = ((rows_of == 0) & ((lanes == here) | (lanes == here + 8))) | ((rows_of == 1) & ((lanes == 16) | (lanes == 17)))
        pick = pick.astype(f32).astype(bf16)

        def units_of(step):
            plane = gather.planes[step]
            place = pl.ds(pl.multiple_of(plane * chunk, chunk), chunk)
            rows_n = held[plane, :, :, :, 0:width].reshape(chunk, width)
            rows_c = cot_ref[plane].reshape(chunk, width)
            scales = dot_nt(pick, held[plane, :, :, :, width:wide].reshape(chunk, EXTRA))

            def one(i, _):
                span = pl.ds(pl.multiple_of(i * tile, 32), tile)
                scale = jnp.where(i == 2, scales[1:2], scales[0:1])
                gate = dot_nt(weights[0, span, :], rows_n)
                up = dot_nt(weights[1, span, :], rows_n)
                down = dot_nt(weights[2, span, :], rows_c)
                sig = 1.0 / (1.0 + jnp.exp(-gate))
                active = gate * sig
                hid = active * up
                dot = jnp.sum(hid * down, 0, keepdims=True)
                hidden[span, place] = (hid * scale).astype(bf16)
                grad = down * scale
                gate_grad[span, place] = (grad * up * (sig + active * (1.0 - sig))).astype(bf16)
                up_grad[span, place] = (grad * active).astype(bf16)
                routed, shared = lax.cond(i == 2, lambda: (jnp.zeros_like(dot), dot), lambda: (dot, jnp.zeros_like(dot)))
                return (_[0] + routed, _[1] + shared)

            zero = jnp.zeros((1, chunk), f32)
            routed, shared = lax.fori_loop(0, 3, one, (zero, zero))
            row = lax.broadcasted_iota(jnp.int32, (8, chunk), 0)
            both = jnp.where(row == 0, routed, jnp.where(row == 1, shared, 0.0))
            for t in range(2):
                dots_mine[plane, t] = both[:, t * 2 * rows : (t + 1) * 2 * rows]

        def back_of(step):
            plane = gather.planes[step]
            place = pl.ds(pl.multiple_of(plane * chunk, chunk), chunk)

            def one(i, _):
                span = pl.ds(pl.multiple_of(i * column, column), column)
                value = dot_tn(gate_grad[:, place], weights[0, :, span]) + dot_tn(up_grad[:, place], weights[1, :, span])
                part_n[plane, :, :, :, span] = value.astype(bf16).reshape(2, 2, rows, column)
                return 0

            lax.fori_loop(0, width // column, one, 0)

        def out_of(step):
            plane = gather.planes[step]
            place = pl.ds(pl.multiple_of(plane * chunk, chunk), chunk)

            def one(i, _):
                span = pl.ds(pl.multiple_of(i * column, column), column)
                value = dot_tn(hidden[:, place], weights[2, :, span])
                part_o[plane, :, :, :, span] = value.astype(bf16).reshape(2, 2, rows, column)
                return 0

            lax.fori_loop(0, width // column, one, 0)

        g, n, o = gather.steps(), sum_n.steps((0, 1, 2, 3)), sum_o.steps((0, 1, 2, 3))
        run(*g[0:4])
        for load in loads:
            load.wait()
        g[4]()
        units_of(0)
        g[5]()
        back_of(0)
        run(n[0], g[6], g[7])
        units_of(1)
        run(n[1], g[8])
        back_of(1)
        run(n[2], n[3], g[9], g[10])
        units_of(2)
        run(n[4], g[11])
        back_of(2)
        run(n[5], n[6], g[12], g[13])
        units_of(3)
        n[7]()
        back_of(3)
        n[8]()
        out_of(0)
        run(o[0], n[9])
        out_of(1)
        n[10]()
        out_of(2)
        run(o[1], n[11])
        out_of(3)
        for i, other in enumerate(others):
            sends.start(dots_mine.at[other["z"], other["x"]], dot_ref.at[z, x, y], d_send.at[i], d_recv.at[z, x, y], other)
        dot_ref[z, x, y] = dots_mine[z, x]
        pl.semaphore_signal(free, inc=1, device_id={"c": 1 - c}, device_id_type=MESH_ID)

        def gradient(kind, first, count, span):
            if kind < 2:
                side = (gate_grad, up_grad)[kind]
                return dot_nn(side[pl.ds(first, count), :], held[:, :, :, :, span].reshape(tokens, column))
            return dot_nn(hidden[pl.ds(first, count), :], cot_ref[:, :, :, :, span].reshape(tokens, column))

        def away(kind, i):
            span = pl.ds(i * column, column)
            first = pl.multiple_of((1 - c) * tile, 32)
            weights[kind, 0:tile, span] = gradient(kind, first, tile, span).astype(bf16)
            first = pl.multiple_of(routed_units + (1 - c) * half_tile, 16)
            weights[kind, tile:keep, span] = gradient(kind, first, half_tile, span).astype(bf16)

        def stay(kind, i):
            span = pl.ds(i * column, column)
            first = pl.multiple_of(c * tile, 32)
            value = gradient(kind, first, tile, span)
            staged[kind % 2, :, span] = (value + weights[kind, keep : keep + tile, span].astype(f32)).astype(bf16)
            first = pl.multiple_of(routed_units + c * half_tile, 16)
            value = gradient(kind, first, half_tile, span)
            shared_ref[kind, :, span] = (value + weights[kind, keep + tile : 2 * keep, span].astype(f32)).astype(bf16)

        def hand_over(kind):
            sends.start(weights.at[kind, 0:keep], weights.at[kind, keep : 2 * keep], x_send.at[kind], x_recv.at[kind], {"c": 1 - c})

        away(0, 0)
        run(o[2], n[12])
        away(0, 1)
        o[3]()
        pl.semaphore_wait(free, 1)
        hand_over(0)
        for kind in (1, 2):
            away(kind, 0)
            o[2 + 2 * kind]()
            away(kind, 1)
            o[3 + 2 * kind]()
            hand_over(kind)
        writes = []
        for kind in range(3):
            arrive(weights.at[kind, keep : 2 * keep], x_recv.at[kind])
            if kind > 1:
                writes[kind - 2].wait()
            stay(kind, 0)
            o[8 + 2 * kind]()
            stay(kind, 1)
            if kind < 2:
                o[9 + 2 * kind]()
            write = pltpu.make_async_copy(staged.at[kind % 2], (expert0, expert1, expert2)[kind], s_sem.at[kind])
            write.start()
            writes.append(write)
        sum_ref[...] = sum_n.total()
        out_ref[...] = sum_o.total()
        for other in others:
            arrive(dot_ref.at[other["z"], other["x"], other["y"]], d_recv.at[other["z"], other["x"], other["y"]])
        writes[1].wait()
        writes[2].wait()
        sends.finish()

    vmem = pl.BlockSpec(memory_space=pltpu.VMEM)
    anywhere = pl.BlockSpec(memory_space=pl.ANY)
    dma = pltpu.SemaphoreType.DMA
    flops = 2 * tokens * width * units * 9
    return pl.pallas_call(
        kernel,
        name="experts",
        out_shape=(
            jax.ShapeDtypeStruct((rows, width), f32),
            jax.ShapeDtypeStruct((rows, width), f32),
            jax.ShapeDtypeStruct((4, 2, 2, 8, 2 * rows), f32),
            *[jax.ShapeDtypeStruct((tile, width), bf16)] * 3,
            jax.ShapeDtypeStruct((3, half_tile, width), bf16),
        ),
        in_specs=[vmem, anywhere, anywhere],
        out_specs=(vmem, vmem, vmem, anywhere, anywhere, anywhere, vmem),
        scratch_shapes=[
            pltpu.VMEM((4, 2, 2, rows, width), bf16),
            pltpu.VMEM((4, 2, 2, rows, wide), bf16),
            pltpu.VMEM((3, units, width), bf16),
            pltpu.VMEM((units, tokens), bf16),
            pltpu.VMEM((units, tokens), bf16),
            pltpu.VMEM((units, tokens), bf16),
            pltpu.VMEM((4, 2, 2, rows, width), bf16),
            pltpu.VMEM((4, 2, 2, rows, width), bf16),
            pltpu.VMEM((4, 2, 8, 2 * rows), f32),
            pltpu.VMEM((2, tile, width), bf16),
            *Gather.semaphores(),
            dma((4,)),
            dma((15,)),
            dma((4, 2, 2)),
            pltpu.SemaphoreType.REGULAR,
            dma((3,)),
            dma((3,)),
            dma((3,)),
            *Reduce.buffers(rows, width, cut),
            *Reduce.buffers(rows, width, cut),
        ],
        compiler_params=pltpu.CompilerParams(collective_id=2, has_side_effects=True, vmem_limit_bytes=VMEM_LIMIT),
        cost_estimate=pl.CostEstimate(flops=flops, bytes_accessed=40 * 1024 * 1024, transcendentals=tokens * units),
    )(own, cotangents, three)


def plane_partners(z, x, y, c):
    found = []
    for dz in range(4):
        for dx in range(2):
            for dc in range(2):
                if dz or dx or dc:
                    found.append({"z": lax.rem(z + dz, 4), "x": (x + dx) % 2, "c": (c + dc) % 2})
    return found


class Plain:
    def __init__(self):
        self.open = []

    def start(self, source, target, send, receive, where, same):
        far = pltpu.make_async_remote_copy(
            src_ref=source, dst_ref=target, send_sem=send, recv_sem=receive, device_id=where, device_id_type=MESH_ID
        )

        @pl.when(jnp.logical_not(same))
        def _():
            far.start()

        @pl.when(same)
        def _():
            pltpu.make_async_copy(source, target, receive).start()

        self.open.append((far, same))

    def finish(self):
        for far, same in self.open:

            @pl.when(jnp.logical_not(same))
            def _(far=far):
                far.wait_send()

        self.open = []


def front_call(input_rows, cotangent, project, output, rows3, router, positions, parents, bias, table, gate, up, down, experts):
    bf16, f32 = jnp.bfloat16, jnp.float32
    rows, width = input_rows.shape[-2:]
    chunk = 4 * rows
    tokens = 4 * chunk
    seq = 2 * rows
    trees = tokens // seq
    slice_rows = project.shape[1]
    half = slice_rows // 2
    local_heads = project.shape[2] // HD
    sub = down.shape[0] // trees
    tile = experts[0].shape[0]
    routed = 2 * tile
    units = routed + 2 * sub
    cut = width // 2
    late_cut = 5 * width // 8
    column = width // 2
    scale = HD ** (-0.5)
    lines = router.shape[0]

    def kernel(in_ref, cot_ref, project_ref, output_ref, gains_ref, router_ref, position_ref, parent_ref,
               bias_ref, table_ref, gate_ref, up_ref, down_ref, e0, e1, e2,
               sum_ref, normed_out, qkv_ref, prob_ref, heads_ref, head_ref, outw_ref, smalls_ref, turns_ref, cots_out, three_ref,
               all_ref, parts, small_f, small_v, shared_v, three_v, cots_ref, normed_ref, *rest):
        (g_send, g_recv, k_send, k_recv, w_send, w_recv, v_send, v_recv, m_send, m_recv, s_send, s_recv, c_send, c_recv, l_sem, e_send,
         e_recv, o_sem, n_sem, k_sem) = rest[:20]
        z, x, y, c = positions_here()
        here = z * 2 + x
        partners = plane_partners(z, x, y, c)
        other = {"c": 1 - c}
        sends, plain = Sends(), Plain()

        small_f[...] = jnp.zeros_like(small_f)
        small_f[0:2, :] = gains_ref[0:2, :].astype(f32)
        small_f[2 : 2 + lines, :] = router_ref[...].astype(f32)
        small_f[2 + lines : 3 + lines, :] = gains_ref[2:3, :].astype(f32)
        first = c == 0
        small_f[3 + lines : 4 + lines, 0:seq] = jnp.where(first, position_ref[0:1, :], position_ref[1:2, :]).astype(f32)
        segments = parent_ref.shape[1]
        small_f[4 + lines : 5 + lines, 0:segments] = jnp.where(first, parent_ref[0:1, :], parent_ref[1:2, :]).astype(f32)
        small_f[5 + lines : 8 + lines, 0 : bias_ref.shape[1]] = bias_ref[...].astype(f32)
        small_v[...] = small_f[...].astype(bf16)

        greet(pltpu.get_barrier_semaphore(), partners + [{"y": 1 - y}])
        all_ref[z, x, y] = in_ref[c, y]
        all_ref[z, x, 1 - y] = in_ref[c, 1 - y]
        gather = Gather(all_ref, g_send, g_recv, cut, sends, True)
        late = Gather(cots_ref, k_send, k_recv, late_cut, sends, True)
        add = Reduce(parts, rest[20:], late_cut, sends)
        a, g, r = gather.steps(), late.steps(), add.steps((3, 2, 1, 0))
        a[0]()
        for i, to in enumerate(partners):
            sends.start(small_v, smalls_ref.at[z, x, c], m_send.at[i], m_recv.at[z, x, c], to)
        smalls_ref[z, x, c] = small_v[...]
        for local in range(local_heads):
            chip = {"z": 2 * c + local // 2, "x": local % 2}
            home = jnp.logical_and(chip["z"] == z, chip["x"] == x)
            for part in range(2):
                where = {**chip, "c": part}
                same = jnp.logical_and(home, c == part)
                for i in range(3):
                    plain.start(
                        project_ref.at[i, pl.ds(part * half, half), pl.ds(local * HD, HD)],
                        head_ref.at[here, part, :, pl.ds(i * HD, HD)],
                        w_send.at[local, part, i], w_recv.at[here, i], where, same,
                    )
                plain.start(
                    output_ref.at[pl.ds(local * HD + part * HD // 2, HD // 2), :],
                    outw_ref.at[part, :, pl.ds(pl.multiple_of(here * slice_rows, slice_rows), slice_rows)],
                    w_send.at[local, part, 3], w_recv.at[here, 3], where, same,
                )
        mine = pl.ds(pl.multiple_of(c * tile, 16), tile)
        for i, ref in enumerate((e0, e1, e2)):
            sends.start(ref, three_v.at[i, mine], e_send.at[i], e_recv.at[i], other)
            pltpu.make_async_copy(ref, three_v.at[i, mine], l_sem.at[i]).start()

        def flip(i, _):
            span = pl.ds(pl.multiple_of(i * HD, HD), HD)
            shared_v[0, span, :] = gate_ref[:, span].astype(f32).T.astype(bf16)
            shared_v[1, span, :] = up_ref[:, span].astype(f32).T.astype(bf16)
            shared_v[2, span, :] = down_ref[span, :]
            return 0

        flips = down.shape[0] // HD
        for i in range(8):
            lax.fori_loop(i * flips // 8, (i + 1) * flips // 8, flip, 0)
            a[i + 1]()
        place = pl.ds(pl.multiple_of(routed + c * sub, 16), sub)
        lanes = pl.ds(pl.multiple_of(here * slice_rows, slice_rows), slice_rows)

        def share(i):
            to_z, to_x = mirror(z, i // 2), (x + i % 2) % 2
            source = shared_v.at[:, pl.ds(pl.multiple_of((to_z * 2 + to_x) * sub, 16), sub)]
            target = three_v.at[:, place, lanes]
            if i:
                sends.start(source, target, s_send.at[i], s_recv.at[here], {"z": to_z, "x": to_x})
            else:
                pltpu.make_async_copy(source, target, s_recv.at[here]).start()

        def hand_on(i):
            from_z, from_x = mirror(z, i // 2), (x + i % 2) % 2
            source = from_z * 2 + from_x
            span = pl.ds(pl.multiple_of(source * slice_rows, slice_rows), slice_rows)
            piece = three_v.at[:, place, span]
            arrive(piece, s_recv.at[source])
            sends.start(piece, piece, c_send.at[i], c_recv.at[source], other)

        for source in range(trees):
            for i in range(3):
                arrive(head_ref.at[source, c, :, pl.ds(i * HD, HD)], w_recv.at[source, i])
            arrive(outw_ref.at[c, :, pl.ds(source * slice_rows, slice_rows)], w_recv.at[source, 3])
        sends.start(head_ref.at[:, c], head_ref.at[:, c], v_send.at[0], v_recv.at[0], other)
        sends.start(outw_ref.at[c], outw_ref.at[c], v_send.at[1], v_recv.at[1], other)
        share(0)
        share(4)
        run(*a[9:])
        share(5)
        cots_ref[z, x, y] = cot_ref[c, y]
        cots_ref[z, x, 1 - y] = cot_ref[c, 1 - y]
        g[0]()
        for to in partners:
            spot = (to["z"], to["x"], to["c"])
            arrive(smalls_ref.at[spot], m_recv.at[spot])
        gain = jnp.concatenate([smalls_ref[e // 2, e % 2, c, 0:1, :] for e in range(trees)], 1).astype(f32)
        home_z, home_c = lax.rem(here, 4), here // 4
        width_of = bias_ref.shape[1]
        biases = [smalls_ref[home_z, e, home_c, 5 + lines : 8 + lines, 0:width_of] for e in range(2)]
        row_bias = [jnp.concatenate([b[i : i + 1].astype(f32) for b in biases], 1) for i in range(3)]
        row_bias = jnp.concatenate(row_bias, 1)
        arrive(head_ref.at[:, 1 - c], v_recv.at[0])
        arrive(outw_ref.at[1 - c], v_recv.at[1])
        query_of = lax.broadcasted_iota(jnp.int32, (seq, seq), 0)
        key_of = lax.broadcasted_iota(jnp.int32, (seq, seq), 1)
        segment_of = lax.broadcasted_iota(jnp.int32, (1, seq), 1) // SEG
        lane = lax.broadcasted_iota(jnp.int32, (seq, HD), 1)

        def attend(step):
            plane = gather.planes[step]

            def norm(i, _):
                value = all_ref[plane, i // 2, i % 2].astype(f32)
                scaled = value * lax.rsqrt(jnp.mean(value * value, -1, keepdims=True) + EPSILON) * gain
                normed_ref[plane, i // 2, i % 2] = scaled.astype(bf16)
                return 0

            lax.fori_loop(0, 4, norm, 0)
            raw = dot_nn(normed_ref[plane].reshape(chunk, width), head_ref[...].reshape(width, 3 * HD)) + row_bias
            for t in range(2):
                span = slice(t * seq, (t + 1) * seq)
                notes = smalls_ref[plane, t, c].astype(f32)
                hot = (query_of == notes[3 + lines : 4 + lines, 0:seq].astype(jnp.int32)).astype(f32).astype(bf16)
                turn = dot_tn(hot, table_ref[0]) + dot_tn(hot, table_ref[1])
                swapped = pltpu.roll(turn, HD // 2, 1)
                cos = jnp.where(lane < HD // 2, turn, swapped)
                sin = jnp.where(lane < HD // 2, -swapped, turn)
                turns_ref[0, plane, span] = cos
                turns_ref[1, plane, span] = sin
                reach = []
                for s in range(segments):
                    line = (segment_of == s).astype(f32)
                    for u in range(s):
                        line = line + (notes[4 + lines : 5 + lines, s : s + 1] == u).astype(f32) * reach[u]
                    reach.append(line)
                seen = jnp.concatenate([jnp.broadcast_to(line, (SEG, seq)) for line in reach], 0)
                allowed = jnp.logical_and(seen > 0.5, key_of <= query_of)
                turned = []
                for i in range(2):
                    value = raw[span, i * HD : (i + 1) * HD]
                    turned.append((value * cos + pltpu.roll(value, HD // 2, 1) * sin).astype(bf16))
                turned.append(raw[span, 2 * HD :].astype(bf16))
                for i in range(3):
                    qkv_ref[i, plane, span] = turned[i]
                score = jnp.where(allowed, dot_nt(turned[0], turned[1]) * scale, -1e30)
                exponent = jnp.exp(score - jnp.max(score, -1, keepdims=True))
                prob = exponent / jnp.sum(exponent, -1, keepdims=True)
                prob_ref[plane, t] = prob
                heads_ref[plane, span] = dot_nn(prob.astype(bf16), turned[2]).astype(bf16)

            def spread_out(i, _):
                span = pl.ds(pl.multiple_of(i * column, column), column)
                value = dot_nn(heads_ref[plane], outw_ref[:, :, span].reshape(HD, column))
                parts[plane, :, :, :, span] = value.astype(bf16).reshape(2, 2, rows, column)
                return 0

            lax.fori_loop(0, width // column, spread_out, 0)
            copy = pltpu.make_async_copy(normed_ref.at[plane], normed_out.at[plane], n_sem.at[step])
            copy.start()
            saved.append(copy)

        def save(step):
            plane = gather.planes[step]
            copy = pltpu.make_async_copy(cots_ref.at[plane], cots_out.at[plane], k_sem.at[step])
            copy.start()
            saved.append(copy)

        saved = []

        attend(3)
        run(r[0], g[1], g[2])
        share(6)
        attend(2)
        run(r[1], r[2], g[3])
        share(7)
        hand_on(0)
        hand_on(4)
        run(r[3], g[4])
        save(0)
        attend(1)
        share(2)
        run(r[4], r[5], g[5])
        hand_on(5)
        share(3)
        run(r[6], g[6])
        hand_on(6)
        attend(0)
        share(1)
        for i in range(3):
            arrive(three_v.at[i, mine], l_sem.at[i])
            arrive(three_v.at[i, pl.ds(pl.multiple_of((1 - c) * tile, 16), tile)], e_recv.at[i])
        early = pltpu.make_async_copy(three_v.at[:, pl.ds(0, routed)], three_ref.at[:, pl.ds(0, routed)], o_sem.at[0])
        early.start()
        run(r[7], r[8], g[7])
        save(1)
        hand_on(7)
        run(r[9], g[8])
        hand_on(2)
        run(r[10], g[9], r[11], g[10])
        save(2)
        hand_on(3)
        run(r[12], g[11], g[12])
        hand_on(1)
        sum_ref[...] = add.total()
        g[13]()
        save(3)
        theirs = pl.ds(pl.multiple_of(routed + (1 - c) * sub, 16), sub)
        for source in range(trees):
            arrive(three_v.at[:, theirs, pl.ds(source * slice_rows, slice_rows)], c_recv.at[source])
        rest_of = pltpu.make_async_copy(
            three_v.at[:, pl.ds(routed, units - routed)], three_ref.at[:, pl.ds(routed, units - routed)], o_sem.at[1]
        )
        rest_of.start()
        for copy in saved:
            copy.wait()
        early.wait()
        rest_of.wait()
        plain.finish()
        sends.finish()

    vmem = pl.BlockSpec(memory_space=pltpu.VMEM)
    anywhere = pl.BlockSpec(memory_space=pl.ANY)
    dma = pltpu.SemaphoreType.DMA
    shape = jax.ShapeDtypeStruct
    return pl.pallas_call(
        kernel,
        name="front",
        out_shape=(
            shape((rows, width), f32),
            shape((4, 2, 2, rows, width), bf16),
            shape((3, 4, chunk, HD), bf16),
            shape((4, 2, seq, seq), f32),
            shape((4, chunk, HD), bf16),
            shape((trees, 2, half, 3 * HD), bf16),
            shape((2, HD // 2, width), bf16),
            shape((4, 2, 2, 16, slice_rows), bf16),
            shape((2, 4, chunk, HD), f32),
            shape((4, 2, 2, rows, width), bf16),
            shape((3, units, width), bf16),
        ),
        in_specs=[vmem] * 16,
        out_specs=(vmem, anywhere) + (vmem,) * 7 + (anywhere,) * 2,
        scratch_shapes=[
            pltpu.VMEM((4, 2, 2, rows, width), bf16),
            pltpu.VMEM((4, 2, 2, rows, width), bf16),
            pltpu.VMEM((16, slice_rows), f32),
            pltpu.VMEM((16, slice_rows), bf16),
            pltpu.VMEM((3, *down.shape), bf16),
            pltpu.VMEM((3, units, width), bf16),
            pltpu.VMEM((4, 2, 2, rows, width), bf16),
            pltpu.VMEM((4, 2, 2, rows, width), bf16),
            *Gather.semaphores(),
            *Gather.semaphores(),
            dma((local_heads, 2, 4)),
            dma((trees, 4)),
            dma((2,)),
            dma((2,)),
            dma((15,)),
            dma((4, 2, 2)),
            dma((trees,)),
            dma((trees,)),
            dma((trees,)),
            dma((trees,)),
            dma((3,)),
            dma((3,)),
            dma((3,)),
            dma((2,)),
            dma((4,)),
            dma((4,)),
            *Reduce.buffers(rows, width, late_cut),
        ],
        compiler_params=pltpu.CompilerParams(collective_id=8, has_side_effects=True, vmem_limit_bytes=VMEM_LIMIT),
    )(input_rows, cotangent, project, output, rows3, router, positions, parents, bias, table, gate, up, down, *experts)


def all_but(z, x, y, c):
    found = []
    for dz in range(4):
        for dx in range(2):
            for dy in range(2):
                for dc in range(2):
                    if dz or dx or dy or dc:
                        found.append(
                            {"z": lax.rem(z + dz, 4), "x": (x + dx) % 2, "y": (y + dy) % 2, "c": (c + dc) % 2}
                        )
    return found


def attention_back_call(own_grad, normed, qkv, probs, heads, head, out_head, turns, input_rows, hidden_grad, gain, lines,
                        own_output, vectors, shared):
    bf16, f32 = jnp.bfloat16, jnp.float32
    rows, width = own_grad.shape
    chunk = 4 * rows
    tokens = 4 * chunk
    seq = 2 * rows
    trees, _, half, _ = head.shape
    slice_rows = 2 * half
    sub = shared.shape[1]
    cut = 5 * width // 8
    column = width // 2
    scale = HD ** (-0.5)
    local_heads = trees // 2

    def kernel(grad_ref, normed_in, qkv_ref, prob_ref, heads_ref, head_ref, outw_ref, turns_ref, in_ref, hg_ref, gain_ref,
               result_ref, vec_ref, shared_ref,
               layer_ref, ig, pgrad_ref, ograd_ref, gate_ref, up_ref, down_ref, gain1_ref, gain2_ref, router_ref, vector_ref, bias_ref,
               sgrad_ref, normed_ref,               held, parts, raw_grad, dwp, dwp_got, dwp_sum, dwo, dwo_got, dwo_sum, message, got, bias_sum, *rest):
        (g_send, g_recv, l_send, l_recv, i_send, i_recv, m_send, m_recv, s_send, s_recv, c_send, c_recv, w_send,
         w_recv, n_sem) = rest[:15]
        z, x, y, c = positions_here()
        here = z * 2 + x
        everyone = all_but(z, x, y, c)
        load = pltpu.make_async_copy(normed_in, normed_ref, n_sem)
        load.start()
        greet(pltpu.get_barrier_semaphore(), everyone)
        sends = Sends()
        plain = Plain()
        other, across = {"c": 1 - c}, {"y": 1 - y}
        held[z, x, y] = grad_ref[...]
        gather = Gather(held, g_send, g_recv, cut, sends)
        add = Reduce(parts, rest[15:], cut, sends)
        g, r = gather.steps(), add.steps((0, 1, 2, 3))
        g[0]()
        layer_ref[c, y] = result_ref[...]
        sends.start(layer_ref.at[c, y], layer_ref.at[c, y], l_send.at[0], l_recv.at[0], across)
        sends.start(layer_ref.at[c, y], layer_ref.at[c, y], l_send.at[1], l_recv.at[1], other)

        def lanes_of(e):
            return pl.ds(pl.multiple_of(e * slice_rows, slice_rows), slice_rows)

        bias_sum[...] = jnp.zeros_like(bias_sum)

        def attend(step):
            plane = gather.planes[step]
            grads = dot_nt(held[plane].reshape(chunk, width), outw_ref[...].reshape(HD, width)).astype(bf16)
            cos, sin = turns_ref[0, plane], turns_ref[1, plane]
            for t in range(2):
                span = slice(t * seq, (t + 1) * seq)
                prob = prob_ref[plane, t]
                out_grad = grads[span]
                query, key, value = (qkv_ref[i, plane, span] for i in range(3))
                value_grad = dot_tn(prob.astype(bf16), out_grad)
                prob_grad = dot_nt(out_grad, value)
                score_grad = (prob * (prob_grad - jnp.sum(prob * prob_grad, -1, keepdims=True))).astype(bf16)
                sides = [dot_nn(score_grad, key) * scale, dot_tn(score_grad, query) * scale]
                sides = [s * cos[span] - pltpu.roll(s, HD // 2, 1) * sin[span] for s in sides] + [value_grad]
                for i in range(3):
                    side = sides[i].astype(bf16)
                    raw_grad[plane, span, i * HD : (i + 1) * HD] = side
                    bias_sum[0:1, i * HD : (i + 1) * HD] += jnp.sum(side.astype(f32), 0, keepdims=True)

            def back(i, _):
                span = pl.ds(pl.multiple_of(i * column, column), column)
                weight = head_ref[pl.ds(i * (trees // 2), trees // 2)].reshape(column, 3 * HD)
                parts[plane, :, :, :, span] = dot_nt(raw_grad[plane], weight).astype(bf16).reshape(2, 2, rows, column)
                return 0

            lax.fori_loop(0, 2, back, 0)

        def share(i):
            to_z, to_x = mirror(z, i // 2), (x + i % 2) % 2
            source = shared_ref.at[:, :, lanes_of(to_z * 2 + to_x)]
            target = sgrad_ref.at[:, pl.ds(pl.multiple_of(here * sub, 16), sub)]
            if i:
                sends.start(source, target, s_send.at[i], s_recv.at[here], {"z": to_z, "x": to_x})
            else:
                pltpu.make_async_copy(source, target, s_recv.at[here]).start()

        share(0)
        share(4)
        run(*g[1:5])
        share(5)
        attend(0)
        run(g[5], r[0], g[6])
        share(6)
        g[7]()
        attend(1)
        run(r[1], g[8])
        share(7)
        run(r[2], r[3], g[9], g[10])
        attend(2)
        share(2)
        run(r[4], g[11], r[5], r[6])
        share(3)
        run(g[12], g[13])
        share(1)
        attend(3)
        run(r[7], r[8], r[9])
        arrive(layer_ref.at[c, 1 - y], l_recv.at[0])
        sends.start(layer_ref.at[c, 1 - y], layer_ref.at[c, 1 - y], l_send.at[2], l_recv.at[2], other)

        def project(e, _):
            rows_n = normed_ref[:, :, :, :, lanes_of(e)].reshape(tokens, slice_rows)
            value = dot_tn(rows_n, raw_grad[...].reshape(tokens, 3 * HD))
            dwp[e] = value.astype(bf16).reshape(2, half, 3 * HD)
            return 0

        load.wait()
        lax.fori_loop(0, trees, project, 0)
        sends.start(dwp.at[:, 1 - c], dwp_got, c_send.at[0], c_recv.at[0], other)
        run(r[10], r[11])

        def output(i, _):
            span = pl.ds(pl.multiple_of(i * column, column), column)
            rows_g = held[:, :, :, :, span].reshape(tokens, column)
            value = dot_tn(heads_ref[...].reshape(tokens, HD), rows_g)
            dwo[:, :, span] = value.astype(bf16).reshape(2, HD // 2, column)
            return 0

        lax.fori_loop(0, 2, output, 0)
        sends.start(dwo.at[1 - c], dwo_got, c_send.at[1], c_recv.at[1], other)
        r[12]()
        arrive(dwp_got, c_recv.at[0])
        dwp_sum[...] = (dwp[:, c].astype(f32) + dwp_got[...].astype(f32)).astype(bf16)
        arrive(dwo_got, c_recv.at[1])
        dwo_sum[...] = (dwo[c].astype(f32) + dwo_got[...].astype(f32)).astype(bf16)
        holder = z // 2
        place = lax.rem(z, 2) * 2 + x
        for e in range(trees):
            same = jnp.logical_and(here == e, c == holder)
            where = {"z": e // 2, "x": e % 2, "c": holder}
            for i in range(3):
                plain.start(
                    dwp_sum.at[e, :, pl.ds(i * HD, HD)],
                    pgrad_ref.at[i, pl.ds(pl.multiple_of(c * half, 16), half), pl.ds(pl.multiple_of(place * HD, HD), HD)],
                    w_send.at[e, i], w_recv.at[place, c, i], where, same,
                )
            plain.start(
                dwo_sum.at[:, pl.ds(e * slice_rows, slice_rows)],
                ograd_ref.at[pl.ds(pl.multiple_of(place * HD + c * (HD // 2), 16), HD // 2), :],
                w_send.at[e, 3], w_recv.at[place, c, 3], where, same,
            )

        total = add.total()
        value = in_ref[c, y].astype(f32)
        norm = lax.rsqrt(jnp.mean(value * value, -1, keepdims=True) + EPSILON)
        gain_part = jnp.sum(total * value * norm, 0, keepdims=True)
        scaled = total * gain_ref[...]
        ig[c, y] = (
            hg_ref[...] + norm * scaled - value * norm**3 * jnp.mean(scaled * value, -1, keepdims=True)
        ).astype(bf16)
        sends.start(ig.at[c, y], ig.at[c, y], i_send.at[0], i_recv.at[0], across)
        sends.start(ig.at[c, y], ig.at[c, y], i_send.at[1], i_recv.at[1], other)
        row = lax.broadcasted_iota(jnp.int32, (16, slice_rows), 0)
        bias = [
            jnp.concatenate([bias_sum[0:1, i * HD : (i + 1) * HD], jnp.zeros((1, slice_rows - HD), f32)], 1) for i in range(3)
        ]
        for e in range(trees):
            block = vec_ref[:, e * slice_rows : (e + 1) * slice_rows].astype(f32)
            block = jnp.where(row == lines + 2, gain_part[:, e * slice_rows : (e + 1) * slice_rows], block)
            for i in range(3):
                block = jnp.where(row == lines + 3 + i, bias[i], block)
            message[e] = block.astype(bf16)
        for i, to in enumerate(everyone):
            sends.start(message.at[to["z"] * 2 + to["x"]], got.at[z, x, y, c], m_send.at[i], m_recv.at[z, x, y, c], to)
        got[z, x, y, c] = message[here]
        for source in range(trees):
            arrive(sgrad_ref.at[:, pl.ds(source * sub, sub)], s_recv.at[source])

        def flip(i, _):
            span = pl.ds(pl.multiple_of(i * HD, HD), HD)
            gate_ref[:, span] = sgrad_ref[0, span, :].astype(f32).T.astype(bf16)
            up_ref[:, span] = sgrad_ref[1, span, :].astype(f32).T.astype(bf16)
            down_ref[span, :] = sgrad_ref[2, span, :]
            return 0

        lax.fori_loop(0, trees * sub // HD, flip, 0)
        arrive(ig.at[c, 1 - y], i_recv.at[0])
        sends.start(ig.at[c, 1 - y], ig.at[c, 1 - y], i_send.at[2], i_recv.at[2], other)

        for l in range(local_heads):
            for part in range(2):
                for i in range(3):
                    arrive(pgrad_ref.at[i, pl.ds(part * half, half), pl.ds(l * HD, HD)], w_recv.at[l, part, i])
                arrive(ograd_ref.at[pl.ds(l * HD + part * (HD // 2), HD // 2), :], w_recv.at[l, part, 3])
        arrive(layer_ref.at[1 - c, y], l_recv.at[1])
        arrive(layer_ref.at[1 - c, 1 - y], l_recv.at[2])
        for to in everyone:
            spot = (to["z"], to["x"], to["y"], to["c"])
            arrive(got.at[spot], m_recv.at[spot])
        small = jnp.sum(got[...].reshape(32, 16, slice_rows).astype(f32), 0)
        router_ref[...] = small[0:lines]
        vector_ref[...] = small[lines : lines + 1]
        gain2_ref[...] = small[lines + 1 : lines + 2]
        gain1_ref[...] = small[lines + 2 : lines + 3]
        source_z, source_x = 2 * c + z // 2, lax.rem(z, 2)
        both = got[source_z, source_x, y, 0].astype(f32) + got[source_z, source_x, y, 1].astype(f32)
        both = both[:, 0:HD]
        both = jnp.where(x == 1, pltpu.roll(both, HD // 2, 1), both)
        bias_ref[...] = both[lines + 3 : lines + 6, 0 : HD // 2]
        arrive(ig.at[1 - c, y], i_recv.at[1])
        arrive(ig.at[1 - c, 1 - y], i_recv.at[2])
        plain.finish()
        sends.finish()

    vmem = pl.BlockSpec(memory_space=pltpu.VMEM)
    dma = pltpu.SemaphoreType.DMA
    shape = jax.ShapeDtypeStruct
    return pl.pallas_call(
        kernel,
        name="attention_back",
        out_shape=(
            shape((2, 2, rows, width), bf16),
            shape((2, 2, rows, width), bf16),
            shape((3, slice_rows, local_heads * HD), bf16),
            shape((local_heads * HD, slice_rows), bf16),
            shape((slice_rows, trees * sub), bf16),
            shape((slice_rows, trees * sub), bf16),
            shape((trees * sub, slice_rows), bf16),
            shape((1, slice_rows), f32),
            shape((1, slice_rows), f32),
            shape((lines, slice_rows), f32),
            shape((1, slice_rows), f32),
            shape((3, HD // 2), f32),
        ),
        in_specs=[vmem, pl.BlockSpec(memory_space=pl.ANY)] + [vmem] * 12,
        out_specs=(vmem,) * 12,
        scratch_shapes=[
            pltpu.VMEM((3, trees * sub, slice_rows), bf16),
            pltpu.VMEM((4, 2, 2, rows, width), bf16),
            pltpu.VMEM((4, 2, 2, rows, width), bf16),
            pltpu.VMEM((4, 2, 2, rows, width), bf16),
            pltpu.VMEM((4, chunk, 3 * HD), bf16),
            pltpu.VMEM((trees, 2, half, 3 * HD), bf16),
            pltpu.VMEM((trees, half, 3 * HD), bf16),
            pltpu.VMEM((trees, half, 3 * HD), bf16),
            pltpu.VMEM((2, HD // 2, width), bf16),
            pltpu.VMEM((HD // 2, width), bf16),
            pltpu.VMEM((HD // 2, width), bf16),
            pltpu.VMEM((trees, 16, slice_rows), bf16),
            pltpu.VMEM((4, 2, 2, 2, 16, slice_rows), bf16),
            pltpu.VMEM((8, 3 * HD), f32),
            *Gather.semaphores(),
            dma((3,)),
            dma((3,)),
            dma((3,)),
            dma((3,)),
            dma((31,)),
            dma((4, 2, 2, 2)),
            dma((trees,)),
            dma((trees,)),
            dma((2,)),
            dma((2,)),
            dma((trees, 4)),
            dma((local_heads, 2, 4)),
            dma,
            *Reduce.buffers(rows, width, cut),
        ],
        compiler_params=pltpu.CompilerParams(collective_id=10, has_side_effects=True, vmem_limit_bytes=VMEM_LIMIT),
    )(own_grad, normed, qkv, probs, heads, head, out_head, turns, input_rows, hidden_grad, gain, own_output, vectors, shared)


def finish_call(arrays, kinds):
    count = len(arrays)

    def kernel(*refs):
        sources, targets = refs[:count], refs[count : 2 * count]
        narrow, wide = refs[2 * count : 3 * count], refs[3 * count : 4 * count]
        in_sem, out_sem = refs[4 * count :]
        reads = [pltpu.make_async_copy(sources[i], narrow[i], in_sem.at[i]) for i in range(count)]
        for read in reads:
            read.start()
        writes = []
        for i in range(count):
            reads[i].wait()
            wide[i][...] = narrow[i][...].astype(kinds[i])
            write = pltpu.make_async_copy(wide[i], targets[i], out_sem.at[i])
            write.start()
            writes.append(write)
        for write in writes:
            write.wait()

    anywhere = pl.BlockSpec(memory_space=pl.ANY)
    return pl.pallas_call(
        kernel,
        name="finish",
        out_shape=tuple(jax.ShapeDtypeStruct(a.shape, kind) for a, kind in zip(arrays, kinds)),
        in_specs=[anywhere] * count,
        out_specs=(anywhere,) * count,
        scratch_shapes=[
            *[pltpu.VMEM(a.shape, a.dtype) for a in arrays],
            *[pltpu.VMEM(a.shape, kind) for a, kind in zip(arrays, kinds)],
            pltpu.SemaphoreType.DMA((count,)),
            pltpu.SemaphoreType.DMA((count,)),
        ],
        compiler_params=pltpu.CompilerParams(vmem_limit_bytes=VMEM_LIMIT),
    )(*arrays)


def chip_shards(
    layer_input,
    positions,
    parents,
    routes,
    route_slots,
    norm1_gain,
    project_weight,
    project_bias,
    output_weight,
    norm2_gain,
    router_weight,
    shared_vector,
    shared_gate,
    shared_up,
    shared_down,
    expert_gate,
    expert_up,
    expert_down,
    cotangent,
):
    f32, bf16 = jnp.float32, jnp.bfloat16
    micro_count, seq_rows, model_width = layer_input.shape
    top_count = routes.shape[2]
    expert_count = router_weight.shape[1]
    capacity = seq_rows * top_count * 5 // (4 * expert_count)
    z, x, y, c = [lax.axis_index(a) for a in AXES]
    here = z * 2 + x
    trees = expert_count
    tokens = trees * seq_rows
    blocks = (trees // 2, 2, 2, seq_rows // 2, model_width)
    own_rows = seq_rows // 2
    slice_rows = norm1_gain.shape[0]
    score_scale = HD ** (-0.5)

    def own(array):
        return lax.dynamic_slice(
            array, (c, y * own_rows, 0), (1, own_rows, model_width)
        )[0]

    own_input = own(layer_input)
    own_cotangent = own(cotangent)
    by_rows = (2, 2, own_rows, model_width)

    half_size = HD // 2
    inverse = ROPE_BASE ** (-(jnp.arange(half_size, dtype=f32) * 2.0 / HD))
    angles = jnp.arange(seq_rows, dtype=f32)[:, None] * inverse[None, :]
    table = jnp.concatenate([jnp.cos(angles), jnp.sin(angles)], 1)
    coarse = lax.reduce_precision(table, 8, 7)
    table = jnp.stack([coarse, table - coarse]).astype(bf16)
    (
        attention,
        normed_one,
        qkv,
        attention_probs,
        heads_out,
        head_weight,
        out_weight,
        smalls,
        turns,
        all_cotangent,
        three,
    ) = front_call(
        layer_input.reshape(by_rows),
        cotangent.reshape(by_rows),
        project_weight.transpose(1, 0, 2),
        output_weight,
        jnp.stack([norm1_gain, norm2_gain, shared_vector]),
        router_weight.T,
        positions,
        parents[:, 0],
        project_bias,
        table,
        shared_gate,
        shared_up,
        shared_down,
        [expert_gate[0].T, expert_up[0].T, expert_down[0]],
    )
    of_core = lax.dynamic_index_in_dim(smalls.reshape(trees, 2, -1, slice_rows), c, 1, keepdims=False)
    full = of_core[:, : expert_count + 3].transpose(1, 0, 2).reshape(expert_count + 3, model_width)
    gain_one, gain_two = full[0].astype(f32), full[1].astype(f32)
    small_weights = full[2:]
    routed_units = 2 * expert_down.shape[1]
    own_rows_in = own_input.astype(f32)
    hidden_state = own_rows_in + attention
    norm_two = lax.rsqrt(jnp.mean(hidden_state * hidden_state, -1, keepdims=True) + EPSILON)
    own_normed_two = (hidden_state * norm_two * gain_two).astype(bf16)

    first = y * own_rows
    my_routes = lax.dynamic_slice(routes, (c, first, 0), (1, own_rows, top_count))[0]
    my_slots = lax.dynamic_slice(route_slots, (c, first, 0), (1, own_rows, top_count))[0]
    logits = product_right(own_normed_two, small_weights)
    prob = jax.nn.softmax(logits[:, :expert_count], axis=-1)
    shared_scale = jax.nn.sigmoid(logits[:, expert_count:])
    onehot = (my_routes[..., None] == jnp.arange(expert_count, dtype=jnp.int32)).astype(f32)
    kept = jnp.sum(onehot * (my_slots < capacity).astype(f32)[..., None], 1)
    onehot = jnp.sum(onehot, 1)
    picked_sum = jnp.sum(onehot * prob, -1, keepdims=True)
    every_gate = onehot * prob / picked_sum
    row_scales = jnp.concatenate([every_gate * kept, shared_scale], 1)
    high = row_scales.astype(bf16)
    low = (row_scales - high.astype(f32)).astype(bf16)
    extra = jnp.concatenate(
        [
            high[:, :expert_count],
            low[:, :expert_count],
            high[:, expert_count:],
            low[:, expert_count:],
            jnp.zeros((own_rows, EXTRA - 2 * expert_count - 2), bf16),
        ],
        1,
    )
    normed_sum, ffn_out, dots, *expert_sum, shared_sum = experts_call(
        jnp.concatenate([own_normed_two, extra], 1), all_cotangent, three, routed_units
    )
    own_output = (hidden_state + ffn_out).astype(bf16)
    dots = lax.dynamic_slice(dots, (0, 0, 0, 0, first), (*dots.shape[:4], own_rows))
    dots = dots.reshape(trees, 2, 8, own_rows)
    expert_dots = (dots[:, 0, 0] + dots[:, 1, 0]).T
    shared_dot = jnp.sum(dots[:, :, 1], (0, 1))[:, None]

    kept_dots = expert_dots * kept
    picked_grad = (kept_dots - jnp.sum(kept_dots * every_gate, -1, keepdims=True)) / picked_sum
    prob_grad = picked_grad * onehot
    logit_grad = prob * (prob_grad - jnp.sum(prob * prob_grad, -1, keepdims=True))
    scale_grad = shared_dot * shared_scale * (1.0 - shared_scale)
    own_small = jnp.concatenate([logit_grad, scale_grad], 1).astype(bf16)
    grad_small = product_left(own_small, own_normed_two)
    normed_two_grad = normed_sum + product(own_small, small_weights)
    upstream = own_cotangent.astype(f32)
    grad_gain_two = jnp.sum(normed_two_grad * hidden_state * norm_two, 0)
    scaled_two = normed_two_grad * gain_two
    hidden_grad_rows = (
        upstream
        + norm_two * scaled_two
        - hidden_state * norm_two**3 * jnp.mean(scaled_two * hidden_state, -1, keepdims=True)
    )
    vectors = jnp.concatenate([grad_small, grad_gain_two[None]], 0)
    vectors = jnp.pad(vectors, ((0, -vectors.shape[0] % 16), (0, 0))).astype(bf16)
    (
        layer_output,
        input_grad,
        project_out,
        output_out,
        gate_out,
        up_out,
        down_out,
        gain_one_out,
        gain_two_out,
        router_out,
        vector_out,
        bias_out,
    ) = attention_back_call(
        hidden_grad_rows.astype(bf16),
        normed_one,
        qkv,
        attention_probs,
        heads_out,
        head_weight,
        out_weight,
        turns,
        layer_input.reshape(by_rows),
        hidden_grad_rows,
        gain_one[None],
        expert_count,
        own_output,
        vectors,
        shared_sum,
    )
    (
        expert_gate_out,
        expert_up_out,
        expert_down_out,
        gate_out,
        up_out,
        down_out,
        project_out,
        output_out,
        input_grad,
        layer_output,
        gain_one_out,
        gain_two_out,
        router_out,
        vector_out,
        bias_out,
    ) = finish_call(
        [
            *expert_sum,
            gate_out,
            up_out,
            down_out,
            project_out,
            output_out,
            input_grad,
            layer_output,
            gain_one_out,
            gain_two_out,
            router_out,
            vector_out,
            bias_out,
        ],
        [f32] * 9 + [bf16] + [f32] * 5,
    )
    return (
        layer_output.reshape(layer_input.shape),
        input_grad.reshape(layer_input.shape),
        gain_one_out[0],
        project_out.transpose(1, 0, 2),
        bias_out,
        output_out,
        gain_two_out[0],
        router_out.T,
        vector_out[0],
        gate_out,
        up_out,
        down_out,
        expert_gate_out.T[None],
        expert_up_out.T[None],
        expert_down_out[None],
    )


def spread(body, mesh, rows, columns):
    def named(*dims):
        names = {"expert": rows, "tensor": columns, "both": (*columns, *rows), None: None}
        return P(*(names[d] for d in dims))

    return jax.shard_map(
        body,
        mesh=mesh,
        in_specs=(
            named(None, "expert", None),
            named(None, "expert"),
            named(None, "expert", None),
            named(None, "expert", None),
            named(None, "expert", None),
            named("expert"),
            named("expert", None, "tensor"),
            named(None, "both"),
            named("tensor", "expert"),
            named("expert"),
            named("expert", None),
            named("expert"),
            named("expert", "tensor"),
            named("expert", "tensor"),
            named("tensor", "expert"),
            named("expert", None, "tensor"),
            named("expert", None, "tensor"),
            named("expert", "tensor", None),
            named(None, "expert", None),
        ),
        out_specs=(
            named(None, "expert", None),
            named(None, "expert", None),
            named("expert"),
            named("expert", None, "tensor"),
            named(None, "both"),
            named("tensor", "expert"),
            named("expert"),
            named("expert", None),
            named("expert"),
            named("expert", "tensor"),
            named("expert", "tensor"),
            named("tensor", "expert"),
            named("expert", None, "tensor"),
            named("expert", None, "tensor"),
            named("expert", "tensor", None),
        ),
        check_vma=False,
    )


def solution(mesh):
    expert_devices, tensor_devices = mesh.shape["expert"], mesh.shape["tensor"]

    def layer(*arrays):
        heads = arrays[6].shape[2] // HD
        trees = arrays[0].shape[1] // (SEG * arrays[2].shape[2])
        if (
            tensor_devices == 4
            and expert_devices % 2 == 0
            and heads == 2 * expert_devices
            and arrays[10].shape[1] == expert_devices
            and trees == expert_devices
            and arrays[0].shape[0] == 2
        ):
            grid = Mesh(mesh.devices.reshape(expert_devices // 2, 2, 2, 2), AXES)
            body = spread(chip_shards, grid, ("z", "x"), ("y", "c"))
        else:
            body = spread(gathered_shards, mesh, ("expert",), ("tensor",))
        return body(*arrays)

    return layer
```
